32 devices in a mesh: dp: 16 (over z, y, x), head: 2 (over core).
Axes of the slice: x: 2, y: 2, z: 4, core: 2. Of those that a mesh axis runs over, the one named last changes fastest.
Arguments:
- tokens: bfloat16 [65536, 512], P('dp', 'head'), may hold values from -6 to 6
- cotangent: bfloat16 [65536, 512], P('dp', 'head'), may hold values from -6 to 6
- lengths: int32 [32], P('dp'), may hold values from 128 to 2048, as said below
- owners: int32 [5], replicated, may hold values from 0 to 15
- w_qkv: float32 [512, 3, 512], P(None, None, 'head'), may hold values from -0.25 to 0.25
- w_out: float32 [512, 512], P('head'), may hold values from -1 to 1
- w_up: float32 [512, 2048], P(None, 'head'), may hold values from -0.25 to 0.25
- w_down: float32 [2048, 512], P('head'), may hold values from -0.125 to 0.125
- ln_params: float32 [4, 512], replicated
- m_qkv: float32 [512, 3, 512], P(None, None, 'head'), may hold values from -768 to 768
- m_out: float32 [512, 512], P('head'), may hold values from -384 to 384
- m_up: float32 [512, 2048], P(None, 'head'), may hold values from -384 to 384
- m_down: float32 [2048, 512], P('head'), may hold values from -768 to 768
- m_ln: float32 [4, 512], replicated, may hold values from -768 to 768
- v_qkv: float32 [512, 3, 512], P(None, None, 'head'), may hold values from 16384 to 65536
- v_out: float32 [512, 512], P('head'), may hold values from 4096 to 16384
- v_up: float32 [512, 2048], P(None, 'head'), may hold values from 4096 to 16384
- v_down: float32 [2048, 512], P('head'), may hold values from 16384 to 65536
- v_ln: float32 [4, 512], replicated, may hold values from 16384 to 65536
Outputs:
- output: bfloat16 [65536, 512], P('dp', 'head')
- grad_tokens: bfloat16 [65536, 512], P('dp', 'head')
- owned_qkv: float32 [16, 512, 3, 512], P('dp', None, None, 'head')
- owned_out: float32 [16, 512, 512], P('dp', 'head')
- owned_up: float32 [16, 512, 2048], P('dp', None, 'head')
- owned_down: float32 [16, 2048, 512], P('dp', 'head')
- owned_ln: float32 [16, 4, 512], P('dp')
- new_qkv: float32 [512, 3, 512], P(None, None, 'head')
- new_out: float32 [512, 512], P('head')
- new_up: float32 [512, 2048], P(None, 'head')
- new_down: float32 [2048, 512], P('head')
- new_ln: float32 [4, 512], replicated
- first_qkv: float32 [512, 3, 512], P(None, None, 'head')
- first_out: float32 [512, 512], P('head')
- first_up: float32 [512, 2048], P(None, 'head')
- first_down: float32 [2048, 512], P('head')
- first_ln: float32 [4, 512], replicated
- second_qkv: float32 [512, 3, 512], P(None, None, 'head')
- second_out: float32 [512, 512], P('head')
- second_up: float32 [512, 2048], P(None, 'head')
- second_down: float32 [2048, 512], P('head')
- second_ln: float32 [4, 512], replicated
- copy_qkv: bfloat16 [512, 3, 512], P(None, None, 'head')
- copy_out: bfloat16 [512, 512], P('head')
- copy_up: bfloat16 [512, 2048], P(None, 'head')
- copy_down: bfloat16 [2048, 512], P('head')
The draws below stay inside these ranges and needn't reach their ends.
Inputs may be any that keep to these rules, and one draw needn't show every extreme that they name: `lengths`: each length is a multiple of 128; tokens at or past it are padding, which the layer leaves unchanged.
All inputs are finite; a program needn't handle non-finite values.
Results may differ from the reference program's by a relative error of at most 0.025.
Values may be sent and summed in bfloat16 or wider, within the bound.
A program may use at most 320 MiB of HBM per device.

```python
import math
import jax
import jax.numpy as jnp
from jax import lax

D = 512
HEADS = 8
HEAD_DIM = 64
FF = 2048
SPAN = 128
SEQ = 2048
SEQS_DEV = 2
STEP = 5
ROWS = 16
TOKENS = 65536
N_DP = 16


def draw_lengths(key, part):
    seq_total = SEQS_DEV * N_DP
    device_of = jnp.arange(seq_total, dtype=jnp.int32) // SEQS_DEV
    floor_rows = max(ROWS // 3, 1)
    lowest = floor_rows + (ROWS - floor_rows) * device_of // N_DP
    extra = jax.random.randint(key, (seq_total,), 0, 3, dtype=jnp.int32)
    rows_used = jnp.minimum(lowest + extra, ROWS)
    rows_used = jnp.where(jnp.arange(seq_total, dtype=jnp.int32) == seq_total - 1, ROWS, rows_used)
    return (rows_used * SPAN).astype(jnp.int32)


def draw_ln_params(key, part):
    key_gain = jax.random.fold_in(key, 11)
    key_shift = jax.random.fold_in(key, 23)
    gain_rows = jax.random.uniform(key_gain, (4, D), jnp.float32, 0.5, 1.5)
    shift_rows = 0.3 * jax.random.normal(key_shift, (4, D), jnp.float32)
    selector = (jnp.arange(4) % 2 == 0)[:, None]
    return jnp.where(selector, gain_rows, shift_rows)


def with_ends(result, rng, smallest, top_value):
    index_at = [jax.random.randint(jax.random.fold_in(rng, axis), (), 0, length) for axis, length in enumerate(result.shape)]
    longest = result.shape.index(max(result.shape))
    next_to = index_at[:longest] + [(index_at[longest] + 1) % result.shape[longest]] + index_at[longest + 1:]
    return result.at[tuple(index_at)].set(smallest).at[tuple(next_to)].set(top_value)


def steps_of(key, dims, cuts, smallest, top_value):
    level, own = 1.0, jax.random.fold_in(key, 6)
    for axis_at, blocks in cuts:
        steps = jnp.exp(jax.random.uniform(jax.random.fold_in(own, axis_at), (blocks,), jnp.float32, smallest / len(cuts), top_value / len(cuts)))
        level = level * jnp.repeat(steps, dims[axis_at] // blocks).reshape([-1 if axis == axis_at else 1 for axis in range(len(dims))])
    return level


def gaussian(key, shape, scale, reach, pieces=(), kind=jnp.bfloat16):
    loudness = steps_of(key, shape, pieces, -0.22, 0.18) if pieces else 1.0
    array = jax.random.normal(key, shape, jnp.float32) * scale * loudness
    return jnp.minimum(jnp.maximum(array, -reach), reach).astype(kind)


def setup_inputs(seed: int = 0) -> dict:
    key_of = jax.random.split(jax.random.key(seed), 20)
    tokens = gaussian(key_of[0], (TOKENS, D), 1.0, 6.0, ((0, 16), (1, 2)))
    cotangent = gaussian(key_of[1], (TOKENS, D), 1.0, 6.0, ((0, 16), (1, 2)))
    lengths = draw_lengths(jax.random.fold_in(key_of[19], 71), 0)
    owners = with_ends(jax.random.randint(key_of[3], (5,), 0, N_DP), jax.random.fold_in(key_of[3], 1), 0, N_DP - 1).astype(jnp.int32)
    w_qkv = gaussian(key_of[4], (D, 3, D), D ** -0.5, 0.25, ((2, 2),), jnp.float32)
    w_out = gaussian(key_of[5], (D, D), (D // 16) ** -0.5, 1.0, ((0, 2),), jnp.float32)
    w_up = gaussian(key_of[6], (D, FF), D ** -0.5, 0.25, ((1, 2),), jnp.float32)
    w_down = gaussian(key_of[7], (FF, D), FF ** -0.5, 0.125, ((0, 2),), jnp.float32)
    ln_params = draw_ln_params(jax.random.fold_in(key_of[19], 71), 0)
    m_qkv = gaussian(key_of[9], (D, 3, D), (0.5 * TOKENS ** 0.5), 768.0, ((2, 2),), jnp.float32)
    m_out = gaussian(key_of[10], (D, D), (0.25 * TOKENS ** 0.5), 384.0, ((0, 2),), jnp.float32)
    m_up = gaussian(key_of[11], (D, FF), (0.25 * TOKENS ** 0.5), 384.0, ((1, 2),), jnp.float32)
    m_down = gaussian(key_of[12], (FF, D), (0.5 * TOKENS ** 0.5), 768.0, ((0, 2),), jnp.float32)
    m_ln = gaussian(key_of[13], (4, D), (0.5 * TOKENS ** 0.5), 768.0, (), jnp.float32)
    v_qkv = jnp.clip(jnp.exp(math.log(65536.0) - 1.3862944 * jax.random.uniform(key_of[14], (D, 3, D), jnp.float32) ** steps_of(key_of[14], (D, 3, D), ((2, 2),), -0.2, 0.2)), 16384.0, 65536.0)
    v_out = jnp.clip(jnp.exp(math.log(16384.0) - 1.3862944 * jax.random.uniform(key_of[15], (D, D), jnp.float32) ** steps_of(key_of[15], (D, D), ((0, 2),), -0.2, 0.2)), 4096.0, 16384.0)
    v_up = jnp.clip(jnp.exp(math.log(16384.0) - 1.3862944 * jax.random.uniform(key_of[16], (D, FF), jnp.float32) ** steps_of(key_of[16], (D, FF), ((1, 2),), -0.2, 0.2)), 4096.0, 16384.0)
    v_down = jnp.clip(jnp.exp(math.log(65536.0) - 1.3862944 * jax.random.uniform(key_of[17], (FF, D), jnp.float32) ** steps_of(key_of[17], (FF, D), ((0, 2),), -0.2, 0.2)), 16384.0, 65536.0)
    v_ln = jnp.clip(jnp.exp(jax.random.uniform(key_of[18], (4, D), jnp.float32, math.log(16384.0), math.log(65536.0))), 16384.0, 65536.0)
    return dict(tokens=tokens, cotangent=cotangent, lengths=lengths, owners=owners, w_qkv=w_qkv, w_out=w_out, w_up=w_up, w_down=w_down, ln_params=ln_params, m_qkv=m_qkv, m_out=m_out, m_up=m_up, m_down=m_down, m_ln=m_ln, v_qkv=v_qkv, v_out=v_out, v_up=v_up, v_down=v_down, v_ln=v_ln)


@jax.custom_vjp
def low(v):
    return lax.optimization_barrier(v.astype(jnp.bfloat16)).astype(jnp.float32)

@jax.custom_vjp
def low_back(v):
    return v

def low_keep(v):
    return (low(v), None)

def low_pass(kept, grad):
    return (grad,)

def back_keep(v):
    return (v, None)

def back_low(kept, grad):
    return (low(grad),)
low.defvjp(low_keep, low_pass)
low_back.defvjp(back_keep, back_low)
epsilon_norm = 1e-05
epsilon_adam = 1e-08
beta_one = 0.5
beta_two = 0.5
decay_rate = 0.1
masked_score = -1e+30

def layer_norm(values, gain_vec, bias_vec):
    row_mean = lax.optimization_barrier(jnp.mean(values, axis=-1, keepdims=True))
    centered = values - row_mean
    row_var = lax.optimization_barrier(jnp.mean(centered * centered, axis=-1, keepdims=True))
    return centered * lax.rsqrt(row_var + epsilon_norm) * gain_vec + bias_vec

def score_bias():
    row_ids = jnp.arange(ROWS)
    col_ids = jnp.arange(SPAN)
    direct_ok = jnp.broadcast_to((col_ids[None, :] <= col_ids[:, None])[None], (ROWS, SPAN, SPAN))
    summary_ok = jnp.broadcast_to((row_ids >= 1)[:, None, None], (ROWS, SPAN, SPAN))
    allowed = jnp.concatenate([direct_ok, summary_ok], axis=2)
    log_count = jnp.log(jnp.maximum(row_ids, 1).astype(jnp.float32))
    shift = jnp.concatenate([jnp.zeros((ROWS, SPAN, SPAN), jnp.float32), jnp.broadcast_to(log_count[:, None, None], (ROWS, SPAN, SPAN))], axis=2)
    return (allowed[:, None], shift[:, None])

def adam_step(gradient, weight, moment_one, moment_two, step_rate):
    first_new = beta_one * moment_one + (1.0 - beta_one) * gradient
    second_new = beta_two * moment_two + (1.0 - beta_two) * gradient * gradient
    first_hat = first_new / (1.0 - beta_one ** STEP)
    second_hat = second_new / (1.0 - beta_two ** STEP)
    weight_new = weight - step_rate * (first_hat / (jnp.sqrt(second_hat) + epsilon_adam) + decay_rate * weight)
    return (weight_new, first_new, second_new)

def one_sequence(inputs, valid_rows, w_qkv, w_out, w_up, w_down, ln_params):
    highest = lax.Precision.HIGHEST
    scale_factor = float(HEAD_DIM) ** (-0.5)
    normed_one = low(layer_norm(inputs, ln_params[0], ln_params[1]))
    projected = jnp.einsum('sd,dce->sce', normed_one, w_qkv, precision=highest)
    projected = low(low_back(projected))
    split_rows = projected.reshape(ROWS, SPAN, 3, HEADS, HEAD_DIM)
    query_part = split_rows[:, :, 0]
    key_part = split_rows[:, :, 1]
    value_part = split_rows[:, :, 2]
    divisor = jnp.maximum(jnp.arange(ROWS), 1).astype(jnp.float32)[:, None, None, None]
    key_mean = low((jnp.cumsum(key_part, axis=0) - key_part) / divisor)
    value_mean = low((jnp.cumsum(value_part, axis=0) - value_part) / divisor)
    all_keys = jnp.concatenate([key_part, key_mean], axis=1)
    all_values = jnp.concatenate([value_part, value_mean], axis=1)
    raw_scores = jnp.einsum('rqhe,rkhe->rhqk', query_part, all_keys, precision=highest)
    scores = low_back(raw_scores * scale_factor)
    allowed, shift = score_bias()
    scores = jnp.where(allowed, scores + shift, masked_score)
    row_max = lax.optimization_barrier(jnp.max(scores, axis=-1, keepdims=True))
    expo = jnp.exp(scores - row_max)
    prob_rows = low(expo / lax.optimization_barrier(jnp.sum(expo, axis=-1, keepdims=True)))
    context = jnp.einsum('rhqk,rkhe->rqhe', prob_rows, all_values, precision=highest).reshape(SEQ, D)
    context = low(low_back(context))
    attn_out = low_back(jnp.dot(context, w_out, precision=highest))
    residual = inputs + valid_rows * attn_out
    normed_two = low(layer_norm(residual, ln_params[2], ln_params[3]))
    up_proj = low_back(jnp.dot(normed_two, w_up, precision=highest))
    hidden = low(jax.nn.gelu(up_proj, approximate=False))
    mlp_out = low_back(jnp.dot(hidden, w_down, precision=highest))
    return residual + valid_rows * mlp_out

def owned_copy(gradient, owner_id):
    chosen = (jnp.arange(N_DP, dtype=jnp.int32) == owner_id).astype(jnp.float32)
    return chosen.reshape((N_DP,) + (1,) * gradient.ndim) * gradient[None]

def reference(tokens, cotangent, lengths, owners, w_qkv, w_out, w_up, w_down, ln_params, m_qkv, m_out, m_up, m_down, m_ln, v_qkv, v_out, v_up, v_down, v_ln):
    seq_total = tokens.shape[0] // SEQ
    inputs = tokens.astype(jnp.float32).reshape(seq_total, SEQ, D)
    cot_all = cotangent.astype(jnp.float32).reshape(seq_total, SEQ, D)
    positions = jnp.arange(SEQ, dtype=jnp.int32)
    valid_all = (positions[None, :] < lengths[:, None]).astype(jnp.float32)[:, :, None]

    def forward(layer_in, weight_qkv, weight_out, weight_up, weight_down, norm_params):

        def step_one(sequence_pair):
            return one_sequence(sequence_pair[0], sequence_pair[1], weight_qkv, weight_out, weight_up, weight_down, norm_params)
        return lax.map(jax.checkpoint(step_one), (layer_in, valid_all))
    outputs, pullback = jax.vjp(forward, inputs, w_qkv, w_out, w_up, w_down, ln_params)
    gradients = pullback(cot_all)
    output = outputs.reshape(seq_total * SEQ, D).astype(jnp.bfloat16)
    grad_tokens = gradients[0].reshape(seq_total * SEQ, D).astype(jnp.bfloat16)
    weight_grads = gradients[1:]
    masters = (w_qkv, w_out, w_up, w_down, ln_params)
    firsts = (m_qkv, m_out, m_up, m_down, m_ln)
    seconds = (v_qkv, v_out, v_up, v_down, v_ln)
    rates = (float(D) ** (-0.5), 4.0 * float(D) ** (-0.5), float(D) ** (-0.5), float(FF) ** (-0.5), 0.7)
    updated = [adam_step(weight_grads[kind_index], masters[kind_index], firsts[kind_index], seconds[kind_index], rates[kind_index]) for kind_index in range(5)]
    owned_grads = tuple((owned_copy(weight_grads[kind_index], owners[kind_index]) for kind_index in range(5)))
    new_weights = tuple((entry[0] for entry in updated))
    new_firsts = tuple((entry[1] for entry in updated))
    new_seconds = tuple((entry[2] for entry in updated))
    copies = tuple((new_weights[kind_index].astype(jnp.bfloat16) for kind_index in range(4)))
    return (output, grad_tokens) + owned_grads + new_weights + new_firsts + new_seconds + copies
```

```python
import functools

import jax
import jax.numpy as jnp
import numpy as np
from jax import lax
from jax.experimental import pallas as pl
from jax.experimental.pallas import tpu as pltpu
from jax.sharding import PartitionSpec as P

D = 512
HALF = 256
HEAD_DIM = 64
FF = 2048
SPAN = 128
SEQ = 2048
STEP = 5
ROWS = 16
PAIRS = 4
TILE = 512
TILES = SEQ // TILE
SPANS_TILE = TILE // SPAN

epsilon_norm = 1e-05
epsilon_adam = 1e-08
beta_one = 0.5
beta_two = 0.5
decay_rate = 0.1
masked_score = -1e30

bf16 = jnp.bfloat16
f32 = jnp.float32

NN = (((1,), (0,)), ((), ()))
NT = (((1,), (1,)), ((), ()))
TN = (((0,), (0,)), ((), ()))


def mm(left, right, dims=NN):
    return lax.dot_general(left, right, dims, preferred_element_type=f32)


def join_columns(head, own, other):
    low = jnp.where(head == 0, own, other)
    high = jnp.where(head == 0, other, own)
    return jnp.concatenate([low, high], axis=1)


def norm_stats(values):
    mean = jnp.mean(values, axis=1, keepdims=True)
    centered = values - mean
    rstd = lax.rsqrt(jnp.mean(centered * centered, axis=1, keepdims=True) + epsilon_norm)
    return centered * rstd, rstd


def head_stack(pair, low_lanes, high_lanes):
    return jnp.concatenate([pair * low_lanes, pair * high_lanes], axis=0)


def lane_masks(dtype):
    lane = lax.broadcasted_iota(jnp.int32, (1, 2 * HEAD_DIM), 1)
    low = (lane < HEAD_DIM).astype(f32)
    return low.astype(dtype), (1.0 - low).astype(dtype)


def pair_columns(pair):
    base = 3 * HALF * (pair // 2) + 2 * HEAD_DIM * (pair % 2)
    return base, base + HALF, base + 2 * HALF


def unstack_transposed(product):
    joined = jnp.concatenate(
        [product[:HEAD_DIM, :SPAN], product[HEAD_DIM:, SPAN:]], axis=0
    )
    return joined.T


def forward_attention(
    table, x_own, x_other, ln, w_own, w_other, causal, qkv, bars, probs, ctx, run_sum, normed
):
    head = lax.axis_index("head")
    step = pl.program_id(0)

    @pl.when(step == 0)
    def _():
        run_sum[...] = jnp.zeros_like(run_sum)

    for row in range(0, TILE, 128):
        rows = pl.ds(row, 128)
        x = join_columns(head, x_own[rows, :].astype(f32), x_other[rows, :].astype(f32))
        xhat, _ = norm_stats(x)
        normed[rows, :] = (xhat * ln[0:1, :] + ln[1:2, :]).astype(bf16)
    for side, w in enumerate((w_own, w_other)):
        for part in range(3):
            value = mm(normed[...], w[part])
            if part == 0:
                value = value * float(HEAD_DIM) ** (-0.5)
            base = side * 3 * HALF + part * HALF
            qkv[:, base : base + HALF] = value.astype(bf16)
    low_lanes, high_lanes = lane_masks(bf16)
    for span in range(SPANS_TILE):
        rows = pl.ds(span * SPAN, SPAN)
        row_id = step * SPANS_TILE + span
        inverse = table[0, row_id]
        shift = table[1, row_id]
        for pair in range(PAIRS):
            at_q, at_k, at_v = pair_columns(pair)
            lanes = pl.ds(pair * 128, 128)
            lanes_v = pl.ds(512 + pair * 128, 128)
            key = qkv[rows, at_k : at_k + 128]
            value = qkv[rows, at_v : at_v + 128]
            key_bar = (run_sum[:, lanes] * inverse).astype(bf16)
            value_bar = (run_sum[:, lanes_v] * inverse).astype(bf16)
            run_sum[:, lanes] += key.astype(f32)
            run_sum[:, lanes_v] += value.astype(f32)
            bars[rows, lanes] = key_bar
            bars[rows, lanes_v] = value_bar
            query = head_stack(qkv[rows, at_q : at_q + 128], low_lanes, high_lanes)
            direct = mm(key, query, NT) + causal[...]
            summary = mm(key_bar, query, NT) + shift
            top = jnp.maximum(
                jnp.max(direct, axis=0, keepdims=True), jnp.max(summary, axis=0, keepdims=True)
            )
            direct = jnp.exp(direct - top)
            summary = jnp.exp(summary - top)
            total = jnp.sum(direct, axis=0, keepdims=True) + jnp.sum(
                summary, axis=0, keepdims=True
            )
            scale = 1.0 / total
            direct = (direct * scale).astype(bf16)
            summary = (summary * scale).astype(bf16)
            slot = span * PAIRS + pair
            probs[slot, :SPAN, :] = direct
            probs[slot, SPAN:, :] = summary
            values = jnp.concatenate([value, value_bar], axis=0)
            both = jnp.concatenate([direct, summary], axis=0)
            ctx[rows, lanes] = unstack_transposed(mm(values, both, TN)).astype(bf16)


def gelu_parts(u):
    size = jnp.abs(u)
    bell = jnp.exp(u * u * -0.5)
    denom = 1.0 + (0.3275911 * 0.7071067811865476) * size
    t = 1.0 / denom
    poly = t * (
        0.5 * 0.254829592
        + t
        * (
            0.5 * -0.284496736
            + t * (0.5 * 1.421413741 + t * (0.5 * -1.453152027 + t * (0.5 * 1.061405429)))
        )
    )
    tail = poly * bell
    share = jnp.where(u >= 0.0, 1.0 - tail, tail)
    return u * share, share + u * bell * 0.3989422804014327


def mlp_both_ways(
    lengths,
    x_own,
    x_other,
    dy_own,
    dy_other,
    ln,
    ctx,
    out_own,
    out_other,
    up_own,
    up_other,
    down_own,
    down_other,
    y_own,
    y_other,
    grad_res,
    grad_ctx,
    g_out,
    g_up,
    g_down,
    g_ln,
    acc_out,
    acc_up,
    acc_down,
    acc_ln,
    res,
    xhat,
    rstd_at,
    normed,
    gm,
    mlp,
    grad_n,
    hid,
    slope,
    act,
    grad_hid,
    gu,
    ga,
):
    head = lax.axis_index("head")
    step = pl.program_id(0)
    used = lengths[head]

    @pl.when(step == 0)
    def _():
        acc_out[...] = jnp.zeros_like(acc_out)
        acc_up[...] = jnp.zeros_like(acc_up)
        acc_down[...] = jnp.zeros_like(acc_down)
        acc_ln[...] = jnp.zeros_like(acc_ln)

    def valid_rows(row, count):
        ids = lax.broadcasted_iota(jnp.int32, (count, 1), 0) + (step * TILE + row)
        return (ids < used).astype(f32)

    res[...] = mm(ctx[:, :HALF], out_own[...]) + mm(ctx[:, HALF:], out_other[...])
    for row in range(0, TILE, 128):
        rows = pl.ds(row, 128)
        valid = valid_rows(row, 128)
        x = join_columns(head, x_own[rows, :].astype(f32), x_other[rows, :].astype(f32))
        h = x + valid * res[rows, :]
        res[rows, :] = h
        hat, rstd = norm_stats(h)
        xhat[rows, :] = hat
        rstd_at[rows, :] = rstd
        normed[rows, :] = (hat * ln[2:3, :] + ln[3:4, :]).astype(bf16)
        dy = join_columns(head, dy_own[rows, :].astype(f32), dy_other[rows, :].astype(f32))
        gm[rows, :] = (valid * dy).astype(bf16)
    chunk = 512
    for index in range(FF // chunk):
        up_w, down_w = ((up_own, down_own), (up_other, down_other))[index // 2]
        cut = (index % 2) * chunk
        up_c = up_w[:, cut : cut + chunk]
        down_c = down_w[cut : cut + chunk, :]
        at = index * chunk
        slot = index % 2
        hid[slot] = mm(normed[...], up_c)
        grad_hid[slot] = mm(gm[...], down_c, NT)
        for row in range(0, TILE, 16):
            rows = pl.ds(row, 16)
            a, da = gelu_parts(hid[slot, rows, :])
            act[slot, rows, :] = a.astype(bf16)
            gu[slot, rows, :] = (grad_hid[slot, rows, :] * da).astype(bf16)
        part_m = mm(act[slot], down_c)
        part_n = mm(gu[slot], up_c, NT)
        if index == 0:
            mlp[...] = part_m
            grad_n[...] = part_n
        else:
            mlp[...] += part_m
            grad_n[...] += part_n
        acc_down[at : at + chunk, :] += mm(act[slot], gm[...], TN)
        acc_up[:, at : at + chunk] += mm(normed[...], gu[slot], TN)
    for row in range(0, TILE, 128):
        rows = pl.ds(row, 128)
        valid = valid_rows(row, 128)
        y = res[rows, :] + valid * mlp[rows, :]
        low, high = y[:, :HALF], y[:, HALF:]
        y_own[rows, :] = jnp.where(head == 0, low, high).astype(bf16)
        y_other[rows, :] = jnp.where(head == 0, high, low).astype(bf16)
        gn = grad_n[rows, :]
        hat = xhat[rows, :]
        acc_ln[0:1, :] += jnp.sum(gn * hat, axis=0, keepdims=True)
        acc_ln[1:2, :] += jnp.sum(gn, axis=0, keepdims=True)
        scaled = gn * ln[2:3, :]
        back = rstd_at[rows, :] * (
            scaled
            - jnp.mean(scaled, axis=1, keepdims=True)
            - hat * jnp.mean(scaled * hat, axis=1, keepdims=True)
        )
        dy = join_columns(head, dy_own[rows, :].astype(f32), dy_other[rows, :].astype(f32))
        gh = dy + back
        grad_res[rows, :] = gh
        ga[rows, :] = (valid * gh).astype(bf16)
    acc_out[...] += mm(ctx[...], ga[...], TN)
    grad_ctx[:, :HALF] = mm(ga[...], out_own[...], NT).astype(bf16)
    grad_ctx[:, HALF:] = mm(ga[...], out_other[...], NT).astype(bf16)

    @pl.when(step == TILES - 1)
    def _():
        g_out[...] = acc_out[...].astype(bf16)
        g_up[0] = acc_up[:, : FF // 2].astype(bf16)
        g_up[1] = acc_up[:, FF // 2 :].astype(bf16)
        g_down[...] = acc_down[...].astype(bf16)
        g_ln[...] = acc_ln[...]


def backward_attention(
    table,
    x_own,
    x_other,
    ln,
    w_own,
    w_other,
    qkv,
    bars,
    probs,
    grad_ctx,
    grad_res,
    gx_own,
    gx_other,
    g_qkv,
    g_ln,
    acc_qkv,
    acc_ln,
    after,
    grad_qkv,
    normed,
    grad_n,
):
    head = lax.axis_index("head")
    step = pl.program_id(0)

    @pl.when(step == 0)
    def _():
        acc_qkv[...] = jnp.zeros_like(acc_qkv)
        acc_ln[...] = jnp.zeros_like(acc_ln)
        after[...] = jnp.zeros_like(after)

    low_lanes, high_lanes = lane_masks(bf16)
    scale_factor = float(HEAD_DIM) ** (-0.5)
    for span in reversed(range(SPANS_TILE)):
        rows = pl.ds(span * SPAN, SPAN)
        row_id = (TILES - 1 - step) * SPANS_TILE + span
        inverse = table[0, row_id]
        for pair in range(PAIRS):
            at_q, at_k, at_v = pair_columns(pair)
            lanes = pl.ds(pair * 128, 128)
            lanes_v = pl.ds(512 + pair * 128, 128)
            keys = jnp.concatenate([qkv[rows, at_k : at_k + 128], bars[rows, lanes]], axis=0)
            values = jnp.concatenate([qkv[rows, at_v : at_v + 128], bars[rows, lanes_v]], axis=0)
            query = head_stack(qkv[rows, at_q : at_q + 128], low_lanes, high_lanes)
            grad = head_stack(grad_ctx[rows, lanes], low_lanes, high_lanes)
            prob = probs[span * PAIRS + pair]
            prob_f = prob.astype(f32)
            weighted = mm(values, grad, NT)
            weighted = weighted * prob_f
            delta = jnp.sum(weighted, axis=0, keepdims=True)
            score = (weighted - prob_f * delta).astype(bf16)
            grad_q = unstack_transposed(mm(keys, score, TN)) * scale_factor
            grad_k = mm(score, query)
            grad_v = mm(prob, grad)
            grad_qkv[rows, at_q : at_q + 128] = grad_q.astype(bf16)
            grad_qkv[rows, at_k : at_k + 128] = (grad_k[:SPAN] + after[:, lanes]).astype(bf16)
            grad_qkv[rows, at_v : at_v + 128] = (grad_v[:SPAN] + after[:, lanes_v]).astype(bf16)
            after[:, lanes] += grad_k[SPAN:] * inverse
            after[:, lanes_v] += grad_v[SPAN:] * inverse
    for row in range(0, TILE, 128):
        rows = pl.ds(row, 128)
        x = join_columns(head, x_own[rows, :].astype(f32), x_other[rows, :].astype(f32))
        hat, _ = norm_stats(x)
        normed[rows, :] = (hat * ln[0:1, :] + ln[1:2, :]).astype(bf16)
    for side, w in enumerate((w_own, w_other)):
        for part in range(3):
            at = side * 3 * HALF + part * HALF
            piece = grad_qkv[:, at : at + HALF]
            acc_qkv[side, part] += mm(normed[...], piece, TN)
            back = mm(piece, w[part], NT)
            if side == 0 and part == 0:
                grad_n[...] = back
            else:
                grad_n[...] += back
    for row in range(0, TILE, 128):
        rows = pl.ds(row, 128)
        x = join_columns(head, x_own[rows, :].astype(f32), x_other[rows, :].astype(f32))
        hat, rstd = norm_stats(x)
        gn = grad_n[rows, :]
        acc_ln[0:1, :] += jnp.sum(gn * hat, axis=0, keepdims=True)
        acc_ln[1:2, :] += jnp.sum(gn, axis=0, keepdims=True)
        scaled = gn * ln[0:1, :]
        back = rstd * (
            scaled
            - jnp.mean(scaled, axis=1, keepdims=True)
            - hat * jnp.mean(scaled * hat, axis=1, keepdims=True)
        )
        gx = grad_res[rows, :] + back
        low, high = gx[:, :HALF], gx[:, HALF:]
        gx_own[rows, :] = jnp.where(head == 0, low, high).astype(bf16)
        gx_other[rows, :] = jnp.where(head == 0, high, low).astype(bf16)

    @pl.when(step == TILES - 1)
    def _():
        g_qkv[...] = acc_qkv[...].astype(bf16)
        g_ln[...] = acc_ln[...]


def rows_spec(width, back=False):
    if back:
        return pl.BlockSpec((TILE, width), lambda i: (TILES - 1 - i, 0))
    return pl.BlockSpec((TILE, width), lambda i: (i, 0))


def probs_spec(back=False):
    shape = (SPANS_TILE * PAIRS, 2 * SPAN, 2 * SPAN)
    if back:
        return pl.BlockSpec(shape, lambda i: (TILES - 1 - i, 0, 0))
    return pl.BlockSpec(shape, lambda i: (i, 0, 0))


def whole_spec(shape):
    rank = len(shape)
    return pl.BlockSpec(shape, lambda i: (0,) * rank, pipeline_mode=pl.Buffered(1))


def shaped(shape, dtype=bf16):
    return jax.ShapeDtypeStruct(shape, dtype)


smem_spec = pl.BlockSpec(memory_space=pltpu.SMEM)
limits = pltpu.CompilerParams(vmem_limit_bytes=60 * 1024 * 1024)


def span_table():
    ids = np.arange(ROWS)
    inverse = 1.0 / np.maximum(ids, 1)
    shift = np.where(ids >= 1, np.log(np.maximum(ids, 1)), masked_score)
    return jnp.asarray(np.stack([inverse, shift]).astype(np.float32))


def causal_bias():
    key = np.arange(SPAN)[:, None]
    query = np.arange(2 * SPAN)[None, :] % SPAN
    return jnp.asarray(np.where(key <= query, 0.0, masked_score).astype(np.float32))


def layer_local(x_own, x_other, dy_own, dy_other, lengths, ln_params, weights):
    qkv_own, qkv_other, out_own, out_other, up_own, up_other, down_own, down_other = weights
    table = span_table()
    qkv, bars, probs, ctx = pl.pallas_call(
        forward_attention,
        grid=(TILES,),
        in_specs=[
            smem_spec,
            rows_spec(HALF),
            rows_spec(HALF),
            whole_spec((4, D)),
            whole_spec((3, D, HALF)),
            whole_spec((3, D, HALF)),
            whole_spec((SPAN, 2 * SPAN)),
        ],
        out_specs=[rows_spec(3 * D), rows_spec(2 * D), probs_spec(), rows_spec(D)],
        out_shape=[
            shaped((SEQ, 3 * D)),
            shaped((SEQ, 2 * D)),
            shaped((ROWS * PAIRS, 2 * SPAN, 2 * SPAN)),
            shaped((SEQ, D)),
        ],
        scratch_shapes=[pltpu.VMEM((SPAN, 2 * D), f32), pltpu.VMEM((TILE, D), bf16)],
        compiler_params=limits,
        name="forward_attention",
    )(table, x_own, x_other, ln_params, qkv_own, qkv_other, causal_bias())
    y_own, y_other, grad_res, grad_ctx, g_out, g_up, g_down, g_ln_two = pl.pallas_call(
        mlp_both_ways,
        grid=(TILES,),
        in_specs=[
            smem_spec,
            rows_spec(HALF),
            rows_spec(HALF),
            rows_spec(HALF),
            rows_spec(HALF),
            whole_spec((4, D)),
            rows_spec(D),
            whole_spec((HALF, D)),
            whole_spec((HALF, D)),
            whole_spec((D, FF // 2)),
            whole_spec((D, FF // 2)),
            whole_spec((FF // 2, D)),
            whole_spec((FF // 2, D)),
        ],
        out_specs=[
            rows_spec(HALF),
            rows_spec(HALF),
            rows_spec(D),
            rows_spec(D),
            whole_spec((D, D)),
            whole_spec((2, D, FF // 2)),
            whole_spec((FF, D)),
            whole_spec((2, D)),
        ],
        out_shape=[
            shaped((SEQ, HALF)),
            shaped((SEQ, HALF)),
            shaped((SEQ, D), f32),
            shaped((SEQ, D)),
            shaped((D, D)),
            shaped((2, D, FF // 2)),
            shaped((FF, D)),
            shaped((2, D), f32),
        ],
        scratch_shapes=[
            pltpu.VMEM((D, D), f32),
            pltpu.VMEM((D, FF), f32),
            pltpu.VMEM((FF, D), f32),
            pltpu.VMEM((2, D), f32),
            pltpu.VMEM((TILE, D), f32),
            pltpu.VMEM((TILE, D), f32),
            pltpu.VMEM((TILE, 1), f32),
            pltpu.VMEM((TILE, D), bf16),
            pltpu.VMEM((TILE, D), bf16),
            pltpu.VMEM((TILE, D), f32),
            pltpu.VMEM((TILE, D), f32),
            pltpu.VMEM((2, TILE, 512), f32),
            pltpu.VMEM((8, 128), f32),
            pltpu.VMEM((2, TILE, 512), bf16),
            pltpu.VMEM((2, TILE, 512), f32),
            pltpu.VMEM((2, TILE, 512), bf16),
            pltpu.VMEM((TILE, D), bf16),
        ],
        compiler_params=limits,
        name="mlp_both_ways",
    )(
        lengths,
        x_own,
        x_other,
        dy_own,
        dy_other,
        ln_params,
        ctx,
        out_own,
        out_other,
        up_own,
        up_other,
        down_own,
        down_other,
    )
    gx_own, gx_other, g_qkv, g_ln_one = pl.pallas_call(
        backward_attention,
        grid=(TILES,),
        in_specs=[
            smem_spec,
            rows_spec(HALF, True),
            rows_spec(HALF, True),
            whole_spec((4, D)),
            whole_spec((3, D, HALF)),
            whole_spec((3, D, HALF)),
            rows_spec(3 * D, True),
            rows_spec(2 * D, True),
            probs_spec(True),
            rows_spec(D, True),
            rows_spec(D, True),
        ],
        out_specs=[
            rows_spec(HALF, True),
            rows_spec(HALF, True),
            whole_spec((2, 3, D, HALF)),
            whole_spec((2, D)),
        ],
        out_shape=[
            shaped((SEQ, HALF)),
            shaped((SEQ, HALF)),
            shaped((2, 3, D, HALF)),
            shaped((2, D), f32),
        ],
        scratch_shapes=[
            pltpu.VMEM((2, 3, D, HALF), f32),
            pltpu.VMEM((2, D), f32),
            pltpu.VMEM((SPAN, 2 * D), f32),
            pltpu.VMEM((TILE, 3 * D), bf16),
            pltpu.VMEM((TILE, D), bf16),
            pltpu.VMEM((TILE, D), f32),
        ],
        compiler_params=limits,
        name="backward_attention",
    )(table, x_own, x_other, ln_params, qkv_own, qkv_other, qkv, bars, probs, grad_ctx, grad_res)
    return (
        (y_own, y_other),
        (gx_own, gx_other),
        g_qkv,
        g_out.reshape(2, HALF, D),
        g_up,
        g_down.reshape(2, FF // 2, D),
        jnp.concatenate([g_ln_one, g_ln_two], axis=0),
    )


def swap_heads(value):
    return lax.ppermute(value, "head", [(0, 1), (1, 0)])


def adam_step(gradient, weight, moment_one, moment_two, step_rate):
    first_new = beta_one * moment_one + (1.0 - beta_one) * gradient
    second_new = beta_two * moment_two + (1.0 - beta_two) * gradient * gradient
    first_hat = first_new / (1.0 - beta_one**STEP)
    second_hat = second_new / (1.0 - beta_two**STEP)
    weight_new = weight - step_rate * (
        first_hat / (jnp.sqrt(second_hat) + epsilon_adam) + decay_rate * weight
    )
    return (weight_new, first_new, second_new)


def gather_inputs(tokens, cotangent, w_qkv, w_out, w_up, w_down):
    head = lax.axis_index("head")

    def both(array):
        halves = array.reshape(2, SEQ, HALF)
        own = lax.dynamic_index_in_dim(halves, head, 0, keepdims=False)
        other = lax.dynamic_index_in_dim(halves, 1 - head, 0, keepdims=False)
        return own, swap_heads(other)

    x_own, x_other = both(tokens)
    qkv_own = w_qkv.transpose(1, 0, 2).astype(bf16)
    out_own = w_out.astype(bf16)
    up_own = w_up.astype(bf16)
    down_own = w_down.astype(bf16)
    qkv_other = swap_heads(qkv_own)
    dy_own, dy_other = both(cotangent)
    weights = (
        qkv_own,
        qkv_other,
        out_own,
        swap_heads(out_own),
        up_own,
        swap_heads(up_own),
        down_own,
        swap_heads(down_own),
    )
    return x_own, x_other, dy_own, dy_other, weights


def place_rows(pieces):
    head = lax.axis_index("head")
    own, away = pieces
    arrived = swap_heads(away)
    return jnp.concatenate(
        [jnp.where(head == 0, own, arrived), jnp.where(head == 0, arrived, own)], axis=0
    )


def body(
    tokens,
    cotangent,
    lengths,
    owners,
    w_qkv,
    w_out,
    w_up,
    w_down,
    ln_params,
    m_qkv,
    m_out,
    m_up,
    m_down,
    m_ln,
    v_qkv,
    v_out,
    v_up,
    v_down,
    v_ln,
):
    x_own, x_other, dy_own, dy_other, weights = gather_inputs(
        tokens, cotangent, w_qkv, w_out, w_up, w_down
    )
    y, gx, g_qkv, g_out, g_up, g_down, g_ln = layer_local(
        x_own, x_other, dy_own, dy_other, lengths, ln_params, weights
    )
    output_rows = place_rows(y)
    grad_input = place_rows(gx)
    halves = []
    for grad in (g_qkv, g_out, g_up, g_down):
        halves.append(grad[0].astype(f32) + swap_heads(grad[1]).astype(f32))
    summed = [lax.psum(half.astype(bf16), "dp").astype(f32) for half in halves]
    summed[0] = summed[0].transpose(1, 0, 2)
    summed.append(lax.psum(g_ln, ("dp", "head")))
    masters = (w_qkv, w_out, w_up, w_down, ln_params)
    firsts = (m_qkv, m_out, m_up, m_down, m_ln)
    seconds = (v_qkv, v_out, v_up, v_down, v_ln)
    rates = (
        float(D) ** (-0.5),
        4.0 * float(D) ** (-0.5),
        float(D) ** (-0.5),
        float(FF) ** (-0.5),
        0.7,
    )
    updated = [
        adam_step(
            summed[kind_index],
            masters[kind_index],
            firsts[kind_index],
            seconds[kind_index],
            rates[kind_index],
        )
        for kind_index in range(5)
    ]
    new_weights = tuple((entry[0] for entry in updated))
    new_firsts = tuple((entry[1] for entry in updated))
    new_seconds = tuple((entry[2] for entry in updated))
    device_index = lax.axis_index("dp")
    owned_grads = tuple(
        (
            jnp.where(owners[kind_index] == device_index, summed[kind_index], 0.0)[None]
            for kind_index in range(5)
        )
    )
    copies = tuple((new_weights[kind_index].astype(jnp.bfloat16) for kind_index in range(4)))
    return (
        (output_rows, grad_input)
        + owned_grads
        + tuple(new_weights)
        + tuple(new_firsts)
        + tuple(new_seconds)
        + copies
    )


PLACED = (
    (P("dp", "head"),) * 2
    + (P("dp"), P())
    + (P(None, None, "head"), P("head", None), P(None, "head"), P("head", None), P()) * 3
)
RESULTS = (
    (P("dp", "head"),) * 2
    + (
        P("dp", None, None, "head"),
        P("dp", "head", None),
        P("dp", None, "head"),
        P("dp", "head", None),
        P("dp", None, None),
    )
    + (P(None, None, "head"), P("head", None), P(None, "head"), P("head", None), P()) * 3
    + (P(None, None, "head"), P("head", None), P(None, "head"), P("head", None))
)


def solution(mesh):
    return jax.shard_map(
        body, mesh=mesh, in_specs=PLACED, out_specs=RESULTS, check_vma=False
    )
```

```python
import functools

import jax
import jax.numpy as jnp
import numpy as np
from jax import lax
from jax.experimental import pallas as pl
from jax.experimental.pallas import tpu as pltpu
from jax.sharding import PartitionSpec as P

D = 512
HALF = 256
HEAD_DIM = 64
FF = 2048
SPAN = 128
SEQ = 2048
STEP = 5
ROWS = 16
PAIRS = 4
TILE = 512
TILES = SEQ // TILE
SPANS_TILE = TILE // SPAN

epsilon_norm = 1e-05
epsilon_adam = 1e-08
beta_one = 0.5
beta_two = 0.5
decay_rate = 0.1
masked_score = -1e30

bf16 = jnp.bfloat16
f32 = jnp.float32

NN = (((1,), (0,)), ((), ()))
NT = (((1,), (1,)), ((), ()))
TN = (((0,), (0,)), ((), ()))


def mm(left, right, dims=NN):
    return lax.dot_general(left, right, dims, preferred_element_type=f32)


def join_columns(head, own, other):
    low = jnp.where(head == 0, own, other)
    high = jnp.where(head == 0, other, own)
    return jnp.concatenate([low, high], axis=1)


def norm_stats(values):
    mean = jnp.mean(values, axis=1, keepdims=True)
    centered = values - mean
    rstd = lax.rsqrt(jnp.mean(centered * centered, axis=1, keepdims=True) + epsilon_norm)
    return centered * rstd, rstd


def head_stack(pair, low_lanes, high_lanes):
    return jnp.concatenate([pair * low_lanes, pair * high_lanes], axis=0)


def lane_masks(dtype):
    lane = lax.broadcasted_iota(jnp.int32, (1, 2 * HEAD_DIM), 1)
    low = (lane < HEAD_DIM).astype(f32)
    return low.astype(dtype), (1.0 - low).astype(dtype)


def pair_columns(pair):
    base = 3 * HALF * (pair // 2) + 2 * HEAD_DIM * (pair % 2)
    return base, base + HALF, base + 2 * HALF


def unstack_transposed(product):
    joined = jnp.concatenate(
        [product[:HEAD_DIM, :SPAN], product[HEAD_DIM:, SPAN:]], axis=0
    )
    return joined.T


def forward_attention(
    table, x_own, x_other, ln, w_own, w_other, causal, qkv, bars, probs, ctx, run_sum, normed
):
    head = lax.axis_index("head")
    step = pl.program_id(0)

    @pl.when(step == 0)
    def _():
        run_sum[...] = jnp.zeros_like(run_sum)

    for row in range(0, TILE, 128):
        rows = pl.ds(row, 128)
        x = join_columns(head, x_own[rows, :].astype(f32), x_other[rows, :].astype(f32))
        xhat, _ = norm_stats(x)
        normed[rows, :] = (xhat * ln[0:1, :] + ln[1:2, :]).astype(bf16)
    for side, w in enumerate((w_own, w_other)):
        for part in range(3):
            value = mm(normed[...], w[part])
            if part == 0:
                value = value * float(HEAD_DIM) ** (-0.5)
            base = side * 3 * HALF + part * HALF
            qkv[:, base : base + HALF] = value.astype(bf16)
    low_lanes, high_lanes = lane_masks(bf16)
    for span in range(SPANS_TILE):
        rows = pl.ds(span * SPAN, SPAN)
        row_id = step * SPANS_TILE + span
        inverse = table[0, row_id]
        shift = table[1, row_id]
        for pair in range(PAIRS):
            at_q, at_k, at_v = pair_columns(pair)
            lanes = pl.ds(pair * 128, 128)
            lanes_v = pl.ds(512 + pair * 128, 128)
            key = qkv[rows, at_k : at_k + 128]
            value = qkv[rows, at_v : at_v + 128]
            key_bar = (run_sum[:, lanes] * inverse).astype(bf16)
            value_bar = (run_sum[:, lanes_v] * inverse).astype(bf16)
            run_sum[:, lanes] += key.astype(f32)
            run_sum[:, lanes_v] += value.astype(f32)
            bars[rows, lanes] = key_bar
            bars[rows, lanes_v] = value_bar
            query = head_stack(qkv[rows, at_q : at_q + 128], low_lanes, high_lanes)
            direct = mm(key, query, NT) + causal[...]
            summary = mm(key_bar, query, NT) + shift
            top = jnp.maximum(
                jnp.max(direct, axis=0, keepdims=True), jnp.max(summary, axis=0, keepdims=True)
            )
            direct = jnp.exp(direct - top)
            summary = jnp.exp(summary - top)
            total = jnp.sum(direct, axis=0, keepdims=True) + jnp.sum(
                summary, axis=0, keepdims=True
            )
            scale = 1.0 / total
            direct = (direct * scale).astype(bf16)
            summary = (summary * scale).astype(bf16)
            slot = span * PAIRS + pair
            probs[slot, :SPAN, :] = direct
            probs[slot, SPAN:, :] = summary
            values = jnp.concatenate([value, value_bar], axis=0)
            both = jnp.concatenate([direct, summary], axis=0)
            ctx[rows, lanes] = unstack_transposed(mm(values, both, TN)).astype(bf16)


def gelu_parts(u):
    size = jnp.abs(u)
    bell = jnp.exp(u * u * -0.5)
    denom = 1.0 + (0.3275911 * 0.7071067811865476) * size
    t = 1.0 / denom
    poly = t * (
        0.5 * 0.254829592
        + t
        * (
            0.5 * -0.284496736
            + t * (0.5 * 1.421413741 + t * (0.5 * -1.453152027 + t * (0.5 * 1.061405429)))
        )
    )
    tail = poly * bell
    share = jnp.where(u >= 0.0, 1.0 - tail, tail)
    return u * share, share + u * bell * 0.3989422804014327


def mlp_both_ways(
    lengths,
    x_own,
    x_other,
    dy_own,
    dy_other,
    ln,
    ctx,
    out_own,
    out_other,
    up_own,
    up_other,
    down_own,
    down_other,
    y_own,
    y_other,
    grad_res,
    grad_ctx,
    g_out,
    g_up,
    g_down,
    g_ln,
    acc_out,
    acc_up,
    acc_down,
    acc_ln,
    res,
    xhat,
    rstd_at,
    normed,
    gm,
    mlp,
    grad_n,
    hid,
    slope,
    act,
    grad_hid,
    gu,
    ga,
):
    head = lax.axis_index("head")
    step = pl.program_id(0)
    used = lengths[head]

    @pl.when(step == 0)
    def _():
        acc_out[...] = jnp.zeros_like(acc_out)
        acc_up[...] = jnp.zeros_like(acc_up)
        acc_down[...] = jnp.zeros_like(acc_down)
        acc_ln[...] = jnp.zeros_like(acc_ln)

    def valid_rows(row, count):
        ids = lax.broadcasted_iota(jnp.int32, (count, 1), 0) + (step * TILE + row)
        return (ids < used).astype(f32)

    res[...] = mm(ctx[:, :HALF], out_own[...]) + mm(ctx[:, HALF:], out_other[...])
    for row in range(0, TILE, 128):
        rows = pl.ds(row, 128)
        valid = valid_rows(row, 128)
        x = join_columns(head, x_own[rows, :].astype(f32), x_other[rows, :].astype(f32))
        h = x + valid * res[rows, :]
        res[rows, :] = h
        hat, rstd = norm_stats(h)
        xhat[rows, :] = hat
        rstd_at[rows, :] = rstd
        normed[rows, :] = (hat * ln[2:3, :] + ln[3:4, :]).astype(bf16)
        dy = join_columns(head, dy_own[rows, :].astype(f32), dy_other[rows, :].astype(f32))
        gm[rows, :] = (valid * dy).astype(bf16)
    chunk = 512
    for index in range(FF // chunk):
        up_w, down_w = ((up_own, down_own), (up_other, down_other))[index // 2]
        cut = (index % 2) * chunk
        up_c = up_w[:, cut : cut + chunk]
        down_c = down_w[cut : cut + chunk, :]
        at = index * chunk
        slot = index % 2
        hid[slot] = mm(normed[...], up_c)
        grad_hid[slot] = mm(gm[...], down_c, NT)
        for row in range(0, TILE, 16):
            rows = pl.ds(row, 16)
            a, da = gelu_parts(hid[slot, rows, :])
            act[slot, rows, :] = a.astype(bf16)
            gu[slot, rows, :] = (grad_hid[slot, rows, :] * da).astype(bf16)
        part_m = mm(act[slot], down_c)
        part_n = mm(gu[slot], up_c, NT)
        if index == 0:
            mlp[...] = part_m
            grad_n[...] = part_n
        else:
            mlp[...] += part_m
            grad_n[...] += part_n
        acc_down[at : at + chunk, :] += mm(act[slot], gm[...], TN)
        acc_up[:, at : at + chunk] += mm(normed[...], gu[slot], TN)
    for row in range(0, TILE, 128):
        rows = pl.ds(row, 128)
        valid = valid_rows(row, 128)
        y = res[rows, :] + valid * mlp[rows, :]
        low, high = y[:, :HALF], y[:, HALF:]
        y_own[rows, :] = jnp.where(head == 0, low, high).astype(bf16)
        y_other[rows, :] = jnp.where(head == 0, high, low).astype(bf16)
        gn = grad_n[rows, :]
        hat = xhat[rows, :]
        acc_ln[0:1, :] += jnp.sum(gn * hat, axis=0, keepdims=True)
        acc_ln[1:2, :] += jnp.sum(gn, axis=0, keepdims=True)
        scaled = gn * ln[2:3, :]
        back = rstd_at[rows, :] * (
            scaled
            - jnp.mean(scaled, axis=1, keepdims=True)
            - hat * jnp.mean(scaled * hat, axis=1, keepdims=True)
        )
        dy = join_columns(head, dy_own[rows, :].astype(f32), dy_other[rows, :].astype(f32))
        gh = dy + back
        grad_res[rows, :] = gh
        ga[rows, :] = (valid * gh).astype(bf16)
    acc_out[...] += mm(ctx[...], ga[...], TN)
    grad_ctx[:, :HALF] = mm(ga[...], out_own[...], NT).astype(bf16)
    grad_ctx[:, HALF:] = mm(ga[...], out_other[...], NT).astype(bf16)

    @pl.when(step == TILES - 1)
    def _():
        for side in range(2):
            for part in range(2):
                lanes = slice(part * HALF, (part + 1) * HALF)
                g_out[side, part] = acc_out[side * HALF : (side + 1) * HALF, lanes].astype(bf16)
                g_down[side, part] = acc_down[side * 1024 : (side + 1) * 1024, lanes].astype(bf16)
                for block in range(2):
                    at = side * 1024 + block * D + part * HALF
                    rows = slice(block * D, (block + 1) * D)
                    g_up[side, part, rows] = acc_up[:, at : at + HALF].astype(bf16)
        g_ln[...] = acc_ln[...]


def backward_attention(
    table,
    x_own,
    x_other,
    ln,
    w_own,
    w_other,
    qkv,
    bars,
    probs,
    grad_ctx,
    grad_res,
    gx_own,
    gx_other,
    g_qkv,
    g_ln,
    acc_qkv,
    acc_ln,
    after,
    grad_qkv,
    normed,
    grad_n,
):
    head = lax.axis_index("head")
    step = pl.program_id(0)

    @pl.when(step == 0)
    def _():
        acc_qkv[...] = jnp.zeros_like(acc_qkv)
        acc_ln[...] = jnp.zeros_like(acc_ln)
        after[...] = jnp.zeros_like(after)

    low_lanes, high_lanes = lane_masks(bf16)
    scale_factor = float(HEAD_DIM) ** (-0.5)
    for span in reversed(range(SPANS_TILE)):
        rows = pl.ds(span * SPAN, SPAN)
        row_id = (TILES - 1 - step) * SPANS_TILE + span
        inverse = table[0, row_id]
        for pair in range(PAIRS):
            at_q, at_k, at_v = pair_columns(pair)
            lanes = pl.ds(pair * 128, 128)
            lanes_v = pl.ds(512 + pair * 128, 128)
            keys = jnp.concatenate([qkv[rows, at_k : at_k + 128], bars[rows, lanes]], axis=0)
            values = jnp.concatenate([qkv[rows, at_v : at_v + 128], bars[rows, lanes_v]], axis=0)
            query = head_stack(qkv[rows, at_q : at_q + 128], low_lanes, high_lanes)
            grad = head_stack(grad_ctx[rows, lanes], low_lanes, high_lanes)
            prob = probs[span * PAIRS + pair]
            prob_f = prob.astype(f32)
            weighted = mm(values, grad, NT)
            weighted = weighted * prob_f
            delta = jnp.sum(weighted, axis=0, keepdims=True)
            score = (weighted - prob_f * delta).astype(bf16)
            grad_q = unstack_transposed(mm(keys, score, TN)) * scale_factor
            grad_k = mm(score, query)
            grad_v = mm(prob, grad)
            grad_qkv[rows, at_q : at_q + 128] = grad_q.astype(bf16)
            grad_qkv[rows, at_k : at_k + 128] = (grad_k[:SPAN] + after[:, lanes]).astype(bf16)
            grad_qkv[rows, at_v : at_v + 128] = (grad_v[:SPAN] + after[:, lanes_v]).astype(bf16)
            after[:, lanes] += grad_k[SPAN:] * inverse
            after[:, lanes_v] += grad_v[SPAN:] * inverse
    for row in range(0, TILE, 128):
        rows = pl.ds(row, 128)
        x = join_columns(head, x_own[rows, :].astype(f32), x_other[rows, :].astype(f32))
        hat, _ = norm_stats(x)
        normed[rows, :] = (hat * ln[0:1, :] + ln[1:2, :]).astype(bf16)
    for side, w in enumerate((w_own, w_other)):
        for part in range(3):
            at = side * 3 * HALF + part * HALF
            piece = grad_qkv[:, at : at + HALF]
            acc_qkv[side, part] += mm(normed[...], piece, TN)
            back = mm(piece, w[part], NT)
            if side == 0 and part == 0:
                grad_n[...] = back
            else:
                grad_n[...] += back
    for row in range(0, TILE, 128):
        rows = pl.ds(row, 128)
        x = join_columns(head, x_own[rows, :].astype(f32), x_other[rows, :].astype(f32))
        hat, rstd = norm_stats(x)
        gn = grad_n[rows, :]
        acc_ln[0:1, :] += jnp.sum(gn * hat, axis=0, keepdims=True)
        acc_ln[1:2, :] += jnp.sum(gn, axis=0, keepdims=True)
        scaled = gn * ln[0:1, :]
        back = rstd * (
            scaled
            - jnp.mean(scaled, axis=1, keepdims=True)
            - hat * jnp.mean(scaled * hat, axis=1, keepdims=True)
        )
        gx = grad_res[rows, :] + back
        low, high = gx[:, :HALF], gx[:, HALF:]
        gx_own[rows, :] = jnp.where(head == 0, low, high).astype(bf16)
        gx_other[rows, :] = jnp.where(head == 0, high, low).astype(bf16)

    @pl.when(step == TILES - 1)
    def _():
        for side in range(2):
            for part in range(2):
                for kind in range(3):
                    rows = slice(kind * HALF, (kind + 1) * HALF)
                    half = slice(part * HALF, (part + 1) * HALF)
                    g_qkv[side, part, rows] = acc_qkv[side, kind, half].astype(bf16)
        g_ln[...] = acc_ln[...]


def rows_spec(width, back=False):
    if back:
        return pl.BlockSpec((TILE, width), lambda i: (TILES - 1 - i, 0))
    return pl.BlockSpec((TILE, width), lambda i: (i, 0))


def probs_spec(back=False):
    shape = (SPANS_TILE * PAIRS, 2 * SPAN, 2 * SPAN)
    if back:
        return pl.BlockSpec(shape, lambda i: (TILES - 1 - i, 0, 0))
    return pl.BlockSpec(shape, lambda i: (i, 0, 0))


def whole_spec(shape):
    rank = len(shape)
    return pl.BlockSpec(shape, lambda i: (0,) * rank, pipeline_mode=pl.Buffered(1))


def shaped(shape, dtype=bf16):
    return jax.ShapeDtypeStruct(shape, dtype)


smem_spec = pl.BlockSpec(memory_space=pltpu.SMEM)
limits = pltpu.CompilerParams(vmem_limit_bytes=60 * 1024 * 1024)


def span_table():
    ids = np.arange(ROWS)
    inverse = 1.0 / np.maximum(ids, 1)
    shift = np.where(ids >= 1, np.log(np.maximum(ids, 1)), masked_score)
    return jnp.asarray(np.stack([inverse, shift]).astype(np.float32))


def causal_bias():
    key = np.arange(SPAN)[:, None]
    query = np.arange(2 * SPAN)[None, :] % SPAN
    return jnp.asarray(np.where(key <= query, 0.0, masked_score).astype(np.float32))


def layer_local(x_own, x_other, dy_own, dy_other, lengths, ln_params, weights):
    qkv_own, qkv_other, out_own, out_other, up_own, up_other, down_own, down_other = weights
    table = span_table()
    qkv, bars, probs, ctx = pl.pallas_call(
        forward_attention,
        grid=(TILES,),
        in_specs=[
            smem_spec,
            rows_spec(HALF),
            rows_spec(HALF),
            whole_spec((4, D)),
            whole_spec((3, D, HALF)),
            whole_spec((3, D, HALF)),
            whole_spec((SPAN, 2 * SPAN)),
        ],
        out_specs=[rows_spec(3 * D), rows_spec(2 * D), probs_spec(), rows_spec(D)],
        out_shape=[
            shaped((SEQ, 3 * D)),
            shaped((SEQ, 2 * D)),
            shaped((ROWS * PAIRS, 2 * SPAN, 2 * SPAN)),
            shaped((SEQ, D)),
        ],
        scratch_shapes=[pltpu.VMEM((SPAN, 2 * D), f32), pltpu.VMEM((TILE, D), bf16)],
        compiler_params=limits,
        name="forward_attention",
    )(table, x_own, x_other, ln_params, qkv_own, qkv_other, causal_bias())
    y_own, y_other, grad_res, grad_ctx, g_out, g_up, g_down, g_ln_two = pl.pallas_call(
        mlp_both_ways,
        grid=(TILES,),
        in_specs=[
            smem_spec,
            rows_spec(HALF),
            rows_spec(HALF),
            rows_spec(HALF),
            rows_spec(HALF),
            whole_spec((4, D)),
            rows_spec(D),
            whole_spec((HALF, D)),
            whole_spec((HALF, D)),
            whole_spec((D, FF // 2)),
            whole_spec((D, FF // 2)),
            whole_spec((FF // 2, D)),
            whole_spec((FF // 2, D)),
        ],
        out_specs=[
            rows_spec(HALF),
            rows_spec(HALF),
            rows_spec(D),
            rows_spec(D),
            whole_spec((2, 2, HALF, HALF)),
            whole_spec((2, 2, 1024, HALF)),
            whole_spec((2, 2, 1024, HALF)),
            whole_spec((2, D)),
        ],
        out_shape=[
            shaped((SEQ, HALF)),
            shaped((SEQ, HALF)),
            shaped((SEQ, D), f32),
            shaped((SEQ, D)),
            shaped((2, 2, HALF, HALF)),
            shaped((2, 2, 1024, HALF)),
            shaped((2, 2, 1024, HALF)),
            shaped((2, D), f32),
        ],
        scratch_shapes=[
            pltpu.VMEM((D, D), f32),
            pltpu.VMEM((D, FF), f32),
            pltpu.VMEM((FF, D), f32),
            pltpu.VMEM((2, D), f32),
            pltpu.VMEM((TILE, D), f32),
            pltpu.VMEM((TILE, D), f32),
            pltpu.VMEM((TILE, 1), f32),
            pltpu.VMEM((TILE, D), bf16),
            pltpu.VMEM((TILE, D), bf16),
            pltpu.VMEM((TILE, D), f32),
            pltpu.VMEM((TILE, D), f32),
            pltpu.VMEM((2, TILE, 512), f32),
            pltpu.VMEM((8, 128), f32),
            pltpu.VMEM((2, TILE, 512), bf16),
            pltpu.VMEM((2, TILE, 512), f32),
            pltpu.VMEM((2, TILE, 512), bf16),
            pltpu.VMEM((TILE, D), bf16),
        ],
        compiler_params=limits,
        name="mlp_both_ways",
    )(
        lengths,
        x_own,
        x_other,
        dy_own,
        dy_other,
        ln_params,
        ctx,
        out_own,
        out_other,
        up_own,
        up_other,
        down_own,
        down_other,
    )
    gx_own, gx_other, g_qkv, g_ln_one = pl.pallas_call(
        backward_attention,
        grid=(TILES,),
        in_specs=[
            smem_spec,
            rows_spec(HALF, True),
            rows_spec(HALF, True),
            whole_spec((4, D)),
            whole_spec((3, D, HALF)),
            whole_spec((3, D, HALF)),
            rows_spec(3 * D, True),
            rows_spec(2 * D, True),
            probs_spec(True),
            rows_spec(D, True),
            rows_spec(D, True),
        ],
        out_specs=[
            rows_spec(HALF, True),
            rows_spec(HALF, True),
            whole_spec((2, 2, 3 * HALF, HALF)),
            whole_spec((2, D)),
        ],
        out_shape=[
            shaped((SEQ, HALF)),
            shaped((SEQ, HALF)),
            shaped((2, 2, 3 * HALF, HALF)),
            shaped((2, D), f32),
        ],
        scratch_shapes=[
            pltpu.VMEM((2, 3, D, HALF), f32),
            pltpu.VMEM((2, D), f32),
            pltpu.VMEM((SPAN, 2 * D), f32),
            pltpu.VMEM((TILE, 3 * D), bf16),
            pltpu.VMEM((TILE, D), bf16),
            pltpu.VMEM((TILE, D), f32),
        ],
        compiler_params=limits,
        name="backward_attention",
    )(table, x_own, x_other, ln_params, qkv_own, qkv_other, qkv, bars, probs, grad_ctx, grad_res)
    return (
        (y_own, y_other),
        (gx_own, gx_other),
        g_qkv,
        g_out,
        g_up,
        g_down,
        jnp.concatenate([g_ln_one, g_ln_two], axis=0),
    )


def swap_heads(value):
    return lax.ppermute(value, "head", [(0, 1), (1, 0)])


def chip_grid(count):
    side = 1 << ((count.bit_length() - 1) // 3)
    return (count // (side * side), side, side)


class Lines:
    def __init__(self, count):
        self.sizes = chip_grid(count)
        self.strides = (self.sizes[1] * self.sizes[2], self.sizes[2], 1)
        self.chip = lax.axis_index("dp")
        self.head = lax.axis_index("head")
        self.places = [
            lax.rem(self.chip // stride, size) for stride, size in zip(self.strides, self.sizes)
        ]

    def partner(self):
        return (self.chip, 1 - self.head)

    def member(self, axis, ahead):
        size = self.sizes[axis]
        place = lax.rem(self.places[axis] + ahead, size)
        chip = self.chip + (place - self.places[axis]) * self.strides[axis]
        return place, (chip, self.head)

    def greet(self):
        barrier = pltpu.get_barrier_semaphore()
        others = [self.partner()]
        for axis in range(3):
            others += [self.member(axis, ahead)[1] for ahead in range(1, self.sizes[axis])]
        for other in others:
            pl.semaphore_signal(
                barrier, inc=1, device_id=other, device_id_type=pl.DeviceIdType.MESH
            )
        pl.semaphore_wait(barrier, len(others))


ORDERS = ((2, 1, 0), (1, 2, 0))


def padded_rows(rows, count):
    unit = 16 * count
    return -(-rows // unit) * unit


def chunk_rows(rows):
    return next(chunk for chunk in (64, 48, 32, 16) if rows % chunk == 0)


def sum_scratch(rows, count):
    sizes = chip_grid(count)
    shapes = [
        pltpu.VMEM((2, rows, HALF), bf16),
        pltpu.VMEM((2, rows, HALF), bf16),
        pltpu.VMEM((2, rows, HALF), bf16),
    ]
    sems = [pltpu.SemaphoreType.DMA((2,))]
    for order in ORDERS:
        left = rows
        for axis in order:
            left //= sizes[axis]
            shapes.append(pltpu.VMEM((sizes[axis] - 1, left, HALF), bf16))
            sems.append(pltpu.SemaphoreType.DMA((2, 2, sizes[axis] - 1)))
    return shapes + sems


class DpSum:
    def __init__(self, lines, grads, total, scratch):
        self.lines = lines
        self.grads = grads
        self.total = total
        self.rows = total.shape[1]
        self.used = grads.shape[2]
        self.work, self.arrived, self.final = scratch[:3]
        self.slots = (scratch[3:6], scratch[6:9])
        self.core_sem = scratch[9]
        self.sems = (scratch[10:13], scratch[13:16])
        self.base = [[0], [0]]
        self.length = [self.rows, self.rows]

    def remote(self, source, target, send_sem, recv_sem, device):
        return pltpu.make_async_remote_copy(
            src_ref=source,
            dst_ref=target,
            send_sem=send_sem,
            recv_sem=recv_sem,
            device_id=device,
            device_id_type=pl.DeviceIdType.MESH,
        )

    def core_copy(self):
        return self.remote(
            self.grads.at[1],
            self.arrived.at[:, pl.ds(0, self.used)],
            self.core_sem.at[0],
            self.core_sem.at[1],
            self.lines.partner(),
        )

    def core_send(self):
        self.core_copy().start()

    def core_sum(self):
        self.core_copy().wait()
        chunk = chunk_rows(self.used)
        for part in range(2):

            def add(index, carry, part=part):
                rows = pl.ds(pl.multiple_of(index * chunk, chunk), chunk)
                own = self.grads[0, part, rows, :].astype(f32)
                away = self.arrived[part, rows, :].astype(f32)
                self.work[part, rows, :] = (own + away).astype(bf16)
                return carry

            lax.fori_loop(0, self.used // chunk, add, 0)

    def spread_copies(self, part, stage):
        axis = ORDERS[part][stage]
        size = self.lines.sizes[axis]
        base = self.base[part][stage]
        piece = self.rows
        for at in ORDERS[part][: stage + 1]:
            piece //= self.lines.sizes[at]
        copies = []
        for ahead in range(1, size):
            place, device = self.lines.member(axis, ahead)
            start = pl.multiple_of(base + place * piece, 16)
            copies.append(
                self.remote(
                    self.work.at[part, pl.ds(start, piece)],
                    self.slots[part][stage].at[ahead - 1],
                    self.sems[part][stage].at[0, 0, ahead - 1],
                    self.sems[part][stage].at[0, 1, ahead - 1],
                    device,
                )
            )
        mine = base + self.lines.places[axis] * piece
        return copies, mine, piece

    def spread_send(self, part, stage):
        copies, mine, _ = self.spread_copies(part, stage)
        for copy in copies:
            copy.start()
        self.base[part] = self.base[part][: stage + 1] + [mine]

    def spread_sum(self, part, stage):
        copies, mine, piece = self.spread_copies(part, stage)
        for copy in copies:
            copy.wait()
        slots = self.slots[part][stage]
        target = self.final if stage == 2 else self.work
        chunk = chunk_rows(piece)

        def add(index, carry):
            offset = pl.multiple_of(index * chunk, chunk)
            rows = pl.ds(pl.multiple_of(mine + offset, 16), chunk)
            value = self.work[part, rows, :].astype(f32)
            for slot in range(len(copies)):
                value = value + slots[slot, pl.ds(offset, chunk), :].astype(f32)
            target[part, rows, :] = value.astype(bf16)
            return carry

        lax.fori_loop(0, piece // chunk, add, 0)

    def gather_copies(self, part, stage):
        axis = ORDERS[part][stage]
        size = self.lines.sizes[axis]
        piece = self.rows
        for at in ORDERS[part][: stage + 1]:
            piece //= self.lines.sizes[at]
        mine = pl.multiple_of(self.base[part][stage + 1], 16)
        rows = pl.ds(mine, piece)
        copies = []
        for ahead in range(1, size):
            _, device = self.lines.member(axis, ahead)
            copies.append(
                self.remote(
                    self.final.at[part, rows],
                    self.final.at[part, rows],
                    self.sems[part][stage].at[1, 0, ahead - 1],
                    self.sems[part][stage].at[1, 1, ahead - 1],
                    device,
                )
            )
        return copies

    def gather_send(self, part, stage):
        for copy in self.gather_copies(part, stage):
            copy.start()

    def gather_wait(self, part, stage):
        for copy in self.gather_copies(part, stage):
            copy.wait()

    def store(self):
        self.total[...] = self.final[...]


def both_parts(sums, action, stage):
    for entry in sums:
        for part in range(2):
            getattr(entry, action)(part, stage)


def ln_scratch(count):
    return [
        pltpu.VMEM((2, 4, D), f32),
        pltpu.SemaphoreType.DMA((2,)),
        *[pltpu.VMEM((size, 4, D), f32) for size in chip_grid(count)],
        *[pltpu.SemaphoreType.DMA((2, max(size - 1, 1))) for size in chip_grid(count)],
    ]


class LnSum:
    def __init__(self, lines, value, total, scratch):
        self.lines = lines
        self.value = value
        self.total = total
        self.core, self.core_sem = scratch[:2]
        self.slots = scratch[2:5]
        self.sems = scratch[5:8]

    def stage_copies(self, stage):
        lines = self.lines
        if stage == 0:
            mine = self.core.at[lines.head]
            return [
                pltpu.make_async_remote_copy(
                    src_ref=mine,
                    dst_ref=mine,
                    send_sem=self.core_sem.at[0],
                    recv_sem=self.core_sem.at[1],
                    device_id=lines.partner(),
                    device_id_type=pl.DeviceIdType.MESH,
                )
            ]
        axis = stage - 1
        mine = self.slots[axis].at[lines.places[axis]]
        return [
            pltpu.make_async_remote_copy(
                src_ref=mine,
                dst_ref=mine,
                send_sem=self.sems[axis].at[0, ahead - 1],
                recv_sem=self.sems[axis].at[1, ahead - 1],
                device_id=lines.member(axis, ahead)[1],
                device_id_type=pl.DeviceIdType.MESH,
            )
            for ahead in range(1, lines.sizes[axis])
        ]

    def send(self, stage):
        if stage == 0:
            self.core[self.lines.head] = self.value[...]
        for copy in self.stage_copies(stage):
            copy.start()

    def finish(self, stage):
        for copy in self.stage_copies(stage):
            copy.wait()
        slots = self.core if stage == 0 else self.slots[stage - 1]
        value = slots[0]
        for slot in range(1, slots.shape[0]):
            value = value + slots[slot]
        if stage == 3:
            self.total[...] = value
        else:
            self.slots[stage][self.lines.places[stage]] = value


def sum_kernel(count, kinds, *refs):
    grads, ln = refs[:kinds], refs[kinds]
    totals, ln_total = refs[kinds + 1 : 2 * kinds + 1], refs[2 * kinds + 1]
    scratch = refs[2 * kinds + 2 :]
    lines = Lines(count)
    each = 16
    sums = [
        DpSum(lines, grads[kind], totals[kind], scratch[kind * each : (kind + 1) * each])
        for kind in range(kinds)
    ]
    small = LnSum(lines, ln, ln_total, scratch[kinds * each :])
    lines.greet()
    for entry in sums:
        entry.core_send()
    small.send(0)
    for entry in sums:
        entry.core_sum()
        both_parts([entry], "spread_send", 0)
    small.finish(0)
    small.send(1)
    for stage in range(3):
        for entry in sums:
            both_parts([entry], "spread_sum", stage)
            if stage < 2:
                both_parts([entry], "spread_send", stage + 1)
            else:
                both_parts([entry], "gather_send", 2)
        small.finish(stage + 1)
        if stage < 2:
            small.send(stage + 2)
    for stage in reversed(range(3)):
        for entry in sums:
            both_parts([entry], "gather_wait", stage)
            if stage > 0:
                both_parts([entry], "gather_send", stage - 1)
            else:
                entry.store()


def sum_over_all(grads, ln):
    count = lax.axis_size("dp")
    kinds = len(grads)
    rows = [padded_rows(grad.shape[2], count) for grad in grads]
    vmem = pl.BlockSpec(memory_space=pltpu.VMEM)
    scratch = []
    for count_rows in rows:
        scratch += sum_scratch(count_rows, count)
    scratch += ln_scratch(count)
    return pl.pallas_call(
        functools.partial(sum_kernel, count, kinds),
        in_specs=[vmem] * (kinds + 1),
        out_specs=[vmem] * (kinds + 1),
        out_shape=[shaped((2, count_rows, HALF)) for count_rows in rows] + [shaped((4, D), f32)],
        scratch_shapes=scratch,
        compiler_params=pltpu.CompilerParams(
            collective_id=0, has_side_effects=True, vmem_limit_bytes=60 * 1024 * 1024
        ),
        name="sum_over_all",
    )(*grads, ln)


RATES = (
    float(D) ** (-0.5),
    4.0 * float(D) ** (-0.5),
    float(D) ** (-0.5),
    float(FF) ** (-0.5),
    0.7,
)


def adam_step(gradient, weight, moment_one, moment_two, step_rate):
    first_new = beta_one * moment_one + (1.0 - beta_one) * gradient
    second_new = beta_two * moment_two + (1.0 - beta_two) * gradient * gradient
    first_hat = first_new * (1.0 / (1.0 - beta_one**STEP))
    second_hat = second_new * (1.0 / (1.0 - beta_two**STEP))
    weight_new = weight - step_rate * (
        first_hat / (jnp.sqrt(second_hat) + epsilon_adam) + decay_rate * weight
    )
    return (weight_new, first_new, second_new)


def kind_gradient(kind, ref):
    if kind == 0:
        return jnp.concatenate([ref[0, 0], ref[1, 0]], axis=0).astype(f32)[None]
    if kind == 2:
        blocks = [ref[part, block] for block in range(2) for part in range(2)]
        return jnp.concatenate(blocks, axis=1).astype(f32)
    return jnp.concatenate([ref[0], ref[1]], axis=1).astype(f32)


BLOCKS = (
    (3, (1, D, HALF), (2, 1, HALF, HALF)),
    (1, (HALF, D), (2, HALF, HALF)),
    (4, (128, 1024), (2, 2, 128, HALF)),
    (4, (HALF, D), (2, HALF, HALF)),
)


def adam_kernel(kinds, owners, *refs):
    step = pl.program_id(0)
    chip = lax.axis_index("dp")
    count = len(kinds)
    first = 0
    for index, kind in enumerate(kinds):
        grad, weight, one, two = refs[index * 4 : index * 4 + 4]
        owned, new, first_new, second_new, copy = refs[
            count * 4 + index * 5 : count * 4 + index * 5 + 5
        ]
        steps = BLOCKS[kind][0]

        @pl.when((step >= first) & (step < first + steps))
        def _(kind=kind, grad=grad, weight=weight, one=one, two=two, owned=owned, new=new,
              first_new=first_new, second_new=second_new, copy=copy):
            gradient = kind_gradient(kind, grad)
            results = adam_step(gradient, weight[...], one[...], two[...], RATES[kind])
            owned[...] = jnp.where(owners[kind] == chip, gradient, 0.0)
            new[...] = results[0]
            first_new[...] = results[1]
            second_new[...] = results[2]
            copy[...] = results[0].astype(bf16)

        first += steps


def adam_update(kinds, owners, grads, weights, ones, twos):
    in_specs, out_specs, out_shape, operands = [smem_spec], [], [], [owners]
    first = 0
    for index, kind in enumerate(kinds):
        steps, block, grad_block = BLOCKS[kind]

        def place(i, first=first, steps=steps):
            return jnp.clip(i - first, 0, steps - 1)

        def at(i, place=place, rank=len(block)):
            return (place(i),) + (0,) * (rank - 1)

        def grad_at(i, place=place, kind=kind):
            if kind == 0:
                return (0, place(i), 0, 0)
            if kind == 2:
                return (0, 0, place(i), 0)
            return (0, place(i), 0)

        spec = pl.BlockSpec(block, at)
        in_specs += [pl.BlockSpec(grad_block, grad_at), spec, spec, spec]
        out_specs += [spec] * 5
        whole = weights[index].shape
        out_shape += [shaped(whole, f32)] * 4 + [shaped(whole)]
        operands += [grads[index], weights[index], ones[index], twos[index]]
        first += steps
    results = pl.pallas_call(
        functools.partial(adam_kernel, kinds),
        grid=(first,),
        in_specs=in_specs,
        out_specs=out_specs,
        out_shape=out_shape,
        compiler_params=limits,
        name="adam_update",
    )(*operands)
    return [results[index * 5 : index * 5 + 5] for index in range(len(kinds))]


def gather_inputs(tokens, cotangent, w_qkv, w_out, w_up, w_down):
    head = lax.axis_index("head")

    def both(array):
        halves = array.reshape(2, SEQ, HALF)
        own = lax.dynamic_index_in_dim(halves, head, 0, keepdims=False)
        other = lax.dynamic_index_in_dim(halves, 1 - head, 0, keepdims=False)
        return own, swap_heads(other)

    x_own, x_other = both(tokens)
    qkv_own = w_qkv.transpose(1, 0, 2).astype(bf16)
    out_own = w_out.astype(bf16)
    up_own = w_up.astype(bf16)
    down_own = w_down.astype(bf16)
    qkv_other = swap_heads(qkv_own)
    dy_own, dy_other = both(cotangent)
    weights = (
        qkv_own,
        qkv_other,
        out_own,
        swap_heads(out_own),
        up_own,
        swap_heads(up_own),
        down_own,
        swap_heads(down_own),
    )
    return x_own, x_other, dy_own, dy_other, weights


def place_rows(pieces):
    head = lax.axis_index("head")
    own, away = pieces
    arrived = swap_heads(away)
    return jnp.concatenate(
        [jnp.where(head == 0, own, arrived), jnp.where(head == 0, arrived, own)], axis=0
    )


def body(
    tokens,
    cotangent,
    lengths,
    owners,
    w_qkv,
    w_out,
    w_up,
    w_down,
    ln_params,
    m_qkv,
    m_out,
    m_up,
    m_down,
    m_ln,
    v_qkv,
    v_out,
    v_up,
    v_down,
    v_ln,
):
    x_own, x_other, dy_own, dy_other, weights = gather_inputs(
        tokens, cotangent, w_qkv, w_out, w_up, w_down
    )
    y, gx, g_qkv, g_out, g_up, g_down, g_ln = layer_local(
        x_own, x_other, dy_own, dy_other, lengths, ln_params, weights
    )
    output_rows = place_rows(y)
    grad_input = place_rows(gx)
    totals = sum_over_all((g_down, g_up, g_out, g_qkv), g_ln)
    t_down, t_up, t_out, t_qkv = [
        total[:, :rows] for total, rows in zip(totals, (1024, 1024, HALF, 3 * HALF))
    ]

    def as_blocks(array):
        return array.transpose(1, 0, 2)

    t_ln = totals[4]
    results = adam_update(
        (0, 1, 2, 3),
        owners,
        (t_qkv.reshape(2, 3, HALF, HALF), t_out, t_up.reshape(2, 2, D, HALF), t_down),
        (as_blocks(w_qkv), w_out, w_up, w_down),
        (as_blocks(m_qkv), m_out, m_up, m_down),
        (as_blocks(v_qkv), v_out, v_up, v_down),
    )
    results[0] = [as_blocks(array) for array in results[0]]
    mine = owners[4] == lax.axis_index("dp")
    ln_results = adam_step(t_ln, ln_params, m_ln, v_ln, RATES[4])
    results.append([jnp.where(mine, t_ln, 0.0), *ln_results])
    owned, new, first, second = [
        tuple(results[kind][slot] for kind in range(5)) for slot in range(4)
    ]
    copies = tuple(results[kind][4] for kind in range(4))
    owned = tuple(array[None] for array in owned)
    return (output_rows, grad_input) + owned + new + first + second + copies


PLACED = (
    (P("dp", "head"),) * 2
    + (P("dp"), P())
    + (P(None, None, "head"), P("head", None), P(None, "head"), P("head", None), P()) * 3
)
RESULTS = (
    (P("dp", "head"),) * 2
    + (
        P("dp", None, None, "head"),
        P("dp", "head", None),
        P("dp", None, "head"),
        P("dp", "head", None),
        P("dp", None, None),
    )
    + (P(None, None, "head"), P("head", None), P(None, "head"), P("head", None), P()) * 3
    + (P(None, None, "head"), P("head", None), P(None, "head"), P("head", None))
)


def solution(mesh):
    return jax.shard_map(
        body, mesh=mesh, in_specs=PLACED, out_specs=RESULTS, check_vma=False
    )
```

```python
import functools

import jax
import jax.numpy as jnp
import numpy as np
from jax import lax
from jax.experimental import pallas as pl
from jax.experimental.pallas import tpu as pltpu
from jax.sharding import PartitionSpec as P

D = 512
HALF = 256
HEAD_DIM = 64
FF = 2048
SPAN = 128
SEQ = 2048
STEP = 5
ROWS = 16
PAIRS = 4
TILE = 512
TILES = SEQ // TILE
SPANS_TILE = TILE // SPAN

epsilon_norm = 1e-05
epsilon_adam = 1e-08
beta_one = 0.5
beta_two = 0.5
decay_rate = 0.1
masked_score = -1e30

bf16 = jnp.bfloat16
f32 = jnp.float32

NN = (((1,), (0,)), ((), ()))
NT = (((1,), (1,)), ((), ()))
TN = (((0,), (0,)), ((), ()))


def mm(left, right, dims=NN):
    return lax.dot_general(left, right, dims, preferred_element_type=f32)


def join_columns(head, own, other):
    low = jnp.where(head == 0, own, other)
    high = jnp.where(head == 0, other, own)
    return jnp.concatenate([low, high], axis=1)


def norm_stats(values):
    mean = jnp.mean(values, axis=1, keepdims=True)
    centered = values - mean
    rstd = lax.rsqrt(jnp.mean(centered * centered, axis=1, keepdims=True) + epsilon_norm)
    return centered * rstd, rstd


def head_stack(pair, low_lanes, high_lanes):
    return jnp.concatenate([pair * low_lanes, pair * high_lanes], axis=0)


def lane_masks(dtype):
    lane = lax.broadcasted_iota(jnp.int32, (1, 2 * HEAD_DIM), 1)
    low = (lane < HEAD_DIM).astype(f32)
    return low.astype(dtype), (1.0 - low).astype(dtype)


def pair_columns(pair):
    base = 3 * HALF * (pair // 2) + 2 * HEAD_DIM * (pair % 2)
    return base, base + HALF, base + 2 * HALF


def unstack_transposed(product):
    joined = jnp.concatenate(
        [product[:HEAD_DIM, :SPAN], product[HEAD_DIM:, SPAN:]], axis=0
    )
    return joined.T


def forward_attention(
    table, x_own, x_other, ln, w_own, w_other, causal, qkv, bars, probs, ctx, run_sum, normed
):
    head = lax.axis_index("head")
    step = pl.program_id(0)

    @pl.when(step == 0)
    def _():
        run_sum[...] = jnp.zeros_like(run_sum)

    for row in range(0, TILE, 128):
        rows = pl.ds(row, 128)
        x = join_columns(head, x_own[rows, :].astype(f32), x_other[rows, :].astype(f32))
        xhat, _ = norm_stats(x)
        normed[rows, :] = (xhat * ln[0:1, :] + ln[1:2, :]).astype(bf16)
    for side, w in enumerate((w_own, w_other)):
        for part in range(3):
            value = mm(normed[...], w[part])
            if part == 0:
                value = value * float(HEAD_DIM) ** (-0.5)
            base = side * 3 * HALF + part * HALF
            qkv[:, base : base + HALF] = value.astype(bf16)
    low_lanes, high_lanes = lane_masks(bf16)
    for span in range(SPANS_TILE):
        rows = pl.ds(span * SPAN, SPAN)
        row_id = step * SPANS_TILE + span
        inverse = table[0, row_id]
        shift = table[1, row_id]
        for pair in range(PAIRS):
            at_q, at_k, at_v = pair_columns(pair)
            lanes = pl.ds(pair * 128, 128)
            lanes_v = pl.ds(512 + pair * 128, 128)
            key = qkv[rows, at_k : at_k + 128]
            value = qkv[rows, at_v : at_v + 128]
            key_bar = (run_sum[:, lanes] * inverse).astype(bf16)
            value_bar = (run_sum[:, lanes_v] * inverse).astype(bf16)
            run_sum[:, lanes] += key.astype(f32)
            run_sum[:, lanes_v] += value.astype(f32)
            bars[rows, lanes] = key_bar
            bars[rows, lanes_v] = value_bar
            query = head_stack(qkv[rows, at_q : at_q + 128], low_lanes, high_lanes)
            direct = mm(key, query, NT) + causal[...]
            summary = mm(key_bar, query, NT) + shift
            top = jnp.maximum(
                jnp.max(direct, axis=0, keepdims=True), jnp.max(summary, axis=0, keepdims=True)
            )
            direct = jnp.exp(direct - top)
            summary = jnp.exp(summary - top)
            total = jnp.sum(direct, axis=0, keepdims=True) + jnp.sum(
                summary, axis=0, keepdims=True
            )
            scale = 1.0 / total
            direct = (direct * scale).astype(bf16)
            summary = (summary * scale).astype(bf16)
            slot = span * PAIRS + pair
            probs[slot, :SPAN, :] = direct
            probs[slot, SPAN:, :] = summary
            values = jnp.concatenate([value, value_bar], axis=0)
            both = jnp.concatenate([direct, summary], axis=0)
            ctx[rows, lanes] = unstack_transposed(mm(values, both, TN)).astype(bf16)


def gelu_parts(u):
    size = jnp.abs(u)
    bell = jnp.exp(u * u * -0.5)
    denom = 1.0 + (0.3275911 * 0.7071067811865476) * size
    t = 1.0 / denom
    poly = t * (
        0.5 * 0.254829592
        + t
        * (
            0.5 * -0.284496736
            + t * (0.5 * 1.421413741 + t * (0.5 * -1.453152027 + t * (0.5 * 1.061405429)))
        )
    )
    tail = poly * bell
    share = jnp.where(u >= 0.0, 1.0 - tail, tail)
    return u * share, share + u * bell * 0.3989422804014327


def mlp_both_ways(
    lengths,
    x_own,
    x_other,
    dy_own,
    dy_other,
    ln,
    ctx,
    out_own,
    out_other,
    up_own,
    up_other,
    down_own,
    down_other,
    y_own,
    y_other,
    grad_res,
    grad_ctx,
    g_out,
    g_up,
    g_down,
    g_ln,
    acc_out,
    acc_up,
    acc_down,
    acc_ln,
    res,
    xhat,
    rstd_at,
    normed,
    gm,
    mlp,
    grad_n,
    hid,
    slope,
    act,
    grad_hid,
    gu,
    ga,
):
    head = lax.axis_index("head")
    step = pl.program_id(0)
    used = lengths[head]

    @pl.when(step == 0)
    def _():
        acc_out[...] = jnp.zeros_like(acc_out)
        acc_up[...] = jnp.zeros_like(acc_up)
        acc_down[...] = jnp.zeros_like(acc_down)
        acc_ln[...] = jnp.zeros_like(acc_ln)

    def valid_rows(row, count):
        ids = lax.broadcasted_iota(jnp.int32, (count, 1), 0) + (step * TILE + row)
        return (ids < used).astype(f32)

    res[...] = mm(ctx[:, :HALF], out_own[...]) + mm(ctx[:, HALF:], out_other[...])
    for row in range(0, TILE, 128):
        rows = pl.ds(row, 128)
        valid = valid_rows(row, 128)
        x = join_columns(head, x_own[rows, :].astype(f32), x_other[rows, :].astype(f32))
        h = x + valid * res[rows, :]
        res[rows, :] = h
        hat, rstd = norm_stats(h)
        xhat[rows, :] = hat
        rstd_at[rows, :] = rstd
        normed[rows, :] = (hat * ln[2:3, :] + ln[3:4, :]).astype(bf16)
        dy = join_columns(head, dy_own[rows, :].astype(f32), dy_other[rows, :].astype(f32))
        gm[rows, :] = (valid * dy).astype(bf16)
    chunk = 512
    for index in range(FF // chunk):
        up_w, down_w = ((up_own, down_own), (up_other, down_other))[index // 2]
        cut = (index % 2) * chunk
        up_c = up_w[:, cut : cut + chunk]
        down_c = down_w[cut : cut + chunk, :]
        at = index * chunk
        slot = index % 2
        hid[slot] = mm(normed[...], up_c)
        grad_hid[slot] = mm(gm[...], down_c, NT)
        for row in range(0, TILE, 16):
            rows = pl.ds(row, 16)
            a, da = gelu_parts(hid[slot, rows, :])
            act[slot, rows, :] = a.astype(bf16)
            gu[slot, rows, :] = (grad_hid[slot, rows, :] * da).astype(bf16)
        part_m = mm(act[slot], down_c)
        part_n = mm(gu[slot], up_c, NT)
        if index == 0:
            mlp[...] = part_m
            grad_n[...] = part_n
        else:
            mlp[...] += part_m
            grad_n[...] += part_n
        acc_down[at : at + chunk, :] += mm(act[slot], gm[...], TN)
        acc_up[:, at : at + chunk] += mm(normed[...], gu[slot], TN)
    for row in range(0, TILE, 128):
        rows = pl.ds(row, 128)
        valid = valid_rows(row, 128)
        y = res[rows, :] + valid * mlp[rows, :]
        low, high = y[:, :HALF], y[:, HALF:]
        y_own[rows, :] = jnp.where(head == 0, low, high).astype(bf16)
        y_other[rows, :] = jnp.where(head == 0, high, low).astype(bf16)
        gn = grad_n[rows, :]
        hat = xhat[rows, :]
        acc_ln[0:1, :] += jnp.sum(gn * hat, axis=0, keepdims=True)
        acc_ln[1:2, :] += jnp.sum(gn, axis=0, keepdims=True)
        scaled = gn * ln[2:3, :]
        back = rstd_at[rows, :] * (
            scaled
            - jnp.mean(scaled, axis=1, keepdims=True)
            - hat * jnp.mean(scaled * hat, axis=1, keepdims=True)
        )
        dy = join_columns(head, dy_own[rows, :].astype(f32), dy_other[rows, :].astype(f32))
        gh = dy + back
        grad_res[rows, :] = gh
        ga[rows, :] = (valid * gh).astype(bf16)
    acc_out[...] += mm(ctx[...], ga[...], TN)
    grad_ctx[:, :HALF] = mm(ga[...], out_own[...], NT).astype(bf16)
    grad_ctx[:, HALF:] = mm(ga[...], out_other[...], NT).astype(bf16)

    @pl.when(step == TILES - 1)
    def _():
        for side in range(2):
            for part in range(2):
                lanes = slice(part * HALF, (part + 1) * HALF)
                g_out[side, part] = acc_out[side * HALF : (side + 1) * HALF, lanes].astype(bf16)
                g_down[side, part] = acc_down[side * 1024 : (side + 1) * 1024, lanes].astype(bf16)
                for block in range(2):
                    at = side * 1024 + block * D + part * HALF
                    rows = slice(block * D, (block + 1) * D)
                    g_up[side, part, rows] = acc_up[:, at : at + HALF].astype(bf16)
        g_ln[...] = acc_ln[...]


def swap_heads(value):
    return lax.ppermute(value, "head", [(0, 1), (1, 0)])


def chip_grid(count):
    side = 1 << ((count.bit_length() - 1) // 3)
    return (count // (side * side), side, side)


class Lines:
    def __init__(self, count):
        self.sizes = chip_grid(count)
        self.strides = (self.sizes[1] * self.sizes[2], self.sizes[2], 1)
        self.chip = lax.axis_index("dp")
        self.head = lax.axis_index("head")
        self.places = [
            lax.rem(self.chip // stride, size) for stride, size in zip(self.strides, self.sizes)
        ]

    def partner(self):
        return (self.chip, 1 - self.head)

    def member(self, axis, ahead):
        size = self.sizes[axis]
        place = lax.rem(self.places[axis] + ahead, size)
        chip = self.chip + (place - self.places[axis]) * self.strides[axis]
        return place, (chip, self.head)

    def greet(self):
        barrier = pltpu.get_barrier_semaphore()
        others = [self.partner()]
        for axis in range(3):
            others += [self.member(axis, ahead)[1] for ahead in range(1, self.sizes[axis])]
        for other in others:
            pl.semaphore_signal(
                barrier, inc=1, device_id=other, device_id_type=pl.DeviceIdType.MESH
            )
        pl.semaphore_wait(barrier, len(others))


ORDERS = ((2, 1, 0), (1, 2, 0))


def whole_slices(count):
    return all(rows % (16 * count) == 0 for rows in PIECE_ROWS + (3 * HALF,))


def chunk_rows(rows):
    return next(chunk for chunk in (64, 48, 32, 16) if rows % chunk == 0)


def sum_scratch(rows, count):
    sizes = chip_grid(count)
    shapes = [
        pltpu.VMEM((2, rows, HALF), bf16),
        pltpu.VMEM((2, rows, HALF), bf16),
        pltpu.VMEM((2, rows, HALF), bf16),
    ]
    sems = [pltpu.SemaphoreType.DMA((2,))]
    for order in ORDERS:
        left = rows
        for axis in order:
            left //= sizes[axis]
            shapes.append(pltpu.VMEM((sizes[axis] - 1, left, HALF), bf16))
            sems.append(pltpu.SemaphoreType.DMA((2, 2, sizes[axis] - 1)))
    return shapes + sems + [pltpu.SemaphoreType.DMA((1,))]


class DpSum:
    def __init__(self, lines, grads, total, scratch):
        self.lines = lines
        self.grads = grads
        self.total = total
        self.rows = grads.shape[2]
        self.work, self.arrived, self.final = scratch[:3]
        self.slots = (scratch[3:6], scratch[6:9])
        self.core_sem = scratch[9]
        self.sems = (scratch[10:13], scratch[13:16])
        self.store_sem = scratch[16]
        self.base = []
        for order in ORDERS:
            bases, piece = [0], self.rows
            for axis in order:
                piece //= lines.sizes[axis]
                bases.append(bases[-1] + lines.places[axis] * piece)
            self.base.append(bases)

    def remote(self, source, target, send_sem, recv_sem, device):
        return pltpu.make_async_remote_copy(
            src_ref=source,
            dst_ref=target,
            send_sem=send_sem,
            recv_sem=recv_sem,
            device_id=device,
            device_id_type=pl.DeviceIdType.MESH,
        )

    def core_copy(self):
        return self.remote(
            self.grads.at[1],
            self.arrived,
            self.core_sem.at[0],
            self.core_sem.at[1],
            self.lines.partner(),
        )

    def core_send(self):
        self.core_copy().start()

    def core_sum(self):
        self.core_copy().wait()
        chunk = chunk_rows(self.rows)
        for part in range(2):

            def add(index, carry, part=part):
                rows = pl.ds(pl.multiple_of(index * chunk, chunk), chunk)
                own = self.grads[0, part, rows, :].astype(f32)
                away = self.arrived[part, rows, :].astype(f32)
                self.work[part, rows, :] = (own + away).astype(bf16)
                return carry

            lax.fori_loop(0, self.rows // chunk, add, 0)

    def spread_copies(self, part, stage):
        axis = ORDERS[part][stage]
        size = self.lines.sizes[axis]
        base = self.base[part][stage]
        piece = self.rows
        for at in ORDERS[part][: stage + 1]:
            piece //= self.lines.sizes[at]
        copies = []
        for ahead in range(1, size):
            place, device = self.lines.member(axis, ahead)
            start = pl.multiple_of(base + place * piece, 16)
            copies.append(
                self.remote(
                    self.work.at[part, pl.ds(start, piece)],
                    self.slots[part][stage].at[ahead - 1],
                    self.sems[part][stage].at[0, 0, ahead - 1],
                    self.sems[part][stage].at[0, 1, ahead - 1],
                    device,
                )
            )
        return copies, self.base[part][stage + 1], piece

    def spread_send(self, part, stage):
        for copy in self.spread_copies(part, stage)[0]:
            copy.start()

    def spread_sum(self, part, stage):
        copies, mine, piece = self.spread_copies(part, stage)
        for copy in copies:
            copy.wait()
        slots = self.slots[part][stage]
        target = self.final if stage == 2 else self.work
        chunk = chunk_rows(piece)

        def add(index, carry):
            offset = pl.multiple_of(index * chunk, chunk)
            rows = pl.ds(pl.multiple_of(mine + offset, 16), chunk)
            value = self.work[part, rows, :].astype(f32)
            for slot in range(len(copies)):
                value = value + slots[slot, pl.ds(offset, chunk), :].astype(f32)
            target[part, rows, :] = value.astype(bf16)
            return carry

        lax.fori_loop(0, piece // chunk, add, 0)

    def gather_copies(self, part, stage):
        axis = ORDERS[part][stage]
        size = self.lines.sizes[axis]
        piece = self.rows
        for at in ORDERS[part][: stage + 1]:
            piece //= self.lines.sizes[at]
        mine = pl.multiple_of(self.base[part][stage + 1], 16)
        rows = pl.ds(mine, piece)
        copies = []
        for ahead in range(1, size):
            _, device = self.lines.member(axis, ahead)
            copies.append(
                self.remote(
                    self.final.at[part, rows],
                    self.final.at[part, rows],
                    self.sems[part][stage].at[1, 0, ahead - 1],
                    self.sems[part][stage].at[1, 1, ahead - 1],
                    device,
                )
            )
        return copies

    def gather_send(self, part, stage):
        for copy in self.gather_copies(part, stage):
            copy.start()

    def gather_wait(self, part, stage):
        for copy in self.gather_copies(part, stage):
            copy.wait()

    def store_copy(self):
        return pltpu.make_async_copy(self.final, self.total, self.store_sem.at[0])

    def event(self, index):
        if index == 0:
            self.core_send()
        elif index == 1:
            self.core_sum()
        for part in range(2):
            if 2 <= index <= 4:
                self.spread_sum(part, index - 2)
            elif index >= 5:
                self.gather_wait(part, 7 - index)
            if 1 <= index <= 3:
                self.spread_send(part, index - 1)
            elif 4 <= index <= 6:
                self.gather_send(part, 6 - index)
        if index == 7:
            self.store_copy().start()

    def finish(self):
        self.store_copy().wait()


EVENTS = 8


def ln_scratch(count):
    return [
        pltpu.VMEM((2, 4, D), f32),
        pltpu.SemaphoreType.DMA((2,)),
        *[pltpu.VMEM((size, 4, D), f32) for size in chip_grid(count)],
        *[pltpu.SemaphoreType.DMA((2, max(size - 1, 1))) for size in chip_grid(count)],
    ]


class LnSum:
    def __init__(self, lines, value, total, scratch):
        self.lines = lines
        self.value = value
        self.total = total
        self.core, self.core_sem = scratch[:2]
        self.slots = scratch[2:5]
        self.sems = scratch[5:8]

    def stage_copies(self, stage):
        lines = self.lines
        if stage == 0:
            mine = self.core.at[lines.head]
            return [
                pltpu.make_async_remote_copy(
                    src_ref=mine,
                    dst_ref=mine,
                    send_sem=self.core_sem.at[0],
                    recv_sem=self.core_sem.at[1],
                    device_id=lines.partner(),
                    device_id_type=pl.DeviceIdType.MESH,
                )
            ]
        axis = stage - 1
        mine = self.slots[axis].at[lines.places[axis]]
        return [
            pltpu.make_async_remote_copy(
                src_ref=mine,
                dst_ref=mine,
                send_sem=self.sems[axis].at[0, ahead - 1],
                recv_sem=self.sems[axis].at[1, ahead - 1],
                device_id=lines.member(axis, ahead)[1],
                device_id_type=pl.DeviceIdType.MESH,
            )
            for ahead in range(1, lines.sizes[axis])
        ]

    def send(self, stage):
        if stage == 0:
            self.core[self.lines.head] = self.value[...]
        for copy in self.stage_copies(stage):
            copy.start()

    def finish(self, stage):
        for copy in self.stage_copies(stage):
            copy.wait()
        slots = self.core if stage == 0 else self.slots[stage - 1]
        value = slots[0]
        for slot in range(1, slots.shape[0]):
            value = value + slots[slot]
        if stage == 3:
            self.total[...] = value
        else:
            self.slots[stage][self.lines.places[stage]] = value


SCRATCH_EACH = 17
PIECES = ((0, 0), (0, 512), (1, 0), (1, 512), (2, 0))
PIECE_ROWS = (512, 512, 512, 512, HALF)
SLOT_AT_HOOK = {0: 0, 1: 1, 3: 2, 4: 3, 6: 4, 7: 5, 9: 6, 10: 7}


def backward_attention(
    count,
    table,
    x_own,
    x_other,
    ln,
    w_own,
    w_other,
    qkv,
    bars,
    probs,
    grad_ctx,
    grad_res,
    g_down,
    g_up,
    g_out,
    g_ln_two,
    gx_own,
    gx_other,
    *refs,
):
    summing = whole_slices(count)
    kinds = len(PIECES) + 1 if summing else 1
    totals, ln_total = refs[:kinds], refs[kinds]
    acc_qkv, acc_ln, after, grad_qkv, normed, grad_n, g_qkv, ln_all = refs[kinds + 1 : kinds + 9]
    scratch = refs[kinds + 9 :]
    head = lax.axis_index("head")
    step = pl.program_id(0)
    sums = []
    if summing:
        lines = Lines(count)
        sources = (g_down, g_up, g_out)
        for index, (source, start) in enumerate(PIECES):
            view = sources[source].at[:, :, pl.ds(start, PIECE_ROWS[index])]
            part_scratch = scratch[index * SCRATCH_EACH : (index + 1) * SCRATCH_EACH]
            sums.append(DpSum(lines, view, totals[index], part_scratch))
        last = len(PIECES)
        end = (last + 1) * SCRATCH_EACH
        last_sum = DpSum(lines, g_qkv, totals[last], scratch[last * SCRATCH_EACH : end])
        small = LnSum(lines, ln_all, ln_total, scratch[end:])

    def run_slot(slot):
        for index, entry in enumerate(sums):
            if 0 <= slot - index < EVENTS:
                entry.event(slot - index)

    def hook(place):
        for at in range(TILES if summing else 0):
            slot = SLOT_AT_HOOK.get(at * 3 + place)
            if slot is None:
                continue

            @pl.when(step == at)
            def _(slot=slot):
                if slot == 0:
                    lines.greet()
                run_slot(slot)

    @pl.when(step == 0)
    def _():
        acc_qkv[...] = jnp.zeros_like(acc_qkv)
        acc_ln[...] = jnp.zeros_like(acc_ln)
        after[...] = jnp.zeros_like(after)

    low_lanes, high_lanes = lane_masks(bf16)
    scale_factor = float(HEAD_DIM) ** (-0.5)

    def attention(span):
        rows = pl.ds(span * SPAN, SPAN)
        row_id = (TILES - 1 - step) * SPANS_TILE + span
        inverse = table[0, row_id]
        for pair in range(PAIRS):
            at_q, at_k, at_v = pair_columns(pair)
            lanes = pl.ds(pair * 128, 128)
            lanes_v = pl.ds(512 + pair * 128, 128)
            keys = jnp.concatenate([qkv[rows, at_k : at_k + 128], bars[rows, lanes]], axis=0)
            values = jnp.concatenate([qkv[rows, at_v : at_v + 128], bars[rows, lanes_v]], axis=0)
            query = head_stack(qkv[rows, at_q : at_q + 128], low_lanes, high_lanes)
            grad = head_stack(grad_ctx[rows, lanes], low_lanes, high_lanes)
            prob = probs[span * PAIRS + pair]
            prob_f = prob.astype(f32)
            weighted = mm(values, grad, NT)
            weighted = weighted * prob_f
            delta = jnp.sum(weighted, axis=0, keepdims=True)
            score = (weighted - prob_f * delta).astype(bf16)
            grad_q = unstack_transposed(mm(keys, score, TN)) * scale_factor
            grad_k = mm(score, query)
            grad_v = mm(prob, grad)
            grad_qkv[rows, at_q : at_q + 128] = grad_q.astype(bf16)
            grad_qkv[rows, at_k : at_k + 128] = (grad_k[:SPAN] + after[:, lanes]).astype(bf16)
            grad_qkv[rows, at_v : at_v + 128] = (grad_v[:SPAN] + after[:, lanes_v]).astype(bf16)
            after[:, lanes] += grad_k[SPAN:] * inverse
            after[:, lanes_v] += grad_v[SPAN:] * inverse

    hook(0)
    attention(3)
    attention(2)
    hook(1)
    attention(1)
    attention(0)
    hook(2)
    for row in range(0, TILE, 128):
        rows = pl.ds(row, 128)
        x = join_columns(head, x_own[rows, :].astype(f32), x_other[rows, :].astype(f32))
        hat, _ = norm_stats(x)
        normed[rows, :] = (hat * ln[0:1, :] + ln[1:2, :]).astype(bf16)
    for side, w in enumerate((w_own, w_other)):
        for part in range(3):
            at = side * 3 * HALF + part * HALF
            piece = grad_qkv[:, at : at + HALF]
            acc_qkv[side, part] += mm(normed[...], piece, TN)
            back = mm(piece, w[part], NT)
            if side == 0 and part == 0:
                grad_n[...] = back
            else:
                grad_n[...] += back
    for row in range(0, TILE, 128):
        rows = pl.ds(row, 128)
        x = join_columns(head, x_own[rows, :].astype(f32), x_other[rows, :].astype(f32))
        hat, rstd = norm_stats(x)
        gn = grad_n[rows, :]
        acc_ln[0:1, :] += jnp.sum(gn * hat, axis=0, keepdims=True)
        acc_ln[1:2, :] += jnp.sum(gn, axis=0, keepdims=True)
        scaled = gn * ln[0:1, :]
        back = rstd * (
            scaled
            - jnp.mean(scaled, axis=1, keepdims=True)
            - hat * jnp.mean(scaled * hat, axis=1, keepdims=True)
        )
        gx = grad_res[rows, :] + back
        low, high = gx[:, :HALF], gx[:, HALF:]
        gx_own[rows, :] = jnp.where(head == 0, low, high).astype(bf16)
        gx_other[rows, :] = jnp.where(head == 0, high, low).astype(bf16)

    @pl.when(step == TILES - 1)
    def _():
        for side in range(2):
            for part in range(2):
                for kind in range(3):
                    rows = slice(kind * HALF, (kind + 1) * HALF)
                    half = slice(part * HALF, (part + 1) * HALF)
                    g_qkv[side, part, rows] = acc_qkv[side, kind, half].astype(bf16)
        ln_all[0:2, :] = acc_ln[...]
        ln_all[2:4, :] = g_ln_two[...]
        if not summing:
            totals[0][...] = g_qkv[...]
            ln_total[...] = ln_all[...]
            return
        late = len(SLOT_AT_HOOK)
        for index in range(EVENTS):
            last_sum.event(index)
            if 1 <= index <= 4:
                small.finish(index - 1)
            if index <= 3:
                small.send(index)
            run_slot(late + index)
        for entry in sums:
            entry.finish()
        last_sum.finish()


def rows_spec(width, back=False):
    if back:
        return pl.BlockSpec((TILE, width), lambda i: (TILES - 1 - i, 0))
    return pl.BlockSpec((TILE, width), lambda i: (i, 0))


def probs_spec(back=False):
    shape = (SPANS_TILE * PAIRS, 2 * SPAN, 2 * SPAN)
    if back:
        return pl.BlockSpec(shape, lambda i: (TILES - 1 - i, 0, 0))
    return pl.BlockSpec(shape, lambda i: (i, 0, 0))


def whole_spec(shape):
    rank = len(shape)
    return pl.BlockSpec(shape, lambda i: (0,) * rank, pipeline_mode=pl.Buffered(1))


def shaped(shape, dtype=bf16):
    return jax.ShapeDtypeStruct(shape, dtype)


smem_spec = pl.BlockSpec(memory_space=pltpu.SMEM)
limits = pltpu.CompilerParams(vmem_limit_bytes=60 * 1024 * 1024)


def span_table():
    ids = np.arange(ROWS)
    inverse = 1.0 / np.maximum(ids, 1)
    shift = np.where(ids >= 1, np.log(np.maximum(ids, 1)), masked_score)
    return jnp.asarray(np.stack([inverse, shift]).astype(np.float32))


def causal_bias():
    key = np.arange(SPAN)[:, None]
    query = np.arange(2 * SPAN)[None, :] % SPAN
    return jnp.asarray(np.where(key <= query, 0.0, masked_score).astype(np.float32))


def layer_local(x_own, x_other, dy_own, dy_other, lengths, ln_params, weights):
    qkv_own, qkv_other, out_own, out_other, up_own, up_other, down_own, down_other = weights
    table = span_table()
    qkv, bars, probs, ctx = pl.pallas_call(
        forward_attention,
        grid=(TILES,),
        in_specs=[
            smem_spec,
            rows_spec(HALF),
            rows_spec(HALF),
            whole_spec((4, D)),
            whole_spec((3, D, HALF)),
            whole_spec((3, D, HALF)),
            whole_spec((SPAN, 2 * SPAN)),
        ],
        out_specs=[rows_spec(3 * D), rows_spec(2 * D), probs_spec(), rows_spec(D)],
        out_shape=[
            shaped((SEQ, 3 * D)),
            shaped((SEQ, 2 * D)),
            shaped((ROWS * PAIRS, 2 * SPAN, 2 * SPAN)),
            shaped((SEQ, D)),
        ],
        scratch_shapes=[pltpu.VMEM((SPAN, 2 * D), f32), pltpu.VMEM((TILE, D), bf16)],
        compiler_params=limits,
        name="forward_attention",
    )(table, x_own, x_other, ln_params, qkv_own, qkv_other, causal_bias())
    y_own, y_other, grad_res, grad_ctx, g_out, g_up, g_down, g_ln_two = pl.pallas_call(
        mlp_both_ways,
        grid=(TILES,),
        in_specs=[
            smem_spec,
            rows_spec(HALF),
            rows_spec(HALF),
            rows_spec(HALF),
            rows_spec(HALF),
            whole_spec((4, D)),
            rows_spec(D),
            whole_spec((HALF, D)),
            whole_spec((HALF, D)),
            whole_spec((D, FF // 2)),
            whole_spec((D, FF // 2)),
            whole_spec((FF // 2, D)),
            whole_spec((FF // 2, D)),
        ],
        out_specs=[
            rows_spec(HALF),
            rows_spec(HALF),
            rows_spec(D),
            rows_spec(D),
            whole_spec((2, 2, HALF, HALF)),
            whole_spec((2, 2, 1024, HALF)),
            whole_spec((2, 2, 1024, HALF)),
            whole_spec((2, D)),
        ],
        out_shape=[
            shaped((SEQ, HALF)),
            shaped((SEQ, HALF)),
            shaped((SEQ, D), f32),
            shaped((SEQ, D)),
            shaped((2, 2, HALF, HALF)),
            shaped((2, 2, 1024, HALF)),
            shaped((2, 2, 1024, HALF)),
            shaped((2, D), f32),
        ],
        scratch_shapes=[
            pltpu.VMEM((D, D), f32),
            pltpu.VMEM((D, FF), f32),
            pltpu.VMEM((FF, D), f32),
            pltpu.VMEM((2, D), f32),
            pltpu.VMEM((TILE, D), f32),
            pltpu.VMEM((TILE, D), f32),
            pltpu.VMEM((TILE, 1), f32),
            pltpu.VMEM((TILE, D), bf16),
            pltpu.VMEM((TILE, D), bf16),
            pltpu.VMEM((TILE, D), f32),
            pltpu.VMEM((TILE, D), f32),
            pltpu.VMEM((2, TILE, 512), f32),
            pltpu.VMEM((8, 128), f32),
            pltpu.VMEM((2, TILE, 512), bf16),
            pltpu.VMEM((2, TILE, 512), f32),
            pltpu.VMEM((2, TILE, 512), bf16),
            pltpu.VMEM((TILE, D), bf16),
        ],
        compiler_params=limits,
        name="mlp_both_ways",
    )(
        lengths,
        x_own,
        x_other,
        dy_own,
        dy_other,
        ln_params,
        ctx,
        out_own,
        out_other,
        up_own,
        up_other,
        down_own,
        down_other,
    )
    count = lax.axis_size("dp")
    summing = whole_slices(count)
    sum_buffers, extra, total_specs, total_shapes = [], {}, [], []
    if summing:
        for rows in PIECE_ROWS + (3 * HALF,):
            sum_buffers += sum_scratch(rows, count)
            total_specs.append(pl.BlockSpec(memory_space=pl.ANY))
            total_shapes.append(shaped((2, rows, HALF)))
        sum_buffers += ln_scratch(count)
        extra = dict(collective_id=0, has_side_effects=True)
    else:
        total_specs.append(whole_spec((2, 2, 3 * HALF, HALF)))
        total_shapes.append(shaped((2, 2, 3 * HALF, HALF)))
    gx_own, gx_other, *totals = pl.pallas_call(
        functools.partial(backward_attention, count),
        grid=(TILES,),
        in_specs=[
            smem_spec,
            rows_spec(HALF, True),
            rows_spec(HALF, True),
            whole_spec((4, D)),
            whole_spec((3, D, HALF)),
            whole_spec((3, D, HALF)),
            rows_spec(3 * D, True),
            rows_spec(2 * D, True),
            probs_spec(True),
            rows_spec(D, True),
            rows_spec(D, True),
            whole_spec((2, 2, 1024, HALF)),
            whole_spec((2, 2, 1024, HALF)),
            whole_spec((2, 2, HALF, HALF)),
            whole_spec((2, D)),
        ],
        out_specs=[rows_spec(HALF, True), rows_spec(HALF, True)]
        + total_specs
        + [whole_spec((4, D))],
        out_shape=[shaped((SEQ, HALF)), shaped((SEQ, HALF))]
        + total_shapes
        + [shaped((4, D), f32)],
        scratch_shapes=[
            pltpu.VMEM((2, 3, D, HALF), f32),
            pltpu.VMEM((2, D), f32),
            pltpu.VMEM((SPAN, 2 * D), f32),
            pltpu.VMEM((TILE, 3 * D), bf16),
            pltpu.VMEM((TILE, D), bf16),
            pltpu.VMEM((TILE, D), f32),
            pltpu.VMEM((2, 2, 3 * HALF, HALF), bf16),
            pltpu.VMEM((4, D), f32),
        ]
        + sum_buffers,
        compiler_params=pltpu.CompilerParams(vmem_limit_bytes=60 * 1024 * 1024, **extra),
        name="backward_attention",
    )(
        table,
        x_own,
        x_other,
        ln_params,
        qkv_own,
        qkv_other,
        qkv,
        bars,
        probs,
        grad_ctx,
        grad_res,
        g_down,
        g_up,
        g_out,
        g_ln_two,
    )
    if not summing:
        g_qkv, g_ln = totals
        grads = (g_down, g_up, g_out, g_qkv)
        chips = [grad[0].astype(f32) + swap_heads(grad[1]).astype(f32) for grad in grads]
        down, up, out, three = [lax.psum(chip.astype(bf16), "dp") for chip in chips]
        ln_total = lax.psum(g_ln, ("dp", "head"))
        totals = (down[:, :D], down[:, D:], up[:, :D], up[:, D:], out, three, ln_total)
    return (y_own, y_other), (gx_own, gx_other), totals


RATES = (
    float(D) ** (-0.5),
    4.0 * float(D) ** (-0.5),
    float(D) ** (-0.5),
    float(FF) ** (-0.5),
    0.7,
)


def adam_step(gradient, weight, moment_one, moment_two, step_rate):
    first_new = beta_one * moment_one + (1.0 - beta_one) * gradient
    second_new = beta_two * moment_two + (1.0 - beta_two) * gradient * gradient
    first_hat = first_new * (1.0 / (1.0 - beta_one**STEP))
    second_hat = second_new * (1.0 / (1.0 - beta_two**STEP))
    weight_new = weight - step_rate * (
        first_hat / (jnp.sqrt(second_hat) + epsilon_adam) + decay_rate * weight
    )
    return (weight_new, first_new, second_new)


def kind_gradient(kind, refs, step):
    if kind == 0:
        ref = refs[0]
        return jnp.concatenate([ref[0, 0], ref[1, 0]], axis=0).astype(f32)[None]
    sides = [jnp.concatenate([ref[0], ref[1]], axis=1) for ref in refs]
    if kind == 2:
        return jnp.concatenate(sides, axis=1).astype(f32)
    if kind == 3:
        return jnp.where(step < 2, sides[0].astype(f32), sides[1].astype(f32))
    return sides[0].astype(f32)


BLOCKS = (
    (3, (1, D, HALF), (2, 1, HALF, HALF)),
    (1, (HALF, D), (2, HALF, HALF)),
    (4, (128, 1024), (2, 128, HALF)),
    (4, (HALF, D), (2, HALF, HALF)),
)
GRADS = (1, 1, 2, 2)


def adam_kernel(kinds, owners, *refs):
    step = pl.program_id(0)
    chip = lax.axis_index("dp")
    ins = sum(GRADS[kind] + 3 for kind in kinds)
    inputs, outputs = list(refs[:ins]), list(refs[ins:])
    first = 0
    for kind in kinds:
        grads = [inputs.pop(0) for _ in range(GRADS[kind])]
        weight, one, two = [inputs.pop(0) for _ in range(3)]
        owned, new, first_new, second_new, copy = [outputs.pop(0) for _ in range(5)]
        steps = BLOCKS[kind][0]

        @pl.when((step >= first) & (step < first + steps))
        def _(kind=kind, grads=grads, weight=weight, one=one, two=two, owned=owned, new=new,
              first_new=first_new, second_new=second_new, copy=copy, first=first):
            gradient = kind_gradient(kind, grads, step - first)
            results = adam_step(gradient, weight[...], one[...], two[...], RATES[kind])
            owned[...] = jnp.where(owners[kind] == chip, gradient, 0.0)
            new[...] = results[0]
            first_new[...] = results[1]
            second_new[...] = results[2]
            copy[...] = results[0].astype(bf16)

        first += steps


def adam_update(kinds, owners, grads, weights, ones, twos):
    in_specs, out_specs, out_shape, operands = [smem_spec], [], [], [owners]
    first = 0
    for index, kind in enumerate(kinds):
        steps, block, grad_block = BLOCKS[kind]

        def place(i, first=first, steps=steps):
            return jnp.clip(i - first, 0, steps - 1)

        def at(i, place=place, rank=len(block)):
            return (place(i),) + (0,) * (rank - 1)

        for piece in range(GRADS[kind]):

            def grad_at(i, place=place, kind=kind, piece=piece):
                if kind == 0:
                    return (0, place(i), 0, 0)
                if kind == 3:
                    return (0, jnp.clip(place(i) - 2 * piece, 0, 1), 0)
                return (0, place(i), 0)

            in_specs.append(pl.BlockSpec(grad_block, grad_at))
        spec = pl.BlockSpec(block, at)
        in_specs += [spec] * 3
        out_specs += [spec] * 5
        whole = weights[index].shape
        out_shape += [shaped(whole, f32)] * 4 + [shaped(whole)]
        operands += [*grads[index], weights[index], ones[index], twos[index]]
        first += steps
    results = pl.pallas_call(
        functools.partial(adam_kernel, kinds),
        grid=(first,),
        in_specs=in_specs,
        out_specs=out_specs,
        out_shape=out_shape,
        compiler_params=limits,
        name="adam_update",
    )(*operands)
    return [results[index * 5 : index * 5 + 5] for index in range(len(kinds))]


def gather_inputs(tokens, cotangent, w_qkv, w_out, w_up, w_down):
    head = lax.axis_index("head")

    def both(array):
        halves = array.reshape(2, SEQ, HALF)
        own = lax.dynamic_index_in_dim(halves, head, 0, keepdims=False)
        other = lax.dynamic_index_in_dim(halves, 1 - head, 0, keepdims=False)
        return own, swap_heads(other)

    x_own, x_other = both(tokens)
    qkv_own = w_qkv.transpose(1, 0, 2).astype(bf16)
    out_own = w_out.astype(bf16)
    up_own = w_up.astype(bf16)
    down_own = w_down.astype(bf16)
    qkv_other = swap_heads(qkv_own)
    dy_own, dy_other = both(cotangent)
    weights = (
        qkv_own,
        qkv_other,
        out_own,
        swap_heads(out_own),
        up_own,
        swap_heads(up_own),
        down_own,
        swap_heads(down_own),
    )
    return x_own, x_other, dy_own, dy_other, weights


def place_rows(pieces):
    head = lax.axis_index("head")
    own, away = pieces
    arrived = swap_heads(away)
    return jnp.concatenate(
        [jnp.where(head == 0, own, arrived), jnp.where(head == 0, arrived, own)], axis=0
    )


def body(
    tokens,
    cotangent,
    lengths,
    owners,
    w_qkv,
    w_out,
    w_up,
    w_down,
    ln_params,
    m_qkv,
    m_out,
    m_up,
    m_down,
    m_ln,
    v_qkv,
    v_out,
    v_up,
    v_down,
    v_ln,
):
    x_own, x_other, dy_own, dy_other, weights = gather_inputs(
        tokens, cotangent, w_qkv, w_out, w_up, w_down
    )
    y, gx, totals = layer_local(
        x_own, x_other, dy_own, dy_other, lengths, ln_params, weights
    )
    output_rows = place_rows(y)
    grad_input = place_rows(gx)
    *pieces, t_ln = totals

    def as_blocks(array):
        return array.transpose(1, 0, 2)

    results = adam_update(
        (0, 1, 2, 3),
        owners,
        (
            (pieces[5].reshape(2, 3, HALF, HALF),),
            (pieces[4],),
            (pieces[2], pieces[3]),
            (pieces[0], pieces[1]),
        ),
        (as_blocks(w_qkv), w_out, w_up, w_down),
        (as_blocks(m_qkv), m_out, m_up, m_down),
        (as_blocks(v_qkv), v_out, v_up, v_down),
    )
    results[0] = [as_blocks(array) for array in results[0]]
    mine = owners[4] == lax.axis_index("dp")
    ln_results = adam_step(t_ln, ln_params, m_ln, v_ln, RATES[4])
    results.append([jnp.where(mine, t_ln, 0.0), *ln_results])
    owned, new, first, second = [
        tuple(results[kind][slot] for kind in range(5)) for slot in range(4)
    ]
    copies = tuple(results[kind][4] for kind in range(4))
    owned = tuple(array[None] for array in owned)
    return (output_rows, grad_input) + owned + new + first + second + copies


PLACED = (
    (P("dp", "head"),) * 2
    + (P("dp"), P())
    + (P(None, None, "head"), P("head", None), P(None, "head"), P("head", None), P()) * 3
)
RESULTS = (
    (P("dp", "head"),) * 2
    + (
        P("dp", None, None, "head"),
        P("dp", "head", None),
        P("dp", None, "head"),
        P("dp", "head", None),
        P("dp", None, None),
    )
    + (P(None, None, "head"), P("head", None), P(None, "head"), P("head", None), P()) * 3
    + (P(None, None, "head"), P("head", None), P(None, "head"), P("head", None))
)


def solution(mesh):
    return jax.shard_map(
        body, mesh=mesh, in_specs=PLACED, out_specs=RESULTS, check_vma=False
    )
```

```python
import functools

import jax
import jax.numpy as jnp
import numpy as np
from jax import lax
from jax.experimental import pallas as pl
from jax.experimental.pallas import tpu as pltpu
from jax.sharding import PartitionSpec as P

D = 512
HALF = 256
HEAD_DIM = 64
FF = 2048
SPAN = 128
SEQ = 2048
STEP = 5
ROWS = 16
PAIRS = 4
TILE = 512
TILES = SEQ // TILE
SPANS_TILE = TILE // SPAN

epsilon_norm = 1e-05
epsilon_adam = 1e-08
beta_one = 0.5
beta_two = 0.5
decay_rate = 0.1
masked_score = -1e30

bf16 = jnp.bfloat16
f32 = jnp.float32

NN = (((1,), (0,)), ((), ()))
NT = (((1,), (1,)), ((), ()))
TN = (((0,), (0,)), ((), ()))


def mm(left, right, dims=NN):
    return lax.dot_general(left, right, dims, preferred_element_type=f32)


def join_columns(head, own, other):
    low = jnp.where(head == 0, own, other)
    high = jnp.where(head == 0, other, own)
    return jnp.concatenate([low, high], axis=1)


def norm_stats(values):
    mean = jnp.mean(values, axis=1, keepdims=True)
    centered = values - mean
    rstd = lax.rsqrt(jnp.mean(centered * centered, axis=1, keepdims=True) + epsilon_norm)
    return centered * rstd, rstd


def head_stack(pair, low_lanes, high_lanes):
    return jnp.concatenate([pair * low_lanes, pair * high_lanes], axis=0)


def lane_masks(dtype):
    lane = lax.broadcasted_iota(jnp.int32, (1, 2 * HEAD_DIM), 1)
    low = (lane < HEAD_DIM).astype(f32)
    return low.astype(dtype), (1.0 - low).astype(dtype)


def pair_columns(pair):
    base = 3 * HALF * (pair // 2) + 2 * HEAD_DIM * (pair % 2)
    return base, base + HALF, base + 2 * HALF


def unstack_transposed(product):
    joined = jnp.concatenate(
        [product[:HEAD_DIM, :SPAN], product[HEAD_DIM:, SPAN:]], axis=0
    )
    return joined.T


def forward_attention(
    table, x_own, x_other, ln, w_own, w_other, causal, qkv, bars, probs, ctx, run_sum, normed
):
    head = lax.axis_index("head")
    step = pl.program_id(0)

    @pl.when(step == 0)
    def _():
        run_sum[...] = jnp.zeros_like(run_sum)

    for row in range(0, TILE, 128):
        rows = pl.ds(row, 128)
        x = join_columns(head, x_own[rows, :].astype(f32), x_other[rows, :].astype(f32))
        xhat, _ = norm_stats(x)
        normed[rows, :] = (xhat * ln[0:1, :] + ln[1:2, :]).astype(bf16)
    for side, w in enumerate((w_own, w_other)):
        for part in range(3):
            value = mm(normed[...], w[part])
            if part == 0:
                value = value * float(HEAD_DIM) ** (-0.5)
            base = side * 3 * HALF + part * HALF
            qkv[:, base : base + HALF] = value.astype(bf16)
    low_lanes, high_lanes = lane_masks(bf16)

    def score_span(span):
        rows = pl.ds(span * SPAN, SPAN)
        row_id = step * SPANS_TILE + span
        inverse = table[0, row_id]
        shift = table[1, row_id]
        scores, stacked = [], []
        for pair in range(PAIRS):
            at_q, at_k, at_v = pair_columns(pair)
            lanes = pl.ds(pair * 128, 128)
            lanes_v = pl.ds(512 + pair * 128, 128)
            key = qkv[rows, at_k : at_k + 128]
            value = qkv[rows, at_v : at_v + 128]
            key_bar = (run_sum[:, lanes] * inverse).astype(bf16)
            value_bar = (run_sum[:, lanes_v] * inverse).astype(bf16)
            run_sum[:, lanes] += key.astype(f32)
            run_sum[:, lanes_v] += value.astype(f32)
            bars[rows, lanes] = key_bar
            bars[rows, lanes_v] = value_bar
            query = head_stack(qkv[rows, at_q : at_q + 128], low_lanes, high_lanes)
            scores.append((mm(key, query, NT) + causal[...], mm(key_bar, query, NT) + shift))
            stacked.append(jnp.concatenate([value, value_bar], axis=0))
        return scores, stacked

    def soft_span(span, scores):
        expo = []
        for direct, summary in scores:
            top = jnp.maximum(
                jnp.max(direct, axis=0, keepdims=True), jnp.max(summary, axis=0, keepdims=True)
            )
            expo.append((jnp.exp(direct - top), jnp.exp(summary - top)))
        both = []
        for pair, (direct, summary) in enumerate(expo):
            total = jnp.sum(direct, axis=0, keepdims=True) + jnp.sum(
                summary, axis=0, keepdims=True
            )
            scale = 1.0 / total
            prob = jnp.concatenate(
                [(direct * scale).astype(bf16), (summary * scale).astype(bf16)], axis=0
            )
            probs[span * PAIRS + pair] = prob
            both.append(prob)
        return both

    def context_span(span, stacked, both):
        rows = pl.ds(span * SPAN, SPAN)
        for pair in range(PAIRS):
            lanes = pl.ds(pair * 128, 128)
            ctx[rows, lanes] = unstack_transposed(mm(stacked[pair], both[pair], TN)).astype(bf16)

    ready = score_span(0)
    for span in range(SPANS_TILE):
        scores, stacked = ready
        if span + 1 < SPANS_TILE:
            ready = score_span(span + 1)
        both = soft_span(span, scores)
        context_span(span, stacked, both)


def gelu_parts(u):
    share = lax.erf(u * 0.7071067811865476) * 0.5 + 0.5
    bell = jnp.exp2((u * u) * -0.7213475204444817)
    return u * share, share + u * bell * 0.3989422804014327


def swap_heads(value):
    return lax.ppermute(value, "head", [(0, 1), (1, 0)])


def chip_grid(count):
    side = 1 << ((count.bit_length() - 1) // 3)
    return (count // (side * side), side, side)


class Lines:
    def __init__(self, count):
        self.sizes = chip_grid(count)
        self.strides = (self.sizes[1] * self.sizes[2], self.sizes[2], 1)
        self.chip = lax.axis_index("dp")
        self.head = lax.axis_index("head")
        self.places = [
            lax.rem(self.chip // stride, size) for stride, size in zip(self.strides, self.sizes)
        ]
        self.members = [
            [self.find(axis, ahead) for ahead in range(1, size)]
            for axis, size in enumerate(self.sizes)
        ]

    def partner(self):
        return (self.chip, 1 - self.head)

    def member(self, axis, ahead):
        return self.members[axis][ahead - 1]

    def find(self, axis, ahead):
        size = self.sizes[axis]
        place = 1 - self.places[axis]
        if size > 2:
            place = lax.rem(self.places[axis] + ahead, size)
        chip = self.chip + (place - self.places[axis]) * self.strides[axis]
        return place, (chip, self.head)

    def greet(self):
        barrier = pltpu.get_barrier_semaphore()
        others = [self.partner()]
        for axis in range(3):
            others += [self.member(axis, ahead)[1] for ahead in range(1, self.sizes[axis])]
        for other in others:
            pl.semaphore_signal(
                barrier, inc=1, device_id=other, device_id_type=pl.DeviceIdType.MESH
            )
        pl.semaphore_wait(barrier, len(others))


X_FIRST, Y_FIRST = (2, 1, 0), (1, 2, 0)


def whole_slices(count):
    return all(shape[1] % (16 * count) == 0 for shape, _ in PIECES)


def chunk_rows(rows):
    return next(chunk for chunk in (128, 96, 64, 48, 32, 16) if rows % chunk == 0)


def sum_scratch(shape, orders, count):
    parts, rows, lanes = shape
    sizes = chip_grid(count)
    shapes = [pltpu.VMEM(shape, bf16)]
    sems = [pltpu.SemaphoreType.DMA((3,))]
    for order in orders:
        left = rows
        for axis in order:
            left //= sizes[axis]
            shapes.append(pltpu.VMEM((sizes[axis] - 1, left, lanes), bf16))
            sems.append(pltpu.SemaphoreType.DMA((2, 2, sizes[axis] - 1)))
    return shapes + sems


class DpSum:
    def __init__(self, lines, orders, grads, total, scratch):
        self.lines = lines
        self.orders = orders
        self.parts = range(len(orders))
        self.grads = grads
        self.total = total
        self.rows = grads.shape[2]
        self.work, self.final = grads.at[0], scratch.pop(0)
        self.slots = [[scratch.pop(0) for _ in order] for order in orders]
        self.core_sem = scratch.pop(0)
        self.sems = [[scratch.pop(0) for _ in order] for order in orders]
        self.base = []
        for order in orders:
            bases, piece = [0], self.rows
            for axis in order:
                piece //= lines.sizes[axis]
                bases.append(bases[-1] + lines.places[axis] * piece)
            self.base.append(bases)

    def remote(self, source, target, send_sem, recv_sem, device):
        return pltpu.make_async_remote_copy(
            src_ref=source,
            dst_ref=target,
            send_sem=send_sem,
            recv_sem=recv_sem,
            device_id=device,
            device_id_type=pl.DeviceIdType.MESH,
        )

    def core_copy(self):
        return self.remote(
            self.grads.at[1],
            self.final,
            self.core_sem.at[0],
            self.core_sem.at[1],
            self.lines.partner(),
        )

    def core_send(self):
        self.core_copy().start()

    def core_sum(self):
        self.core_copy().wait()
        chunk = chunk_rows(self.rows)
        for part in self.parts:

            def add(index, carry, part=part):
                rows = pl.ds(pl.multiple_of(index * chunk, chunk), chunk)
                self.work[part, rows, :] = self.work[part, rows, :] + self.final[part, rows, :]
                return carry

            lax.fori_loop(0, self.rows // chunk, add, 0)

    def spread_copies(self, part, stage):
        axis = self.orders[part][stage]
        size = self.lines.sizes[axis]
        base = self.base[part][stage]
        piece = self.rows
        for at in self.orders[part][: stage + 1]:
            piece //= self.lines.sizes[at]
        copies = []
        for ahead in range(1, size):
            place, device = self.lines.member(axis, ahead)
            start = pl.multiple_of(base + place * piece, 16)
            copies.append(
                self.remote(
                    self.work.at[part, pl.ds(start, piece)],
                    self.slots[part][stage].at[ahead - 1],
                    self.sems[part][stage].at[0, 0, ahead - 1],
                    self.sems[part][stage].at[0, 1, ahead - 1],
                    device,
                )
            )
        return copies, self.base[part][stage + 1], piece

    def spread_send(self, part, stage):
        for copy in self.spread_copies(part, stage)[0]:
            copy.start()

    def spread_sum(self, part, stage):
        copies, mine, piece = self.spread_copies(part, stage)
        for copy in copies:
            copy.wait()
        slots = self.slots[part][stage]
        target = self.final if stage == 2 else self.work
        chunk = chunk_rows(piece)

        def add(index, carry):
            offset = pl.multiple_of(index * chunk, chunk)
            rows = pl.ds(pl.multiple_of(mine + offset, 16), chunk)
            value = self.work[part, rows, :]
            if len(copies) > 1:
                value = value.astype(f32)
            for slot in range(len(copies)):
                value = value + slots[slot, pl.ds(offset, chunk), :].astype(value.dtype)
            target[part, rows, :] = value.astype(bf16)
            return carry

        lax.fori_loop(0, piece // chunk, add, 0)

    def gather_copies(self, part, stage):
        axis = self.orders[part][stage]
        size = self.lines.sizes[axis]
        piece = self.rows
        for at in self.orders[part][: stage + 1]:
            piece //= self.lines.sizes[at]
        mine = pl.multiple_of(self.base[part][stage + 1], 16)
        rows = pl.ds(mine, piece)
        copies = []
        for ahead in range(1, size):
            _, device = self.lines.member(axis, ahead)
            copies.append(
                self.remote(
                    self.final.at[part, rows],
                    self.final.at[part, rows],
                    self.sems[part][stage].at[1, 0, ahead - 1],
                    self.sems[part][stage].at[1, 1, ahead - 1],
                    device,
                )
            )
        return copies

    def gather_send(self, part, stage):
        for copy in self.gather_copies(part, stage):
            copy.start()

    def gather_wait(self, part, stage):
        for copy in self.gather_copies(part, stage):
            copy.wait()

    def store_copy(self):
        return pltpu.make_async_copy(self.final, self.total, self.core_sem.at[2])

    def event(self, index):
        if index == 0:
            self.core_send()
        elif index == 1:
            self.core_sum()
        for part in self.parts:
            if 2 <= index <= 4:
                self.spread_sum(part, index - 2)
            elif index >= 5:
                self.gather_wait(part, 7 - index)
            if 1 <= index <= 3:
                self.spread_send(part, index - 1)
            elif 4 <= index <= 6:
                self.gather_send(part, 6 - index)
        if index == 7:
            self.store_copy().start()

    def finish(self):
        self.store_copy().wait()


EVENTS = 8


def ln_scratch(count):
    return [
        pltpu.VMEM((2, 4, D), f32),
        pltpu.SemaphoreType.DMA((2,)),
        *[pltpu.VMEM((size, 4, D), f32) for size in chip_grid(count)],
        *[pltpu.SemaphoreType.DMA((2, max(size - 1, 1))) for size in chip_grid(count)],
    ]


class LnSum:
    def __init__(self, lines, value, total, scratch):
        self.lines = lines
        self.value = value
        self.total = total
        self.core, self.core_sem = scratch[:2]
        self.slots = scratch[2:5]
        self.sems = scratch[5:8]

    def stage_copies(self, stage):
        lines = self.lines
        if stage == 0:
            mine = self.core.at[lines.head]
            return [
                pltpu.make_async_remote_copy(
                    src_ref=mine,
                    dst_ref=mine,
                    send_sem=self.core_sem.at[0],
                    recv_sem=self.core_sem.at[1],
                    device_id=lines.partner(),
                    device_id_type=pl.DeviceIdType.MESH,
                )
            ]
        axis = stage - 1
        mine = self.slots[axis].at[lines.places[axis]]
        return [
            pltpu.make_async_remote_copy(
                src_ref=mine,
                dst_ref=mine,
                send_sem=self.sems[axis].at[0, ahead - 1],
                recv_sem=self.sems[axis].at[1, ahead - 1],
                device_id=lines.member(axis, ahead)[1],
                device_id_type=pl.DeviceIdType.MESH,
            )
            for ahead in range(1, lines.sizes[axis])
        ]

    def send(self, stage):
        if stage == 0:
            self.core[self.lines.head] = self.value[...]
        for copy in self.stage_copies(stage):
            copy.start()

    def finish(self, stage):
        for copy in self.stage_copies(stage):
            copy.wait()
        slots = self.core if stage == 0 else self.slots[stage - 1]
        value = slots[0]
        for slot in range(1, slots.shape[0]):
            value = value + slots[slot]
        if stage == 3:
            self.total[...] = value
        else:
            self.slots[stage][self.lines.places[stage]] = value


PIECES = (
    ((2, 1024, HALF), (X_FIRST, Y_FIRST)),
    ((2, 1024, HALF), (X_FIRST, Y_FIRST)),
    ((1, HALF, D), (Y_FIRST,)),
    ((2, 3 * HALF, HALF), (X_FIRST, Y_FIRST)),
)
CHUNKS = FF // 512
CHUNK_STEP = TILES
POST_STEP = CHUNK_STEP + CHUNKS
ATT_STEP = POST_STEP + TILES
SPANS_STEP = 2
ATT_STEPS = ROWS // SPANS_STEP
LAST_STEP = ATT_STEP + ATT_STEPS
STEPS = LAST_STEP + TILES
EVENT_AT = (
    ((6, 0), (6, 1), (7, 1), (8, 0), (12, 0), (14, 0), (16, 0), (18, 0)),
    ((8, 0), (9, 0), (13, 0), (15, 0), (17, 0), (19, 0), (21, 0), (23, 0)),
    ((12, 0), (13, 0), (15, 0), (16, 0), (18, 0), (20, 0), (21, 0), (23, 0)),
    ((20, 0), (21, 0), (23, 0)),
)


def mlp_and_back(
    count,
    table,
    lengths,
    ln,
    x_own_at,
    x_other_at,
    dy_own_at,
    dy_other_at,
    ctx_at,
    qkv_at,
    bars_at,
    probs_at,
    out_own_at,
    out_other_at,
    w_own_at,
    w_other_at,
    up_own,
    up_other,
    down_own,
    down_other,
    y_own_at,
    y_other_at,
    gx_own_at,
    gx_other_at,
    *refs,
):
    summing = whole_slices(count)
    kinds = len(PIECES)
    totals, ln_total = refs[:kinds], refs[kinds]
    (x_own, x_other, dy_own, dy_other, ctx, qkv_two, bars_two, probs_two, out_own, out_other,
     w_own, w_other, up_all, down_all, load_sem, weight_sem, block_sem, store_sem, res, grad_qkv,
     normed_t, gm, mlp, grad_n, acc_one, acc_two, hid, grad_hid, after,
     acc_ln) = refs[kinds + 1 : kinds + 31]
    grads = refs[kinds + 31 : kinds + 31 + len(PIECES)]
    scratch = list(refs[kinds + 31 + len(PIECES) :])
    head = lax.axis_index("head")
    used = lengths[head]
    sums = []
    if summing:
        lines = Lines(count)
        for (_, orders), grad, total in zip(PIECES, grads, totals):
            sums.append(DpSum(lines, orders, grad, total, scratch))
        small = LnSum(lines, acc_ln, ln_total, scratch)

    def run_events(events):
        for index, event in events:
            sums[index].event(event)

    def hook(step, first, end, place=0):
        for at in range(first, end if summing else 0):
            events = [
                (index, event)
                for index, times in enumerate(EVENT_AT)
                for event, time in enumerate(times)
                if time == (at, place)
            ]
            if events:

                @pl.when(step == at)
                def _(events=events):
                    run_events(events)

    loads = [
        pltpu.make_async_copy(source, target, load_sem.at[index])
        for index, (source, target) in enumerate(
            (
                (ctx_at, ctx),
                (out_own_at, out_own),
                (out_other_at, out_other),
                (x_own_at, x_own),
                (x_other_at, x_other),
                (dy_own_at, dy_own),
                (dy_other_at, dy_other),
                (w_own_at, w_own),
                (w_other_at, w_other),
            )
        )
    ]
    weight_copies = []
    for chunk in range(CHUNKS):
        up_w, down_w = ((up_own, down_own), (up_other, down_other))[chunk % 2]
        cut = pl.ds(chunk // 2 * 512, 512)
        pairs = ((up_w.at[:, cut], up_all.at[chunk]), (down_w.at[cut], down_all.at[chunk]))
        for which, (source, target) in enumerate(pairs):
            sem = weight_sem.at[2 * chunk + which]
            weight_copies.append(pltpu.make_async_copy(source, target, sem))
    block_rows = SPANS_STEP * SPAN
    block_probs = SPANS_STEP * PAIRS

    def block_copies(index):
        block = ATT_STEPS - 1 - index
        slot = lax.rem(index, 2)
        rows = pl.ds(block * block_rows, block_rows)
        many = pl.ds(block * block_probs, block_probs)
        pairs = (
            (qkv_at.at[rows], qkv_two.at[slot]),
            (bars_at.at[rows], bars_two.at[slot]),
            (probs_at.at[many], probs_two.at[slot]),
        )
        return [
            pltpu.make_async_copy(source, target, block_sem.at[slot, which])
            for which, (source, target) in enumerate(pairs)
        ]

    stores = [
        pltpu.make_async_copy(source, target, store_sem.at[index])
        for index, (source, target) in enumerate(
            (
                (ctx.at[:, pl.ds(0, HALF)], y_own_at),
                (ctx.at[:, pl.ds(HALF, HALF)], y_other_at),
                (dy_own, gx_own_at),
                (dy_other, gx_other_at),
            )
        )
    ]

    def x_rows(rows):
        return join_columns(head, x_own[rows, :].astype(f32), x_other[rows, :].astype(f32))

    def dy_rows(rows):
        return join_columns(head, dy_own[rows, :].astype(f32), dy_other[rows, :].astype(f32))

    def valid_rows(first):
        ids = lax.broadcasted_iota(jnp.int32, (128, 1), 0) + first
        return (ids < used).astype(f32)

    def before_mlp(tile, carry):
        base = tile * TILE
        tokens = pl.ds(pl.multiple_of(base, TILE), TILE)
        res[tokens, :] = mm(ctx[tokens, :HALF], out_own[...]) + mm(
            ctx[tokens, HALF:], out_other[...]
        )
        mlp[tokens, :] = jnp.zeros((TILE, D), f32)
        grad_n[tokens, :] = jnp.zeros((TILE, D), f32)
        for row in range(0, TILE, 128):
            at = pl.ds(pl.multiple_of(base + row, 128), 128)
            valid = valid_rows(base + row)
            h = x_rows(at) + valid * res[at, :]
            res[at, :] = h
            hat, _ = norm_stats(h)
            n2 = (hat * ln[2:3, :] + ln[3:4, :]).astype(bf16)
            grad_qkv[at, :D] = n2
            normed_t[:, at] = n2.T
            gm[at, :] = (valid * dy_rows(at)).astype(bf16)
        return carry

    def chunk_in(chunk, tile):
        tokens = pl.ds(tile * TILE, TILE)
        hid[tile % 2] = mm(grad_qkv[tokens, :D], up_all[chunk])
        grad_hid[tile % 2] = mm(gm[tokens, :], down_all[chunk], NT)

    def act_rows(tile, row, size):
        return pl.ds(tile % 2 * TILE + row, size), pl.ds((2 + tile % 2) * TILE + row, size)

    def chunk_mid(tile):
        slot = tile % 2
        for row in range(0, TILE, 16):
            rows = pl.ds(row, 16)
            a, da = gelu_parts(hid[slot, rows, :])
            at_act, at_gu = act_rows(tile, row, 16)
            grad_qkv[at_act, D : 2 * D] = a.astype(bf16)
            grad_qkv[at_gu, D : 2 * D] = (grad_hid[slot, rows, :] * da).astype(bf16)

    def chunk_out(chunk, tile):
        tokens = pl.ds(tile * TILE, TILE)
        at_act, at_gu = act_rows(tile, 0, TILE)
        act = grad_qkv[at_act, D : 2 * D]
        gu = grad_qkv[at_gu, D : 2 * D]
        mlp[tokens, :] += mm(act, down_all[chunk])
        grad_n[tokens, :] += mm(gu, up_all[chunk], NT)
        part_down = mm(act, gm[tokens, :], TN)
        part_up = mm(normed_t[:, tokens], gu)
        if tile == 0:
            acc_one[...] = part_down
            acc_two[...] = part_up
        else:
            acc_one[...] += part_down
            acc_two[...] += part_up

    def chunk_tiles(chunk, first):
        chunk_in(chunk, first)
        chunk_in(chunk, first + 1)
        chunk_mid(first)
        chunk_out(chunk, first)
        chunk_mid(first + 1)
        chunk_out(chunk, first + 1)

    def hidden_chunk(chunk, carry):
        step = CHUNK_STEP + chunk
        hook(step, CHUNK_STEP, POST_STEP)
        chunk_tiles(chunk, 0)
        hook(step, CHUNK_STEP, POST_STEP, 1)
        chunk_tiles(chunk, 2)
        side = lax.rem(chunk, 2)

        for half in range(2):

            @pl.when(chunk // 2 == half)
            def _(half=half):
                for part in range(2):
                    lanes = slice(part * HALF, (part + 1) * HALF)
                    grads[half][side, part, :512] = acc_one[:, lanes].astype(bf16)
                    grads[half][side, part, 512:] = acc_two[:, lanes].astype(bf16)

        return carry

    def after_mlp(tile, carry):
        hook(POST_STEP + tile, POST_STEP, ATT_STEP)
        base = tile * TILE
        tokens = pl.ds(pl.multiple_of(base, TILE), TILE)
        for row in range(0, TILE, 128):
            at = pl.ds(pl.multiple_of(base + row, 128), 128)
            valid = valid_rows(base + row)
            h = res[at, :]
            mlp[at, :] = h + valid * mlp[at, :]
            gn = grad_n[at, :]
            hat, rstd = norm_stats(h)
            acc_ln[2:3, :] += jnp.sum(gn * hat, axis=0, keepdims=True)
            acc_ln[3:4, :] += jnp.sum(gn, axis=0, keepdims=True)
            scaled = gn * ln[2:3, :]
            back = rstd * (
                scaled
                - jnp.mean(scaled, axis=1, keepdims=True)
                - hat * jnp.mean(scaled * hat, axis=1, keepdims=True)
            )
            gh = dy_rows(at) + back
            res[at, :] = gh
            gm[at, :] = (valid * gh).astype(bf16)
        ga = gm[tokens, :]
        acc_one[...] += mm(ctx[tokens, :], ga, TN)
        low, high = mlp[tokens, :HALF], mlp[tokens, HALF:]
        ctx[tokens, :HALF] = jnp.where(head == 0, low, high).astype(bf16)
        ctx[tokens, HALF:] = jnp.where(head == 0, high, low).astype(bf16)
        grad_low = mm(ga, out_own[...], NT)
        grad_high = mm(ga, out_other[...], NT)
        gm[tokens, :HALF] = grad_low.astype(bf16)
        gm[tokens, HALF:] = grad_high.astype(bf16)
        return carry

    low_lanes, high_lanes = lane_masks(bf16)
    scale_factor = float(HEAD_DIM) ** (-0.5)

    def span_tokens(block, span):
        return pl.ds(pl.multiple_of(block * block_rows + span * SPAN, SPAN), SPAN)

    def attention_in(block, qkv, bars, span):
        rows = pl.ds(span * SPAN, SPAN)
        held = []
        for pair in range(PAIRS):
            _, _, at_v = pair_columns(pair)
            lanes = pl.ds(pair * 128, 128)
            lanes_v = pl.ds(512 + pair * 128, 128)
            values = jnp.concatenate([qkv[rows, at_v : at_v + 128], bars[rows, lanes_v]], axis=0)
            grad = head_stack(gm[span_tokens(block, span), lanes], low_lanes, high_lanes)
            held.append((grad, mm(values, grad, NT)))
        return held

    def attention_mid(probs, span, held):
        scores = []
        for pair in range(PAIRS):
            prob_f = probs[span * PAIRS + pair].astype(f32)
            weighted = held[pair][1] * prob_f
            delta = jnp.sum(weighted, axis=0, keepdims=True)
            scores.append((weighted - prob_f * delta).astype(bf16))
        return scores

    def attention_out(block, qkv, bars, probs, span, held, scores):
        rows = pl.ds(span * SPAN, SPAN)
        tokens = span_tokens(block, span)
        inverse = table[0, block * SPANS_STEP + span]
        for pair in range(PAIRS):
            at_q, at_k, at_v = pair_columns(pair)
            lanes = pl.ds(pair * 128, 128)
            lanes_v = pl.ds(512 + pair * 128, 128)
            keys = jnp.concatenate([qkv[rows, at_k : at_k + 128], bars[rows, lanes]], axis=0)
            query = head_stack(qkv[rows, at_q : at_q + 128], low_lanes, high_lanes)
            grad_q = unstack_transposed(mm(keys, scores[pair], TN)) * scale_factor
            grad_k = mm(scores[pair], query)
            grad_v = mm(probs[span * PAIRS + pair], held[pair][0])
            grad_qkv[tokens, at_q : at_q + 128] = grad_q.astype(bf16)
            grad_qkv[tokens, at_k : at_k + 128] = (grad_k[:SPAN] + after[:, lanes]).astype(bf16)
            grad_qkv[tokens, at_v : at_v + 128] = (grad_v[:SPAN] + after[:, lanes_v]).astype(bf16)
            after[:, lanes] += grad_k[SPAN:] * inverse
            after[:, lanes_v] += grad_v[SPAN:] * inverse

    def attention_block(index, carry):
        block = ATT_STEPS - 1 - index
        slot = lax.rem(index, 2)
        hook(ATT_STEP + index, ATT_STEP, LAST_STEP)
        for copy in block_copies(index):
            copy.wait()
        qkv, bars, probs = qkv_two.at[slot], bars_two.at[slot], probs_two.at[slot]
        for row in range(0, block_rows, 128):
            rows = pl.ds(pl.multiple_of(block * block_rows + row, 128), 128)
            hat, _ = norm_stats(x_rows(rows))
            normed_t[:, row : row + 128] = (hat * ln[0:1, :] + ln[1:2, :]).astype(bf16).T
        held_one = attention_in(block, qkv, bars, 1)
        held_two = attention_in(block, qkv, bars, 0)
        scores = attention_mid(probs, 1, held_one)
        attention_out(block, qkv, bars, probs, 1, held_one, scores)
        scores = attention_mid(probs, 0, held_two)
        attention_out(block, qkv, bars, probs, 0, held_two, scores)
        tokens = pl.ds(pl.multiple_of(block * block_rows, block_rows), block_rows)
        for side in range(2):
            for part in range(3):
                at = side * 3 * HALF + part * HALF
                rows = slice(part * D, (part + 1) * D)
                lanes = slice(side * HALF, (side + 1) * HALF)
                mlp[rows, lanes] += mm(
                    normed_t[:, :block_rows], grad_qkv[tokens, at : at + HALF]
                )


        @pl.when(index + 2 < ATT_STEPS)
        def _():
            for copy in block_copies(index + 2):
                copy.start()

        return carry

    def first_norm(tile, carry):
        hook(LAST_STEP + tile, LAST_STEP, STEPS)
        base = tile * TILE
        tokens = pl.ds(pl.multiple_of(base, TILE), TILE)
        for side, w in enumerate((w_own, w_other)):
            for part in range(3):
                at = side * 3 * HALF + part * HALF
                back = mm(grad_qkv[tokens, at : at + HALF], w[part], NT)
                if side == 0 and part == 0:
                    grad_n[:TILE, :] = back
                else:
                    grad_n[:TILE, :] += back
        for row in range(0, TILE, 128):
            at = pl.ds(pl.multiple_of(base + row, 128), 128)
            hat, rstd = norm_stats(x_rows(at))
            gn = grad_n[row : row + 128, :]
            acc_ln[0:1, :] += jnp.sum(gn * hat, axis=0, keepdims=True)
            acc_ln[1:2, :] += jnp.sum(gn, axis=0, keepdims=True)
            scaled = gn * ln[0:1, :]
            back = rstd * (
                scaled
                - jnp.mean(scaled, axis=1, keepdims=True)
                - hat * jnp.mean(scaled * hat, axis=1, keepdims=True)
            )
            gx = res[at, :] + back
            low, high = gx[:, :HALF], gx[:, HALF:]
            dy_own[at, :] = jnp.where(head == 0, low, high).astype(bf16)
            dy_other[at, :] = jnp.where(head == 0, high, low).astype(bf16)
        return carry

    for copy in loads + weight_copies + block_copies(0) + block_copies(1):
        copy.start()
    if summing:
        lines.greet()
    after[...] = jnp.zeros_like(after)
    acc_ln[...] = jnp.zeros_like(acc_ln)
    for copy in loads:
        copy.wait()
    lax.fori_loop(0, TILES, before_mlp, 0)
    for copy in weight_copies:
        copy.wait()
    lax.fori_loop(0, CHUNKS, hidden_chunk, 0)
    acc_one[...] = jnp.zeros_like(acc_one)
    lax.fori_loop(0, TILES, after_mlp, 0)
    for copy in stores[:2]:
        copy.start()
    for side in range(2):
        grads[2][side, 0] = acc_one[side * HALF : (side + 1) * HALF, :].astype(bf16)
    mlp[...] = jnp.zeros_like(mlp)
    lax.fori_loop(0, ATT_STEPS, attention_block, 0)
    for side in range(2):
        for part in range(2):
            for kind in range(3):
                rows = slice(kind * HALF, (kind + 1) * HALF)
                source = slice(kind * D + part * HALF, kind * D + (part + 1) * HALF)
                lanes = slice(side * HALF, (side + 1) * HALF)
                grads[3][side, part, rows] = mlp[source, lanes].astype(bf16)
    lax.fori_loop(0, TILES, first_norm, 0)
    for copy in stores[2:]:
        copy.start()
    if summing:
        small.send(0)
        for index in range(EVENTS):
            left = [
                (which, len(times) + index)
                for which, times in enumerate(EVENT_AT)
                if len(times) + index < EVENTS
            ]
            run_events(left)
            if index <= 3:
                small.finish(index)
            if index < 3:
                small.send(index + 1)
        for entry in sums:
            entry.finish()
    else:
        for total, grad in zip(totals, grads):
            total[...] = grad[...]
        ln_total[...] = acc_ln[...]
    for copy in stores:
        copy.wait()


def rows_spec(width):
    return pl.BlockSpec((TILE, width), lambda i: (i, 0))


def whole_spec(shape):
    rank = len(shape)
    return pl.BlockSpec(shape, lambda i: (0,) * rank, pipeline_mode=pl.Buffered(1))


def shaped(shape, dtype=bf16):
    return jax.ShapeDtypeStruct(shape, dtype)


smem_spec = pl.BlockSpec(memory_space=pltpu.SMEM)
limits = pltpu.CompilerParams(vmem_limit_bytes=60 * 1024 * 1024)


def span_table():
    ids = np.arange(ROWS)
    inverse = 1.0 / np.maximum(ids, 1)
    shift = np.where(ids >= 1, np.log(np.maximum(ids, 1)), masked_score)
    return jnp.asarray(np.stack([inverse, shift]).astype(np.float32))


def causal_bias():
    key = np.arange(SPAN)[:, None]
    query = np.arange(2 * SPAN)[None, :] % SPAN
    return jnp.asarray(np.where(key <= query, 0.0, masked_score).astype(np.float32))


def layer_local(x_own, x_other, dy_own, dy_other, lengths, ln_params, weights):
    qkv_own, qkv_other, out_own, out_other, up_own, up_other, down_own, down_other = weights
    table = span_table()
    qkv, bars, probs, ctx = pl.pallas_call(
        forward_attention,
        grid=(TILES,),
        in_specs=[
            smem_spec,
            rows_spec(HALF),
            rows_spec(HALF),
            whole_spec((4, D)),
            whole_spec((3, D, HALF)),
            whole_spec((3, D, HALF)),
            whole_spec((SPAN, 2 * SPAN)),
        ],
        out_specs=[
            rows_spec(3 * D),
            rows_spec(2 * D),
            pl.BlockSpec((SPANS_TILE * PAIRS, 2 * SPAN, 2 * SPAN), lambda i: (i, 0, 0)),
            rows_spec(D),
        ],
        out_shape=[
            shaped((SEQ, 3 * D)),
            shaped((SEQ, 2 * D)),
            shaped((ROWS * PAIRS, 2 * SPAN, 2 * SPAN)),
            shaped((SEQ, D)),
        ],
        scratch_shapes=[pltpu.VMEM((SPAN, 2 * D), f32), pltpu.VMEM((TILE, D), bf16)],
        compiler_params=limits,
        name="forward_attention",
    )(table, x_own, x_other, ln_params, qkv_own, qkv_other, causal_bias())
    count = lax.axis_size("dp")
    summing = whole_slices(count)
    sum_buffers, extra, total_specs, total_shapes = [], {}, [], []
    anywhere = pl.BlockSpec(memory_space=pl.ANY)
    if summing:
        for shape, orders in PIECES:
            sum_buffers += sum_scratch(shape, orders, count)
            total_specs.append(anywhere)
            total_shapes.append(shaped(shape))
        sum_buffers += ln_scratch(count)
        extra = dict(collective_id=0, has_side_effects=True)
    else:
        for shape, _ in PIECES:
            total_specs.append(pl.BlockSpec(memory_space=pltpu.VMEM))
            total_shapes.append(shaped((2, *shape)))
    block_rows = SPANS_STEP * SPAN
    vmem = pl.BlockSpec(memory_space=pltpu.VMEM)
    y_own, y_other, gx_own, gx_other, *totals = pl.pallas_call(
        functools.partial(mlp_and_back, count),
        in_specs=[smem_spec, smem_spec, vmem] + [anywhere] * 16,
        out_specs=[anywhere] * 4 + total_specs + [vmem],
        out_shape=[shaped((SEQ, HALF))] * 4 + total_shapes + [shaped((4, D), f32)],
        scratch_shapes=[
            pltpu.VMEM((SEQ, HALF), bf16),
            pltpu.VMEM((SEQ, HALF), bf16),
            pltpu.VMEM((SEQ, HALF), bf16),
            pltpu.VMEM((SEQ, HALF), bf16),
            pltpu.VMEM((SEQ, D), bf16),
            pltpu.VMEM((2, block_rows, 3 * D), bf16),
            pltpu.VMEM((2, block_rows, 2 * D), bf16),
            pltpu.VMEM((2, SPANS_STEP * PAIRS, 2 * SPAN, 2 * SPAN), bf16),
            pltpu.VMEM((HALF, D), bf16),
            pltpu.VMEM((HALF, D), bf16),
            pltpu.VMEM((3, D, HALF), bf16),
            pltpu.VMEM((3, D, HALF), bf16),
            pltpu.VMEM((CHUNKS, D, 512), bf16),
            pltpu.VMEM((CHUNKS, 512, D), bf16),
            pltpu.SemaphoreType.DMA((9,)),
            pltpu.SemaphoreType.DMA((2 * CHUNKS,)),
            pltpu.SemaphoreType.DMA((2, 3)),
            pltpu.SemaphoreType.DMA((4,)),
            pltpu.VMEM((SEQ, D), f32),
            pltpu.VMEM((SEQ, 3 * D), bf16),
            pltpu.VMEM((D, SEQ), bf16),
            pltpu.VMEM((SEQ, D), bf16),
            pltpu.VMEM((SEQ, D), f32),
            pltpu.VMEM((SEQ, D), f32),
            pltpu.VMEM((512, D), f32),
            pltpu.VMEM((D, 512), f32),
            pltpu.VMEM((2, TILE, 512), f32),
            pltpu.VMEM((2, TILE, 512), f32),
            pltpu.VMEM((SPAN, 2 * D), f32),
            pltpu.VMEM((4, D), f32),
        ]
        + [pltpu.VMEM((2, *shape), bf16) for shape, _ in PIECES]
        + sum_buffers,
        compiler_params=pltpu.CompilerParams(vmem_limit_bytes=63 * 1024 * 1024, **extra),
        name="mlp_and_back",
    )(
        table,
        lengths,
        ln_params,
        x_own,
        x_other,
        dy_own,
        dy_other,
        ctx,
        qkv,
        bars,
        probs,
        out_own,
        out_other,
        qkv_own,
        qkv_other,
        up_own,
        up_other,
        down_own,
        down_other,
    )
    if not summing:
        *grads, g_ln = totals
        chips = [grad[0].astype(f32) + swap_heads(grad[1]).astype(f32) for grad in grads]
        pieces = [lax.psum(chip.astype(bf16), "dp") for chip in chips]
        totals = (*pieces, lax.psum(g_ln, ("dp", "head")))
    return (y_own, y_other), (gx_own, gx_other), totals


RATES = (
    float(D) ** (-0.5),
    4.0 * float(D) ** (-0.5),
    float(D) ** (-0.5),
    float(FF) ** (-0.5),
    0.7,
)


def adam_step(gradient, weight, moment_one, moment_two, step_rate):
    first_new = beta_one * moment_one + (1.0 - beta_one) * gradient
    second_new = beta_two * moment_two + (1.0 - beta_two) * gradient * gradient
    first_hat = first_new * (1.0 / (1.0 - beta_one**STEP))
    second_hat = second_new * (1.0 / (1.0 - beta_two**STEP))
    weight_new = weight - step_rate * (
        first_hat / (jnp.sqrt(second_hat) + epsilon_adam) + decay_rate * weight
    )
    return (weight_new, first_new, second_new)


def kind_gradient(kind, refs, step):
    joined = [
        jnp.concatenate([ref[part] for part in range(ref.shape[0])], axis=0 if kind == 0 else 1)
        for ref in refs
    ]
    if kind == 0:
        return joined[0].astype(f32)[None]
    if kind == 2:
        return jnp.concatenate(joined, axis=1).astype(f32)
    if kind == 3:
        return jnp.where(step < 2, joined[0].astype(f32), joined[1].astype(f32))
    return joined[0].astype(f32)


BLOCKS = (
    (3, (1, D, HALF), ((3, (2, HALF, HALF), lambda i: (0, i, 0)),)),
    (1, (HALF, D), ((2, (1, HALF, D), lambda i: (0, i, 0)),)),
    (
        4,
        (128, 1024),
        (
            (0, (2, 128, HALF), lambda i: (0, 4 + i, 0)),
            (1, (2, 128, HALF), lambda i: (0, 4 + i, 0)),
        ),
    ),
    (
        4,
        (HALF, D),
        (
            (0, (2, HALF, HALF), lambda i: (0, jnp.minimum(i, 1), 0)),
            (1, (2, HALF, HALF), lambda i: (0, jnp.maximum(i - 2, 0), 0)),
        ),
    ),
)


def adam_kernel(kinds, owners, *refs):
    step = pl.program_id(0)
    chip = lax.axis_index("dp")
    ins = sum(len(BLOCKS[kind][2]) + 3 for kind in kinds)
    inputs, outputs = list(refs[:ins]), list(refs[ins:])
    first = 0
    for kind in kinds:
        grads = [inputs.pop(0) for _ in BLOCKS[kind][2]]
        weight, one, two = [inputs.pop(0) for _ in range(3)]
        owned, new, first_new, second_new, copy = [outputs.pop(0) for _ in range(5)]
        steps = BLOCKS[kind][0]

        @pl.when((step >= first) & (step < first + steps))
        def _(kind=kind, grads=grads, weight=weight, one=one, two=two, owned=owned, new=new,
              first_new=first_new, second_new=second_new, copy=copy, first=first):
            gradient = kind_gradient(kind, grads, step - first)
            results = adam_step(gradient, weight[...], one[...], two[...], RATES[kind])
            owned[...] = jnp.where(owners[kind] == chip, gradient, 0.0)
            new[...] = results[0]
            first_new[...] = results[1]
            second_new[...] = results[2]
            copy[...] = results[0].astype(bf16)

        first += steps


def adam_update(kinds, owners, pieces, weights, ones, twos):
    in_specs, out_specs, out_shape, operands = [smem_spec], [], [], [owners]
    first = 0
    for index, kind in enumerate(kinds):
        steps, block, sources = BLOCKS[kind]

        def place(i, first=first, steps=steps):
            return jnp.clip(i - first, 0, steps - 1)

        def at(i, place=place, rank=len(block)):
            return (place(i),) + (0,) * (rank - 1)

        for piece, grad_block, grad_place in sources:

            def grad_at(i, place=place, grad_place=grad_place):
                return grad_place(place(i))

            in_specs.append(pl.BlockSpec(grad_block, grad_at))
            operands.append(pieces[piece])
        spec = pl.BlockSpec(block, at)
        in_specs += [spec] * 3
        out_specs += [spec] * 5
        whole = weights[index].shape
        out_shape += [shaped(whole, f32)] * 4 + [shaped(whole)]
        operands += [weights[index], ones[index], twos[index]]
        first += steps
    results = pl.pallas_call(
        functools.partial(adam_kernel, kinds),
        grid=(first,),
        in_specs=in_specs,
        out_specs=out_specs,
        out_shape=out_shape,
        compiler_params=limits,
        name="adam_update",
    )(*operands)
    return [results[index * 5 : index * 5 + 5] for index in range(len(kinds))]


def gather_inputs(tokens, cotangent, w_qkv, w_out, w_up, w_down):
    head = lax.axis_index("head")

    def both(array):
        halves = array.reshape(2, SEQ, HALF)
        own = lax.dynamic_index_in_dim(halves, head, 0, keepdims=False)
        other = lax.dynamic_index_in_dim(halves, 1 - head, 0, keepdims=False)
        return own, swap_heads(other)

    x_own, x_other = both(tokens)
    qkv_own = w_qkv.transpose(1, 0, 2).astype(bf16)
    out_own = w_out.astype(bf16)
    up_own = w_up.astype(bf16)
    down_own = w_down.astype(bf16)
    qkv_other = swap_heads(qkv_own)
    dy_own, dy_other = both(cotangent)
    weights = (
        qkv_own,
        qkv_other,
        out_own,
        swap_heads(out_own),
        up_own,
        swap_heads(up_own),
        down_own,
        swap_heads(down_own),
    )
    return x_own, x_other, dy_own, dy_other, weights


def place_rows(pieces):
    head = lax.axis_index("head")
    own, away = pieces
    arrived = swap_heads(away)
    return jnp.concatenate(
        [jnp.where(head == 0, own, arrived), jnp.where(head == 0, arrived, own)], axis=0
    )


def body(
    tokens,
    cotangent,
    lengths,
    owners,
    w_qkv,
    w_out,
    w_up,
    w_down,
    ln_params,
    m_qkv,
    m_out,
    m_up,
    m_down,
    m_ln,
    v_qkv,
    v_out,
    v_up,
    v_down,
    v_ln,
):
    x_own, x_other, dy_own, dy_other, weights = gather_inputs(
        tokens, cotangent, w_qkv, w_out, w_up, w_down
    )
    y, gx, totals = layer_local(
        x_own, x_other, dy_own, dy_other, lengths, ln_params, weights
    )
    output_rows = place_rows(y)
    grad_input = place_rows(gx)
    *pieces, t_ln = totals

    def as_blocks(array):
        return array.transpose(1, 0, 2)

    results = adam_update(
        (0, 1, 2, 3),
        owners,
        pieces,
        (as_blocks(w_qkv), w_out, w_up, w_down),
        (as_blocks(m_qkv), m_out, m_up, m_down),
        (as_blocks(v_qkv), v_out, v_up, v_down),
    )
    results[0] = [as_blocks(array) for array in results[0]]
    mine = owners[4] == lax.axis_index("dp")
    ln_results = adam_step(t_ln, ln_params, m_ln, v_ln, RATES[4])
    results.append([jnp.where(mine, t_ln, 0.0), *ln_results])
    owned, new, first, second = [
        tuple(results[kind][slot] for kind in range(5)) for slot in range(4)
    ]
    copies = tuple(results[kind][4] for kind in range(4))
    owned = tuple(array[None] for array in owned)
    return (output_rows, grad_input) + owned + new + first + second + copies


PLACED = (
    (P("dp", "head"),) * 2
    + (P("dp"), P())
    + (P(None, None, "head"), P("head", None), P(None, "head"), P("head", None), P()) * 3
)
RESULTS = (
    (P("dp", "head"),) * 2
    + (
        P("dp", None, None, "head"),
        P("dp", "head", None),
        P("dp", None, "head"),
        P("dp", "head", None),
        P("dp", None, None),
    )
    + (P(None, None, "head"), P("head", None), P(None, "head"), P("head", None), P()) * 3
    + (P(None, None, "head"), P("head", None), P(None, "head"), P("head", None))
)


def solution(mesh):
    return jax.shard_map(
        body, mesh=mesh, in_specs=PLACED, out_specs=RESULTS, check_vma=False
    )
```

```python
import functools

import jax
import jax.numpy as jnp
import numpy as np
from jax import lax
from jax.experimental import pallas as pl
from jax.experimental.pallas import tpu as pltpu
from jax.sharding import PartitionSpec as P

D = 512
HALF = 256
HEAD_DIM = 64
FF = 2048
SPAN = 128
SEQ = 2048
STEP = 5
ROWS = 16
PAIRS = 4
TILE = 512
TILES = SEQ // TILE
SPANS_TILE = TILE // SPAN

epsilon_norm = 1e-05
epsilon_adam = 1e-08
beta_one = 0.5
beta_two = 0.5
decay_rate = 0.1
masked_score = -1e30

bf16 = jnp.bfloat16
f32 = jnp.float32

NN = (((1,), (0,)), ((), ()))
NT = (((1,), (1,)), ((), ()))
TN = (((0,), (0,)), ((), ()))


def mm(left, right, dims=NN):
    return lax.dot_general(left, right, dims, preferred_element_type=f32)


def join_columns(head, own, other):
    low = jnp.where(head == 0, own, other)
    high = jnp.where(head == 0, other, own)
    return jnp.concatenate([low, high], axis=1)


def norm_stats(values):
    mean = jnp.mean(values, axis=1, keepdims=True)
    centered = values - mean
    rstd = lax.rsqrt(jnp.mean(centered * centered, axis=1, keepdims=True) + epsilon_norm)
    return centered * rstd, rstd


def head_stack(pair, low_lanes, high_lanes):
    return jnp.concatenate([pair * low_lanes, pair * high_lanes], axis=0)


def lane_masks(dtype):
    lane = lax.broadcasted_iota(jnp.int32, (1, 2 * HEAD_DIM), 1)
    low = (lane < HEAD_DIM).astype(f32)
    return low.astype(dtype), (1.0 - low).astype(dtype)


def pair_columns(pair):
    base = 3 * HALF * (pair // 2) + 2 * HEAD_DIM * (pair % 2)
    return base, base + HALF, base + 2 * HALF


def unstack_transposed(product):
    joined = jnp.concatenate(
        [product[:HEAD_DIM, :SPAN], product[HEAD_DIM:, SPAN:]], axis=0
    )
    return joined.T


def forward_attention(
    head_at, table, x_own, x_other, ln, w_own, w_other, causal, qkv, bars, probs, ctx, run_sum, normed
):
    head = lax.axis_index("head")
    step = pl.program_id(0)

    @pl.when(step == 0)
    def _():
        run_sum[...] = jnp.zeros_like(run_sum)

    for row in range(0, TILE, 128):
        rows = pl.ds(row, 128)
        x = join_columns(head, x_own[rows, :].astype(f32), x_other[rows, :].astype(f32))
        xhat, _ = norm_stats(x)
        normed[rows, :] = (xhat * ln[0:1, :] + ln[1:2, :]).astype(bf16)
    for side, w in enumerate((w_own, w_other)):
        for part in range(3):
            value = mm(normed[...], w[part])
            if part == 0:
                value = value * float(HEAD_DIM) ** (-0.5)
            base = side * 3 * HALF + part * HALF
            qkv[:, base : base + HALF] = value.astype(bf16)
    low_lanes, high_lanes = lane_masks(bf16)

    def score_span(span):
        rows = pl.ds(span * SPAN, SPAN)
        row_id = step * SPANS_TILE + span
        inverse = table[0, row_id]
        shift = table[1, row_id]
        scores, stacked = [], []
        for pair in range(PAIRS):
            at_q, at_k, at_v = pair_columns(pair)
            lanes = pl.ds(pair * 128, 128)
            lanes_v = pl.ds(512 + pair * 128, 128)
            key = qkv[rows, at_k : at_k + 128]
            value = qkv[rows, at_v : at_v + 128]
            key_bar = (run_sum[:, lanes] * inverse).astype(bf16)
            value_bar = (run_sum[:, lanes_v] * inverse).astype(bf16)
            run_sum[:, lanes] += key.astype(f32)
            run_sum[:, lanes_v] += value.astype(f32)
            bars[rows, lanes] = key_bar
            bars[rows, lanes_v] = value_bar
            query = head_stack(qkv[rows, at_q : at_q + 128], low_lanes, high_lanes)
            scores.append((mm(key, query, NT) + causal[...], mm(key_bar, query, NT) + shift))
            stacked.append(jnp.concatenate([value, value_bar], axis=0))
        return scores, stacked

    def soft_span(span, scores):
        expo = []
        for direct, summary in scores:
            top = jnp.maximum(
                jnp.max(direct, axis=0, keepdims=True), jnp.max(summary, axis=0, keepdims=True)
            )
            expo.append((jnp.exp(direct - top), jnp.exp(summary - top)))
        both = []
        for pair, (direct, summary) in enumerate(expo):
            total = jnp.sum(direct, axis=0, keepdims=True) + jnp.sum(
                summary, axis=0, keepdims=True
            )
            scale = 1.0 / total
            prob = jnp.concatenate(
                [(direct * scale).astype(bf16), (summary * scale).astype(bf16)], axis=0
            )
            probs[span * PAIRS + pair] = prob
            both.append(prob)
        return both

    def context_span(span, stacked, both):
        rows = pl.ds(span * SPAN, SPAN)
        for pair in range(PAIRS):
            lanes = pl.ds(pair * 128, 128)
            ctx[rows, lanes] = unstack_transposed(mm(stacked[pair], both[pair], TN)).astype(bf16)

    ready = score_span(0)
    for span in range(SPANS_TILE):
        scores, stacked = ready
        if span + 1 < SPANS_TILE:
            ready = score_span(span + 1)
        both = soft_span(span, scores)
        context_span(span, stacked, both)


def gelu_parts(u):
    share = lax.erf(u * 0.7071067811865476) * 0.5 + 0.5
    bell = jnp.exp2((u * u) * -0.7213475204444817)
    return u * share, share + u * bell * 0.3989422804014327


def swap_heads(value):
    return lax.ppermute(value, "head", [(0, 1), (1, 0)])


def chip_grid(count):
    side = 1 << ((count.bit_length() - 1) // 3)
    return (count // (side * side), side, side)


class Lines:
    def __init__(self, count):
        self.sizes = chip_grid(count)
        self.strides = (self.sizes[1] * self.sizes[2], self.sizes[2], 1)
        self.chip = lax.axis_index("dp")
        self.head = lax.axis_index("head")
        self.places = [
            lax.rem(self.chip // stride, size) for stride, size in zip(self.strides, self.sizes)
        ]
        self.members = [
            [self.find(axis, ahead) for ahead in range(1, size)]
            for axis, size in enumerate(self.sizes)
        ]

    def partner(self):
        return (self.chip, 1 - self.head)

    def member(self, axis, ahead):
        return self.members[axis][ahead - 1]

    def find(self, axis, ahead):
        size = self.sizes[axis]
        place = 1 - self.places[axis]
        if size > 2:
            place = lax.rem(self.places[axis] + ahead, size)
        chip = self.chip + (place - self.places[axis]) * self.strides[axis]
        return place, (chip, self.head)

    def greet(self):
        barrier = pltpu.get_barrier_semaphore()
        others = [self.partner()]
        for axis in range(3):
            others += [self.member(axis, ahead)[1] for ahead in range(1, self.sizes[axis])]
        for other in others:
            pl.semaphore_signal(
                barrier, inc=1, device_id=other, device_id_type=pl.DeviceIdType.MESH
            )
        pl.semaphore_wait(barrier, len(others))


X_FIRST, Y_FIRST = (2, 1, 0), (1, 2, 0)


def whole_slices(count):
    return all(shape[1] % (16 * count) == 0 for shape, _ in PIECES)


def chunk_rows(rows):
    return next(chunk for chunk in (128, 96, 64, 48, 32, 16) if rows % chunk == 0)


def sum_scratch(shape, orders, count):
    parts, rows, lanes = shape
    sizes = chip_grid(count)
    shapes = [pltpu.VMEM(shape, bf16)]
    sems = [pltpu.SemaphoreType.DMA((3,))]
    for order in orders:
        left = rows
        for axis in order:
            left //= sizes[axis]
            shapes.append(pltpu.VMEM((sizes[axis] - 1, left, lanes), bf16))
            sems.append(pltpu.SemaphoreType.DMA((2, 2, sizes[axis] - 1)))
    return shapes + sems


class DpSum:
    def __init__(self, lines, orders, grads, total, scratch):
        self.lines = lines
        self.orders = orders
        self.parts = range(len(orders))
        self.grads = grads
        self.total = total
        self.rows = grads.shape[2]
        self.work, self.final = grads.at[0], scratch.pop(0)
        self.slots = [[scratch.pop(0) for _ in order] for order in orders]
        self.core_sem = scratch.pop(0)
        self.sems = [[scratch.pop(0) for _ in order] for order in orders]
        self.base = []
        for order in orders:
            bases, piece = [0], self.rows
            for axis in order:
                piece //= lines.sizes[axis]
                bases.append(bases[-1] + lines.places[axis] * piece)
            self.base.append(bases)

    def remote(self, source, target, send_sem, recv_sem, device):
        return pltpu.make_async_remote_copy(
            src_ref=source,
            dst_ref=target,
            send_sem=send_sem,
            recv_sem=recv_sem,
            device_id=device,
            device_id_type=pl.DeviceIdType.MESH,
        )

    def core_copy(self):
        return self.remote(
            self.grads.at[1],
            self.final,
            self.core_sem.at[0],
            self.core_sem.at[1],
            self.lines.partner(),
        )

    def core_send(self):
        self.core_copy().start()

    def core_sum(self):
        self.core_copy().wait()
        chunk = chunk_rows(self.rows)
        for part in self.parts:

            def add(index, carry, part=part):
                rows = pl.ds(pl.multiple_of(index * chunk, chunk), chunk)
                self.work[part, rows, :] = self.work[part, rows, :] + self.final[part, rows, :]
                return carry

            lax.fori_loop(0, self.rows // chunk, add, 0)

    def spread_copies(self, part, stage):
        axis = self.orders[part][stage]
        size = self.lines.sizes[axis]
        base = self.base[part][stage]
        piece = self.rows
        for at in self.orders[part][: stage + 1]:
            piece //= self.lines.sizes[at]
        copies = []
        for ahead in range(1, size):
            place, device = self.lines.member(axis, ahead)
            start = pl.multiple_of(base + place * piece, 16)
            copies.append(
                self.remote(
                    self.work.at[part, pl.ds(start, piece)],
                    self.slots[part][stage].at[ahead - 1],
                    self.sems[part][stage].at[0, 0, ahead - 1],
                    self.sems[part][stage].at[0, 1, ahead - 1],
                    device,
                )
            )
        return copies, self.base[part][stage + 1], piece

    def spread_send(self, part, stage):
        for copy in self.spread_copies(part, stage)[0]:
            copy.start()

    def spread_sum(self, part, stage):
        copies, mine, piece = self.spread_copies(part, stage)
        for copy in copies:
            copy.wait()
        slots = self.slots[part][stage]
        target = self.final if stage == 2 else self.work
        chunk = chunk_rows(piece)

        def add(index, carry):
            offset = pl.multiple_of(index * chunk, chunk)
            rows = pl.ds(pl.multiple_of(mine + offset, 16), chunk)
            value = self.work[part, rows, :]
            if len(copies) > 1:
                value = value.astype(f32)
            for slot in range(len(copies)):
                value = value + slots[slot, pl.ds(offset, chunk), :].astype(value.dtype)
            target[part, rows, :] = value.astype(bf16)
            return carry

        lax.fori_loop(0, piece // chunk, add, 0)

    def gather_copies(self, part, stage):
        axis = self.orders[part][stage]
        size = self.lines.sizes[axis]
        piece = self.rows
        for at in self.orders[part][: stage + 1]:
            piece //= self.lines.sizes[at]
        mine = pl.multiple_of(self.base[part][stage + 1], 16)
        rows = pl.ds(mine, piece)
        copies = []
        for ahead in range(1, size):
            _, device = self.lines.member(axis, ahead)
            copies.append(
                self.remote(
                    self.final.at[part, rows],
                    self.final.at[part, rows],
                    self.sems[part][stage].at[1, 0, ahead - 1],
                    self.sems[part][stage].at[1, 1, ahead - 1],
                    device,
                )
            )
        return copies

    def gather_send(self, part, stage):
        for copy in self.gather_copies(part, stage):
            copy.start()

    def gather_wait(self, part, stage):
        for copy in self.gather_copies(part, stage):
            copy.wait()

    def store_copy(self):
        return pltpu.make_async_copy(self.final, self.total, self.core_sem.at[2])

    def event(self, index):
        if index == 0:
            self.core_send()
        elif index == 1:
            self.core_sum()
        for part in self.parts:
            if 2 <= index <= 4:
                self.spread_sum(part, index - 2)
            elif index >= 5:
                self.gather_wait(part, 7 - index)
            if 1 <= index <= 3:
                self.spread_send(part, index - 1)
            elif 4 <= index <= 6:
                self.gather_send(part, 6 - index)
        if index == 7:
            self.store_copy().start()

    def finish(self):
        self.store_copy().wait()


EVENTS = 8


def ln_scratch(count):
    return [
        pltpu.VMEM((2, 4, D), f32),
        pltpu.SemaphoreType.DMA((2,)),
        *[pltpu.VMEM((size, 4, D), f32) for size in chip_grid(count)],
        *[pltpu.SemaphoreType.DMA((2, max(size - 1, 1))) for size in chip_grid(count)],
    ]


class LnSum:
    def __init__(self, lines, value, total, scratch):
        self.lines = lines
        self.value = value
        self.total = total
        self.core, self.core_sem = scratch[:2]
        self.slots = scratch[2:5]
        self.sems = scratch[5:8]

    def stage_copies(self, stage):
        lines = self.lines
        if stage == 0:
            mine = self.core.at[lines.head]
            return [
                pltpu.make_async_remote_copy(
                    src_ref=mine,
                    dst_ref=mine,
                    send_sem=self.core_sem.at[0],
                    recv_sem=self.core_sem.at[1],
                    device_id=lines.partner(),
                    device_id_type=pl.DeviceIdType.MESH,
                )
            ]
        axis = stage - 1
        mine = self.slots[axis].at[lines.places[axis]]
        return [
            pltpu.make_async_remote_copy(
                src_ref=mine,
                dst_ref=mine,
                send_sem=self.sems[axis].at[0, ahead - 1],
                recv_sem=self.sems[axis].at[1, ahead - 1],
                device_id=lines.member(axis, ahead)[1],
                device_id_type=pl.DeviceIdType.MESH,
            )
            for ahead in range(1, lines.sizes[axis])
        ]

    def send(self, stage):
        if stage == 0:
            self.core[self.lines.head] = self.value[...]
        for copy in self.stage_copies(stage):
            copy.start()

    def finish(self, stage):
        for copy in self.stage_copies(stage):
            copy.wait()
        slots = self.core if stage == 0 else self.slots[stage - 1]
        value = slots[0]
        for slot in range(1, slots.shape[0]):
            value = value + slots[slot]
        if stage == 3:
            self.total[...] = value
        else:
            self.slots[stage][self.lines.places[stage]] = value


PIECES = (
    ((2, 1024, HALF), (X_FIRST, Y_FIRST)),
    ((2, 1024, HALF), (X_FIRST, Y_FIRST)),
    ((1, HALF, D), (Y_FIRST,)),
    ((2, 3 * HALF, HALF), (X_FIRST, Y_FIRST)),
)
CHUNKS = FF // 512
CHUNK_STEP = TILES
POST_STEP = CHUNK_STEP + CHUNKS
ATT_STEP = POST_STEP + TILES
SPANS_STEP = 2
ATT_STEPS = ROWS // SPANS_STEP
LAST_STEP = ATT_STEP + ATT_STEPS
STEPS = LAST_STEP + TILES
EVENT_AT = (
    ((6, 0), (6, 1), (7, 1), (8, 0), (12, 0), (15, 0), (17, 0), (19, 0),),
    ((8, 0), (9, 0), (13, 0), (16, 0), (19, 0),),
    ((14, 0), (16, 0), (18, 0),),
    ((20, 0), (22, 0),),
)


def mlp_and_back(
    count,
    table,
    lengths,
    ln,
    x_own_at,
    x_other_at,
    dy_own_at,
    dy_other_at,
    ctx_at,
    qkv_at,
    bars_at,
    probs_at,
    out_own_at,
    out_other_at,
    w_own_at,
    w_other_at,
    up_own,
    up_other,
    down_own,
    down_other,
    y_own_at,
    y_other_at,
    gx_own_at,
    gx_other_at,
    *refs,
):
    summing = whole_slices(count)
    kinds = len(PIECES)
    totals, ln_total = refs[:kinds], refs[kinds]
    (x_own, x_other, dy_own, dy_other, ctx, qkv_two, bars_two, probs_two, out_own, out_other,
     w_own, w_other, up_all, down_all, load_sem, weight_sem, block_sem, store_sem, res, grad_qkv,
     normed_t, gm, mlp, grad_n, acc_one, acc_two, hid, grad_hid, after,
     acc_ln) = refs[kinds + 1 : kinds + 31]
    grads = refs[kinds + 31 : kinds + 31 + len(PIECES)]
    scratch = list(refs[kinds + 31 + len(PIECES) :])
    head = lax.axis_index("head")
    used = lengths[head]
    sums = []
    if summing:
        lines = Lines(count)
        for (_, orders), grad, total in zip(PIECES, grads, totals):
            sums.append(DpSum(lines, orders, grad, total, scratch))
        small = LnSum(lines, acc_ln, ln_total, scratch)

    def run_events(events):
        for index, event in events:
            sums[index].event(event)

    def hook(step, first, end, place=0):
        for at in range(first, end if summing else 0):
            events = [
                (index, event)
                for index, times in enumerate(EVENT_AT)
                for event, time in enumerate(times)
                if time == (at, place)
            ]
            if events:

                @pl.when(step == at)
                def _(events=events):
                    run_events(events)

    mine = pl.ds(head * SEQ, SEQ)
    loads = [
        pltpu.make_async_copy(source, target, load_sem.at[index])
        for index, (source, target) in enumerate(
            (
                (ctx_at, ctx),
                (out_own_at, out_own),
                (out_other_at, out_other),
                (x_own_at.at[mine], x_own),
                (x_other_at.at[mine], x_other),
                (dy_own_at.at[mine], dy_own),
                (dy_other_at.at[mine], dy_other),
                (w_own_at, w_own),
                (w_other_at, w_other),
            )
        )
    ]
    weight_copies = []
    for chunk in range(CHUNKS):
        up_w, down_w = ((up_own, down_own), (up_other, down_other))[chunk % 2]
        cut = pl.ds(chunk // 2 * 512, 512)
        pairs = ((up_w.at[:, cut], up_all.at[chunk]), (down_w.at[cut], down_all.at[chunk]))
        for which, (source, target) in enumerate(pairs):
            sem = weight_sem.at[2 * chunk + which]
            weight_copies.append(pltpu.make_async_copy(source, target, sem))
    block_rows = SPANS_STEP * SPAN
    block_probs = SPANS_STEP * PAIRS

    def block_copies(index):
        block = ATT_STEPS - 1 - index
        slot = lax.rem(index, 2)
        rows = pl.ds(block * block_rows, block_rows)
        many = pl.ds(block * block_probs, block_probs)
        pairs = (
            (qkv_at.at[rows], qkv_two.at[slot]),
            (bars_at.at[rows], bars_two.at[slot]),
            (probs_at.at[many], probs_two.at[slot]),
        )
        return [
            pltpu.make_async_copy(source, target, block_sem.at[slot, which])
            for which, (source, target) in enumerate(pairs)
        ]

    stores = []
    for index, (source, target) in enumerate(
        (
            (ctx.at[:, pl.ds(0, HALF)], y_own_at),
            (ctx.at[:, pl.ds(HALF, HALF)], y_other_at),
            (dy_own, gx_own_at),
            (dy_other, gx_other_at),
        )
    ):
        if summing and index % 2 == 1:
            stores.append(
                pltpu.make_async_remote_copy(
                    src_ref=source,
                    dst_ref=target,
                    send_sem=store_sem.at[index],
                    recv_sem=store_sem.at[4 + index // 2],
                    device_id=lines.partner(),
                    device_id_type=pl.DeviceIdType.MESH,
                )
            )
        else:
            stores.append(pltpu.make_async_copy(source, target, store_sem.at[index]))

    def x_rows(rows):
        return join_columns(head, x_own[rows, :].astype(f32), x_other[rows, :].astype(f32))

    def dy_rows(rows):
        return join_columns(head, dy_own[rows, :].astype(f32), dy_other[rows, :].astype(f32))

    def valid_rows(first):
        ids = lax.broadcasted_iota(jnp.int32, (128, 1), 0) + first
        return (ids < used).astype(f32)

    def before_mlp(tile, carry):
        base = tile * TILE
        tokens = pl.ds(pl.multiple_of(base, TILE), TILE)
        res[tokens, :] = mm(ctx[tokens, :HALF], out_own[...]) + mm(
            ctx[tokens, HALF:], out_other[...]
        )
        mlp[tokens, :] = jnp.zeros((TILE, D), f32)
        grad_n[tokens, :] = jnp.zeros((TILE, D), f32)
        for row in range(0, TILE, 128):
            at = pl.ds(pl.multiple_of(base + row, 128), 128)
            valid = valid_rows(base + row)
            h = x_rows(at) + valid * res[at, :]
            res[at, :] = h
            hat, _ = norm_stats(h)
            n2 = (hat * ln[2:3, :] + ln[3:4, :]).astype(bf16)
            grad_qkv[at, :D] = n2
            normed_t[:, at] = n2.T
            gm[at, :] = (valid * dy_rows(at)).astype(bf16)
        return carry

    def chunk_in(chunk, tile):
        tokens = pl.ds(tile * TILE, TILE)
        hid[tile % 2] = mm(grad_qkv[tokens, :D], up_all[chunk])
        grad_hid[tile % 2] = mm(gm[tokens, :], down_all[chunk], NT)

    def act_rows(tile, row, size):
        return pl.ds(tile % 2 * TILE + row, size), pl.ds((2 + tile % 2) * TILE + row, size)

    def chunk_mid(tile):
        slot = tile % 2
        for row in range(0, TILE, 16):
            rows = pl.ds(row, 16)
            a, da = gelu_parts(hid[slot, rows, :])
            at_act, at_gu = act_rows(tile, row, 16)
            grad_qkv[at_act, D : 2 * D] = a.astype(bf16)
            grad_qkv[at_gu, D : 2 * D] = (grad_hid[slot, rows, :] * da).astype(bf16)

    def chunk_out(chunk, tile):
        tokens = pl.ds(tile * TILE, TILE)
        at_act, at_gu = act_rows(tile, 0, TILE)
        act = grad_qkv[at_act, D : 2 * D]
        gu = grad_qkv[at_gu, D : 2 * D]
        mlp[tokens, :] += mm(act, down_all[chunk])
        grad_n[tokens, :] += mm(gu, up_all[chunk], NT)
        part_down = mm(act, gm[tokens, :], TN)
        part_up = mm(normed_t[:, tokens], gu)
        if tile == 0:
            acc_one[...] = part_down
            acc_two[...] = part_up
        else:
            acc_one[...] += part_down
            acc_two[...] += part_up

    def chunk_tiles(chunk, first):
        chunk_in(chunk, first)
        chunk_in(chunk, first + 1)
        chunk_mid(first)
        chunk_out(chunk, first)
        chunk_mid(first + 1)
        chunk_out(chunk, first + 1)

    def hidden_chunk(chunk, carry):
        step = CHUNK_STEP + chunk
        hook(step, CHUNK_STEP, POST_STEP)
        chunk_tiles(chunk, 0)
        hook(step, CHUNK_STEP, POST_STEP, 1)
        chunk_tiles(chunk, 2)
        side = lax.rem(chunk, 2)

        for half in range(2):

            @pl.when(chunk // 2 == half)
            def _(half=half):
                for part in range(2):
                    lanes = slice(part * HALF, (part + 1) * HALF)
                    grads[half][side, part, :512] = acc_one[:, lanes].astype(bf16)
                    grads[half][side, part, 512:] = acc_two[:, lanes].astype(bf16)

        return carry

    def after_mlp(tile, carry):
        hook(POST_STEP + tile, POST_STEP, ATT_STEP)
        base = tile * TILE
        tokens = pl.ds(pl.multiple_of(base, TILE), TILE)
        for row in range(0, TILE, 128):
            at = pl.ds(pl.multiple_of(base + row, 128), 128)
            valid = valid_rows(base + row)
            h = res[at, :]
            mlp[at, :] = h + valid * mlp[at, :]
            gn = grad_n[at, :]
            hat, rstd = norm_stats(h)
            acc_ln[2:3, :] += jnp.sum(gn * hat, axis=0, keepdims=True)
            acc_ln[3:4, :] += jnp.sum(gn, axis=0, keepdims=True)
            scaled = gn * ln[2:3, :]
            back = rstd * (
                scaled
                - jnp.mean(scaled, axis=1, keepdims=True)
                - hat * jnp.mean(scaled * hat, axis=1, keepdims=True)
            )
            gh = dy_rows(at) + back
            res[at, :] = gh
            gm[at, :] = (valid * gh).astype(bf16)
        ga = gm[tokens, :]
        acc_one[...] += mm(ctx[tokens, :], ga, TN)
        low, high = mlp[tokens, :HALF], mlp[tokens, HALF:]
        ctx[tokens, :HALF] = jnp.where(head == 0, low, high).astype(bf16)
        ctx[tokens, HALF:] = jnp.where(head == 0, high, low).astype(bf16)
        grad_low = mm(ga, out_own[...], NT)
        grad_high = mm(ga, out_other[...], NT)
        gm[tokens, :HALF] = grad_low.astype(bf16)
        gm[tokens, HALF:] = grad_high.astype(bf16)
        return carry

    low_lanes, high_lanes = lane_masks(bf16)
    scale_factor = float(HEAD_DIM) ** (-0.5)

    def span_tokens(block, span):
        return pl.ds(pl.multiple_of(block * block_rows + span * SPAN, SPAN), SPAN)

    def attention_in(block, qkv, bars, span):
        rows = pl.ds(span * SPAN, SPAN)
        held = []
        for pair in range(PAIRS):
            _, _, at_v = pair_columns(pair)
            lanes = pl.ds(pair * 128, 128)
            lanes_v = pl.ds(512 + pair * 128, 128)
            values = jnp.concatenate([qkv[rows, at_v : at_v + 128], bars[rows, lanes_v]], axis=0)
            grad = head_stack(gm[span_tokens(block, span), lanes], low_lanes, high_lanes)
            held.append((grad, mm(values, grad, NT)))
        return held

    def attention_mid(probs, span, held):
        scores = []
        for pair in range(PAIRS):
            prob_f = probs[span * PAIRS + pair].astype(f32)
            weighted = held[pair][1] * prob_f
            delta = jnp.sum(weighted, axis=0, keepdims=True)
            scores.append((weighted - prob_f * delta).astype(bf16))
        return scores

    def attention_out(block, qkv, bars, probs, span, held, scores):
        rows = pl.ds(span * SPAN, SPAN)
        tokens = span_tokens(block, span)
        inverse = table[0, block * SPANS_STEP + span]
        for pair in range(PAIRS):
            at_q, at_k, at_v = pair_columns(pair)
            lanes = pl.ds(pair * 128, 128)
            lanes_v = pl.ds(512 + pair * 128, 128)
            keys = jnp.concatenate([qkv[rows, at_k : at_k + 128], bars[rows, lanes]], axis=0)
            query = head_stack(qkv[rows, at_q : at_q + 128], low_lanes, high_lanes)
            grad_q = unstack_transposed(mm(keys, scores[pair], TN)) * scale_factor
            grad_k = mm(scores[pair], query)
            grad_v = mm(probs[span * PAIRS + pair], held[pair][0])
            grad_qkv[tokens, at_q : at_q + 128] = grad_q.astype(bf16)
            grad_qkv[tokens, at_k : at_k + 128] = (grad_k[:SPAN] + after[:, lanes]).astype(bf16)
            grad_qkv[tokens, at_v : at_v + 128] = (grad_v[:SPAN] + after[:, lanes_v]).astype(bf16)
            after[:, lanes] += grad_k[SPAN:] * inverse
            after[:, lanes_v] += grad_v[SPAN:] * inverse

    def attention_block(index, carry):
        block = ATT_STEPS - 1 - index
        slot = lax.rem(index, 2)
        hook(ATT_STEP + index, ATT_STEP, LAST_STEP)
        for copy in block_copies(index):
            copy.wait()
        qkv, bars, probs = qkv_two.at[slot], bars_two.at[slot], probs_two.at[slot]
        for row in range(0, block_rows, 128):
            rows = pl.ds(pl.multiple_of(block * block_rows + row, 128), 128)
            hat, _ = norm_stats(x_rows(rows))
            normed_t[:, row : row + 128] = (hat * ln[0:1, :] + ln[1:2, :]).astype(bf16).T
        held_one = attention_in(block, qkv, bars, 1)
        held_two = attention_in(block, qkv, bars, 0)
        scores = attention_mid(probs, 1, held_one)
        attention_out(block, qkv, bars, probs, 1, held_one, scores)
        scores = attention_mid(probs, 0, held_two)
        attention_out(block, qkv, bars, probs, 0, held_two, scores)
        tokens = pl.ds(pl.multiple_of(block * block_rows, block_rows), block_rows)
        for side in range(2):
            for part in range(3):
                at = side * 3 * HALF + part * HALF
                rows = slice(part * D, (part + 1) * D)
                lanes = slice(side * HALF, (side + 1) * HALF)
                mlp[rows, lanes] += mm(
                    normed_t[:, :block_rows], grad_qkv[tokens, at : at + HALF]
                )


        @pl.when(index + 2 < ATT_STEPS)
        def _():
            for copy in block_copies(index + 2):
                copy.start()

        return carry

    def first_norm(tile, carry):
        hook(LAST_STEP + tile, LAST_STEP, STEPS)
        base = tile * TILE
        tokens = pl.ds(pl.multiple_of(base, TILE), TILE)
        for side, w in enumerate((w_own, w_other)):
            for part in range(3):
                at = side * 3 * HALF + part * HALF
                back = mm(grad_qkv[tokens, at : at + HALF], w[part], NT)
                if side == 0 and part == 0:
                    grad_n[:TILE, :] = back
                else:
                    grad_n[:TILE, :] += back
        for row in range(0, TILE, 128):
            at = pl.ds(pl.multiple_of(base + row, 128), 128)
            hat, rstd = norm_stats(x_rows(at))
            gn = grad_n[row : row + 128, :]
            acc_ln[0:1, :] += jnp.sum(gn * hat, axis=0, keepdims=True)
            acc_ln[1:2, :] += jnp.sum(gn, axis=0, keepdims=True)
            scaled = gn * ln[0:1, :]
            back = rstd * (
                scaled
                - jnp.mean(scaled, axis=1, keepdims=True)
                - hat * jnp.mean(scaled * hat, axis=1, keepdims=True)
            )
            gx = res[at, :] + back
            low, high = gx[:, :HALF], gx[:, HALF:]
            dy_own[at, :] = jnp.where(head == 0, low, high).astype(bf16)
            dy_other[at, :] = jnp.where(head == 0, high, low).astype(bf16)
        return carry

    for copy in loads + weight_copies + block_copies(0) + block_copies(1):
        copy.start()
    if summing:
        lines.greet()
    after[...] = jnp.zeros_like(after)
    acc_ln[...] = jnp.zeros_like(acc_ln)
    for copy in loads:
        copy.wait()
    lax.fori_loop(0, TILES, before_mlp, 0)
    for copy in weight_copies:
        copy.wait()
    lax.fori_loop(0, CHUNKS, hidden_chunk, 0)
    acc_one[...] = jnp.zeros_like(acc_one)
    lax.fori_loop(0, TILES, after_mlp, 0)
    for copy in stores[:2]:
        copy.start()
    for side in range(2):
        grads[2][side, 0] = acc_one[side * HALF : (side + 1) * HALF, :].astype(bf16)
    mlp[...] = jnp.zeros_like(mlp)
    lax.fori_loop(0, ATT_STEPS, attention_block, 0)
    for side in range(2):
        for part in range(2):
            for kind in range(3):
                rows = slice(kind * HALF, (kind + 1) * HALF)
                source = slice(kind * D + part * HALF, kind * D + (part + 1) * HALF)
                lanes = slice(side * HALF, (side + 1) * HALF)
                grads[3][side, part, rows] = mlp[source, lanes].astype(bf16)
    lax.fori_loop(0, TILES, first_norm, 0)
    for copy in stores[2:]:
        copy.start()
    if summing:
        small.send(0)
        for index in range(EVENTS):
            left = [
                (which, len(times) + index)
                for which, times in enumerate(EVENT_AT)
                if len(times) + index < EVENTS
            ]
            run_events(left)
            if index <= 3:
                small.finish(index)
            if index < 3:
                small.send(index + 1)
        for entry in sums:
            entry.finish()
    else:
        for total, grad in zip(totals, grads):
            total[...] = grad[...]
        ln_total[...] = acc_ln[...]
    for copy in stores:
        copy.wait()


def rows_spec(width):
    return pl.BlockSpec((TILE, width), lambda i, *_: (i, 0))


def whole_spec(shape):
    rank = len(shape)
    return pl.BlockSpec(shape, lambda i, *_: (0,) * rank, pipeline_mode=pl.Buffered(1))


def shaped(shape, dtype=bf16):
    return jax.ShapeDtypeStruct(shape, dtype)


smem_spec = pl.BlockSpec(memory_space=pltpu.SMEM)
limits = pltpu.CompilerParams(vmem_limit_bytes=60 * 1024 * 1024)


def span_table():
    ids = np.arange(ROWS)
    inverse = 1.0 / np.maximum(ids, 1)
    shift = np.where(ids >= 1, np.log(np.maximum(ids, 1)), masked_score)
    return jnp.asarray(np.stack([inverse, shift]).astype(np.float32))


def causal_bias():
    key = np.arange(SPAN)[:, None]
    query = np.arange(2 * SPAN)[None, :] % SPAN
    return jnp.asarray(np.where(key <= query, 0.0, masked_score).astype(np.float32))


def layer_local(x_own, x_other, dy_own, dy_other, lengths, ln_params, weights):
    qkv_own, qkv_other, out_own, out_other, up_own, up_other, down_own, down_other = weights
    table = span_table()
    qkv, bars, probs, ctx = pl.pallas_call(
        forward_attention,
        grid_spec=pltpu.PrefetchScalarGridSpec(
        num_scalar_prefetch=1,
        grid=(TILES,),
        in_specs=[
            smem_spec,
            pl.BlockSpec((TILE, HALF), lambda i, head: (head[0] * TILES + i, 0)),
            pl.BlockSpec((TILE, HALF), lambda i, head: (head[0] * TILES + i, 0)),
            whole_spec((4, D)),
            whole_spec((3, D, HALF)),
            whole_spec((3, D, HALF)),
            whole_spec((SPAN, 2 * SPAN)),
        ],
        out_specs=[
            rows_spec(3 * D),
            rows_spec(2 * D),
            pl.BlockSpec((SPANS_TILE * PAIRS, 2 * SPAN, 2 * SPAN), lambda i, head: (i, 0, 0)),
            rows_spec(D),
        ],
        scratch_shapes=[pltpu.VMEM((SPAN, 2 * D), f32), pltpu.VMEM((TILE, D), bf16)],
        ),
        out_shape=[
            shaped((SEQ, 3 * D)),
            shaped((SEQ, 2 * D)),
            shaped((ROWS * PAIRS, 2 * SPAN, 2 * SPAN)),
            shaped((SEQ, D)),
        ],
        compiler_params=limits,
        name="forward_attention",
    )(lax.axis_index("head").reshape(1), table, x_own, x_other, ln_params, qkv_own, qkv_other, causal_bias())
    count = lax.axis_size("dp")
    summing = whole_slices(count)
    sum_buffers, extra, total_specs, total_shapes = [], {}, [], []
    anywhere = pl.BlockSpec(memory_space=pl.ANY)
    if summing:
        for shape, orders in PIECES:
            sum_buffers += sum_scratch(shape, orders, count)
            total_specs.append(anywhere)
            total_shapes.append(shaped(shape))
        sum_buffers += ln_scratch(count)
        extra = dict(collective_id=0, has_side_effects=True)
    else:
        for shape, _ in PIECES:
            total_specs.append(pl.BlockSpec(memory_space=pltpu.VMEM))
            total_shapes.append(shaped((2, *shape)))
    block_rows = SPANS_STEP * SPAN
    vmem = pl.BlockSpec(memory_space=pltpu.VMEM)
    y_own, y_other, gx_own, gx_other, *totals = pl.pallas_call(
        functools.partial(mlp_and_back, count),
        in_specs=[smem_spec, smem_spec, vmem] + [anywhere] * 16,
        out_specs=[anywhere] * 4 + total_specs + [vmem],
        out_shape=[shaped((SEQ, HALF))] * 4 + total_shapes + [shaped((4, D), f32)],
        scratch_shapes=[
            pltpu.VMEM((SEQ, HALF), bf16),
            pltpu.VMEM((SEQ, HALF), bf16),
            pltpu.VMEM((SEQ, HALF), bf16),
            pltpu.VMEM((SEQ, HALF), bf16),
            pltpu.VMEM((SEQ, D), bf16),
            pltpu.VMEM((2, block_rows, 3 * D), bf16),
            pltpu.VMEM((2, block_rows, 2 * D), bf16),
            pltpu.VMEM((2, SPANS_STEP * PAIRS, 2 * SPAN, 2 * SPAN), bf16),
            pltpu.VMEM((HALF, D), bf16),
            pltpu.VMEM((HALF, D), bf16),
            pltpu.VMEM((3, D, HALF), bf16),
            pltpu.VMEM((3, D, HALF), bf16),
            pltpu.VMEM((CHUNKS, D, 512), bf16),
            pltpu.VMEM((CHUNKS, 512, D), bf16),
            pltpu.SemaphoreType.DMA((9,)),
            pltpu.SemaphoreType.DMA((2 * CHUNKS,)),
            pltpu.SemaphoreType.DMA((2, 3)),
            pltpu.SemaphoreType.DMA((6,)),
            pltpu.VMEM((SEQ, D), f32),
            pltpu.VMEM((SEQ, 3 * D), bf16),
            pltpu.VMEM((D, SEQ), bf16),
            pltpu.VMEM((SEQ, D), bf16),
            pltpu.VMEM((SEQ, D), f32),
            pltpu.VMEM((SEQ, D), f32),
            pltpu.VMEM((512, D), f32),
            pltpu.VMEM((D, 512), f32),
            pltpu.VMEM((2, TILE, 512), f32),
            pltpu.VMEM((2, TILE, 512), f32),
            pltpu.VMEM((SPAN, 2 * D), f32),
            pltpu.VMEM((4, D), f32),
        ]
        + [pltpu.VMEM((2, *shape), bf16) for shape, _ in PIECES]
        + sum_buffers,
        compiler_params=pltpu.CompilerParams(vmem_limit_bytes=63 * 1024 * 1024, **extra),
        name="mlp_and_back",
    )(
        table,
        lengths,
        ln_params,
        x_own,
        x_other,
        dy_own,
        dy_other,
        ctx,
        qkv,
        bars,
        probs,
        out_own,
        out_other,
        qkv_own,
        qkv_other,
        up_own,
        up_other,
        down_own,
        down_other,
    )
    if not summing:
        *grads, g_ln = totals
        chips = [grad[0].astype(f32) + swap_heads(grad[1]).astype(f32) for grad in grads]
        pieces = [lax.psum(chip.astype(bf16), "dp") for chip in chips]
        totals = (*pieces, lax.psum(g_ln, ("dp", "head")))
        y_other, gx_other = swap_heads(y_other), swap_heads(gx_other)
    return (y_own, y_other), (gx_own, gx_other), totals


RATES = (
    float(D) ** (-0.5),
    4.0 * float(D) ** (-0.5),
    float(D) ** (-0.5),
    float(FF) ** (-0.5),
    0.7,
)


def adam_step(gradient, weight, moment_one, moment_two, step_rate):
    first_new = beta_one * moment_one + (1.0 - beta_one) * gradient
    second_new = beta_two * moment_two + (1.0 - beta_two) * gradient * gradient
    first_hat = first_new * (1.0 / (1.0 - beta_one**STEP))
    second_hat = second_new * (1.0 / (1.0 - beta_two**STEP))
    weight_new = weight - step_rate * (
        first_hat / (jnp.sqrt(second_hat) + epsilon_adam) + decay_rate * weight
    )
    return (weight_new, first_new, second_new)


KINDS = (
    ((3 * D, HALF), 3, D),
    ((HALF, D), 1, HALF),
    ((D, FF // 2), 4, 128),
    ((FF // 2, D), 4, HALF),
)
BLOCK_LIST = [(kind, block) for kind in (3, 2, 1, 0) for block in range(KINDS[kind][1])]
STRIP = 32


def strip_gradient(kind, block, strip, pieces):
    def take(piece, part, start):
        rows = pl.ds(pl.multiple_of(start + strip * STRIP, STRIP), STRIP)
        return pieces[piece][part, rows, :].astype(f32)

    if kind == 1:
        return take(2, 0, 0)
    if kind == 2:
        start = 512 + block * 128
        return jnp.concatenate(
            [take(piece, part, start) for piece in range(2) for part in range(2)], axis=1
        )
    start = (block % 2) * HALF
    return jnp.concatenate([take(block // 2, part, start) for part in range(2)], axis=1)


def finish_step(owners, t_ln, ln, m_ln, v_ln, *refs):
    refs = list(refs)

    def some(count):
        taken, refs[:] = refs[:count], refs[count:]
        return taken

    pieces_at, weights_at, ones_at, twos_at = some(4), some(4), some(4), some(4)
    rows_at = some(4)
    owned_at, new_at, first_at, second_at, copy_at = [some(4) for _ in range(5)]
    y_at, gx_at = some(2)
    ln_owned, ln_new, ln_first, ln_second = some(4)
    pieces, weights, ones, twos, owned, copies = [some(4) for _ in range(6)]
    row_buffer, piece_sem, in_sem, out_sem, row_sem = some(5)
    head, chip = lax.axis_index("head"), lax.axis_index("dp")

    def block_copies(index, arrays, buffers, sems, back):
        kind, block = BLOCK_LIST[index]
        rows = pl.ds(block * KINDS[kind][2], KINDS[kind][2])
        result = []
        for which, (array, buffer) in enumerate(zip(arrays, buffers)):
            outside, inside = array[kind].at[rows], buffer[kind].at[rows]
            pair = (inside, outside) if back else (outside, inside)
            result.append(pltpu.make_async_copy(*pair, sems.at[index, which]))
        return result

    row_reads = [
        pltpu.make_async_copy(rows_at[index], row_buffer.at[index], row_sem.at[0, index])
        for index in range(4)
    ]
    row_writes = [
        pltpu.make_async_copy(
            row_buffer.at[index],
            (y_at, gx_at)[index // 2].at[pl.ds((head if index % 2 == 0 else 1 - head) * SEQ, SEQ)],
            row_sem.at[1, index],
        )
        for index in range(4)
    ]
    piece_copies = [
        pltpu.make_async_copy(pieces_at[index], pieces[index], piece_sem.at[index])
        for index in range(4)
    ]
    count = len(BLOCK_LIST)
    reads = [
        block_copies(index, (weights_at, ones_at, twos_at), (weights, ones, twos), in_sem, False)
        for index in range(count)
    ]
    writes = [
        block_copies(
            index,
            (owned_at, new_at, first_at, second_at, copy_at),
            (owned, weights, ones, twos, copies),
            out_sem,
            True,
        )
        for index in range(count)
    ]
    for copy in piece_copies + [copy for block in reads for copy in block]:
        copy.start()
    for copy in row_reads:
        copy.start()
    gradient = t_ln[...]
    results = adam_step(gradient, ln[...], m_ln[...], v_ln[...], RATES[4])
    ln_owned[...] = jnp.where(owners[4] == chip, gradient, 0.0)
    ln_new[...], ln_first[...], ln_second[...] = results
    for copy in piece_copies:
        copy.wait()
    for index, (kind, block) in enumerate(BLOCK_LIST):
        for copy in reads[index]:
            copy.wait()
        size = KINDS[kind][2]
        mine = owners[kind] == chip

        def update(rows, gradient, kind=kind, mine=mine):
            results = adam_step(
                gradient, weights[kind][rows], ones[kind][rows], twos[kind][rows], RATES[kind]
            )
            owned[kind][rows] = jnp.where(mine, gradient, 0.0)
            weights[kind][rows], ones[kind][rows], twos[kind][rows] = results
            copies[kind][rows] = results[0].astype(bf16)

        def strips(strip, carry, kind=kind, block=block, size=size, update=update):
            start = block * size + strip * STRIP
            if kind == 0:
                source = pl.ds(pl.multiple_of(block * HALF + strip * STRIP, STRIP), STRIP)
                for part in range(2):
                    rows = pl.ds(pl.multiple_of(start + part * HALF, STRIP), STRIP)
                    update(rows, pieces[3][part, source, :].astype(f32))
            else:
                rows = pl.ds(pl.multiple_of(start, STRIP), STRIP)
                update(rows, strip_gradient(kind, block, strip, pieces))
            return carry

        lax.fori_loop(0, (HALF if kind == 0 else size) // STRIP, strips, 0)
        for copy in writes[index]:
            copy.start()
    for read, write in zip(row_reads, row_writes):
        read.wait()
        write.start()
    for copy in row_writes + [copy for block in writes for copy in block]:
        copy.wait()


def update_all(owners, pieces, t_ln, ln_all, weights, ones, twos, rows):
    anywhere = pl.BlockSpec(memory_space=pl.ANY)
    vmem = pl.BlockSpec(memory_space=pltpu.VMEM)
    shapes = [kind[0] for kind in KINDS]
    whole = [shaped(shape, f32) for shape in shapes]
    buffers = [pltpu.VMEM(shape, f32) for shape in shapes]
    results = pl.pallas_call(
        finish_step,
        in_specs=[smem_spec] + [vmem] * 4 + [anywhere] * 20,
        out_specs=[anywhere] * 22 + [vmem] * 4,
        out_shape=whole * 4
        + [shaped(shape) for shape in shapes]
        + [shaped((2 * SEQ, HALF))] * 2
        + [shaped((4, D), f32)] * 4,
        scratch_shapes=[pltpu.VMEM(piece.shape, bf16) for piece in pieces]
        + buffers * 4
        + [pltpu.VMEM(shape, bf16) for shape in shapes]
        + [
            pltpu.VMEM((4, SEQ, HALF), bf16),
            pltpu.SemaphoreType.DMA((4,)),
            pltpu.SemaphoreType.DMA((len(BLOCK_LIST), 3)),
            pltpu.SemaphoreType.DMA((len(BLOCK_LIST), 5)),
            pltpu.SemaphoreType.DMA((2, 4)),
        ],
        compiler_params=limits,
        name="update_all",
    )(owners, t_ln, *ln_all, *pieces, *weights, *ones, *twos, *rows)
    return results[:20], results[20:22], results[22:]


def gather_inputs(tokens, cotangent, w_qkv, w_out, w_up, w_down):
    def both(array):
        return array, swap_heads(array)

    x_own, x_other = both(tokens)
    qkv_own = w_qkv.transpose(1, 0, 2).astype(bf16)
    out_own = w_out.astype(bf16)
    up_own = w_up.astype(bf16)
    down_own = w_down.astype(bf16)
    qkv_other = swap_heads(qkv_own)
    later, _, _ = lax.optimization_barrier((cotangent, x_other, qkv_other))
    dy_own, dy_other = cotangent, swap_heads(later)

    def swap_later(value):
        return swap_heads(lax.optimization_barrier((value, x_other, qkv_other))[0])

    weights = (
        qkv_own,
        qkv_other,
        out_own,
        swap_heads(out_own),
        up_own,
        swap_later(up_own),
        down_own,
        swap_later(down_own),
    )
    return x_own, x_other, dy_own, dy_other, weights


def body(
    tokens,
    cotangent,
    lengths,
    owners,
    w_qkv,
    w_out,
    w_up,
    w_down,
    ln_params,
    m_qkv,
    m_out,
    m_up,
    m_down,
    m_ln,
    v_qkv,
    v_out,
    v_up,
    v_down,
    v_ln,
):
    x_own, x_other, dy_own, dy_other, weights = gather_inputs(
        tokens, cotangent, w_qkv, w_out, w_up, w_down
    )
    y, gx, totals = layer_local(
        x_own, x_other, dy_own, dy_other, lengths, ln_params, weights
    )
    *pieces, t_ln = totals

    def as_rows(array):
        return array.transpose(1, 0, 2).reshape(3 * D, HALF)

    results, (output_rows, grad_input), ln_results = update_all(
        owners,
        pieces,
        t_ln,
        (ln_params, m_ln, v_ln),
        (as_rows(w_qkv), w_out, w_up, w_down),
        (as_rows(m_qkv), m_out, m_up, m_down),
        (as_rows(v_qkv), v_out, v_up, v_down),
        (*y, *gx),
    )
    groups = []
    for slot in range(5):
        group = list(results[slot * 4 : slot * 4 + 4])
        group[0] = group[0].reshape(3, D, HALF).transpose(1, 0, 2)
        if slot < 4:
            group.append(ln_results[slot])
        groups.append(tuple(group))
    owned = tuple(array[None] for array in groups[0])
    return (output_rows, grad_input) + owned + groups[1] + groups[2] + groups[3] + groups[4]


PLACED = (
    (P("dp", "head"),) * 2
    + (P("dp"), P())
    + (P(None, None, "head"), P("head", None), P(None, "head"), P("head", None), P()) * 3
)
RESULTS = (
    (P("dp", "head"),) * 2
    + (
        P("dp", None, None, "head"),
        P("dp", "head", None),
        P("dp", None, "head"),
        P("dp", "head", None),
        P("dp", None, None),
    )
    + (P(None, None, "head"), P("head", None), P(None, "head"), P("head", None), P()) * 3
    + (P(None, None, "head"), P("head", None), P(None, "head"), P("head", None))
)


def solution(mesh):
    return jax.shard_map(
        body, mesh=mesh, in_specs=PLACED, out_specs=RESULTS, check_vma=False
    )
```

```python
import functools

import jax
import jax.numpy as jnp
import numpy as np
from jax import lax
from jax.experimental import pallas as pl
from jax.experimental.pallas import tpu as pltpu
from jax.sharding import PartitionSpec as P

D = 512
HALF = 256
HEAD_DIM = 64
FF = 2048
SPAN = 128
SEQ = 2048
STEP = 5
ROWS = 16
PAIRS = 4
TILE = 512
TILES = SEQ // TILE
SPANS_TILE = TILE // SPAN

epsilon_norm = 1e-05
epsilon_adam = 1e-08
beta_one = 0.5
beta_two = 0.5
decay_rate = 0.1
masked_score = -1e30

bf16 = jnp.bfloat16
f32 = jnp.float32

NN = (((1,), (0,)), ((), ()))
NT = (((1,), (1,)), ((), ()))
TN = (((0,), (0,)), ((), ()))


def mm(left, right, dims=NN):
    return lax.dot_general(left, right, dims, preferred_element_type=f32)


def join_columns(head, own, other):
    low = jnp.where(head == 0, own, other)
    high = jnp.where(head == 0, other, own)
    return jnp.concatenate([low, high], axis=1)


def norm_stats(values):
    mean = jnp.mean(values, axis=1, keepdims=True)
    centered = values - mean
    rstd = lax.rsqrt(jnp.mean(centered * centered, axis=1, keepdims=True) + epsilon_norm)
    return centered * rstd, rstd


def head_stack(pair, low_lanes, high_lanes):
    return jnp.concatenate([pair * low_lanes, pair * high_lanes], axis=0)


def lane_masks(dtype):
    lane = lax.broadcasted_iota(jnp.int32, (1, 2 * HEAD_DIM), 1)
    low = (lane < HEAD_DIM).astype(f32)
    return low.astype(dtype), (1.0 - low).astype(dtype)


def pair_columns(pair):
    base = 3 * HALF * (pair // 2) + 2 * HEAD_DIM * (pair % 2)
    return base, base + HALF, base + 2 * HALF


def unstack_transposed(product):
    joined = jnp.concatenate(
        [product[:HEAD_DIM, :SPAN], product[HEAD_DIM:, SPAN:]], axis=0
    )
    return joined.T


def forward_attention(
    head_at, table, x_own, x_other, ln, w_own, w_other, causal, qkv, bars, probs, ctx, run_sum, normed
):
    head = lax.axis_index("head")
    step = pl.program_id(0)

    @pl.when(step == 0)
    def _():
        run_sum[...] = jnp.zeros_like(run_sum)

    for row in range(0, TILE, 128):
        rows = pl.ds(row, 128)
        x = join_columns(head, x_own[rows, :].astype(f32), x_other[rows, :].astype(f32))
        xhat, _ = norm_stats(x)
        normed[rows, :] = (xhat * ln[0:1, :] + ln[1:2, :]).astype(bf16)
    for side, w in enumerate((w_own, w_other)):
        for part in range(3):
            value = mm(normed[...], w[part])
            if part == 0:
                value = value * float(HEAD_DIM) ** (-0.5)
            base = side * 3 * HALF + part * HALF
            qkv[:, base : base + HALF] = value.astype(bf16)
    low_lanes, high_lanes = lane_masks(bf16)

    def score_span(span):
        rows = pl.ds(span * SPAN, SPAN)
        row_id = step * SPANS_TILE + span
        inverse = table[0, row_id]
        shift = table[1, row_id]
        scores, stacked = [], []
        for pair in range(PAIRS):
            at_q, at_k, at_v = pair_columns(pair)
            lanes = pl.ds(pair * 128, 128)
            lanes_v = pl.ds(512 + pair * 128, 128)
            key = qkv[rows, at_k : at_k + 128]
            value = qkv[rows, at_v : at_v + 128]
            key_bar = (run_sum[:, lanes] * inverse).astype(bf16)
            value_bar = (run_sum[:, lanes_v] * inverse).astype(bf16)
            run_sum[:, lanes] += key.astype(f32)
            run_sum[:, lanes_v] += value.astype(f32)
            bars[rows, lanes] = key_bar
            bars[rows, lanes_v] = value_bar
            query = head_stack(qkv[rows, at_q : at_q + 128], low_lanes, high_lanes)
            scores.append((mm(key, query, NT) + causal[...], mm(key_bar, query, NT) + shift))
            stacked.append(jnp.concatenate([value, value_bar], axis=0))
        return scores, stacked

    def soft_span(span, scores):
        expo = []
        for direct, summary in scores:
            top = jnp.maximum(
                jnp.max(direct, axis=0, keepdims=True), jnp.max(summary, axis=0, keepdims=True)
            )
            expo.append((jnp.exp(direct - top), jnp.exp(summary - top)))
        both = []
        for pair, (direct, summary) in enumerate(expo):
            total = jnp.sum(direct, axis=0, keepdims=True) + jnp.sum(
                summary, axis=0, keepdims=True
            )
            scale = 1.0 / total
            prob = jnp.concatenate(
                [(direct * scale).astype(bf16), (summary * scale).astype(bf16)], axis=0
            )
            probs[span * PAIRS + pair] = prob
            both.append(prob)
        return both

    def context_span(span, stacked, both):
        rows = pl.ds(span * SPAN, SPAN)
        for pair in range(PAIRS):
            lanes = pl.ds(pair * 128, 128)
            ctx[rows, lanes] = unstack_transposed(mm(stacked[pair], both[pair], TN)).astype(bf16)

    ready = score_span(0)
    for span in range(SPANS_TILE):
        scores, stacked = ready
        if span + 1 < SPANS_TILE:
            ready = score_span(span + 1)
        both = soft_span(span, scores)
        context_span(span, stacked, both)


def gelu_parts(u):
    share = lax.erf(u * 0.7071067811865476) * 0.5 + 0.5
    bell = jnp.exp2((u * u) * -0.7213475204444817)
    return u * share, share + u * bell * 0.3989422804014327


def swap_heads(value):
    return lax.ppermute(value, "head", [(0, 1), (1, 0)])


def chip_grid(count):
    side = 1 << ((count.bit_length() - 1) // 3)
    return (count // (side * side), side, side)


class Lines:
    def __init__(self, count):
        self.sizes = chip_grid(count)
        self.strides = (self.sizes[1] * self.sizes[2], self.sizes[2], 1)
        self.chip = lax.axis_index("dp")
        self.head = lax.axis_index("head")
        self.places = [
            lax.rem(self.chip // stride, size) for stride, size in zip(self.strides, self.sizes)
        ]
        self.members = [
            [self.find(axis, ahead) for ahead in range(1, size)]
            for axis, size in enumerate(self.sizes)
        ]

    def partner(self):
        return (self.chip, 1 - self.head)

    def member(self, axis, ahead):
        return self.members[axis][ahead - 1]

    def find(self, axis, ahead):
        size = self.sizes[axis]
        place = 1 - self.places[axis]
        if size > 2:
            place = lax.rem(self.places[axis] + ahead, size)
        chip = self.chip + (place - self.places[axis]) * self.strides[axis]
        return place, (chip, self.head)

    def greet(self):
        barrier = pltpu.get_barrier_semaphore()
        others = [self.partner()]
        for axis in range(3):
            others += [self.member(axis, ahead)[1] for ahead in range(1, self.sizes[axis])]
        for other in others:
            pl.semaphore_signal(
                barrier, inc=1, device_id=other, device_id_type=pl.DeviceIdType.MESH
            )
        pl.semaphore_wait(barrier, len(others))


X_FIRST, Y_FIRST = (2, 1, 0), (1, 2, 0)


def whole_slices(count):
    return all(shape[1] % (16 * count) == 0 for shape, _ in PIECES)


def chunk_rows(rows):
    return next(chunk for chunk in (128, 96, 64, 48, 32, 16) if rows % chunk == 0)


def sum_scratch(shape, orders, count):
    parts, rows, lanes = shape
    sizes = chip_grid(count)
    shapes = [pltpu.VMEM(shape, bf16)]
    sems = [pltpu.SemaphoreType.DMA((3,))]
    for order in orders:
        left = rows
        for axis in order:
            left //= sizes[axis]
            shapes.append(pltpu.VMEM((sizes[axis] - 1, left, lanes), bf16))
            sems.append(pltpu.SemaphoreType.DMA((2, 2, sizes[axis] - 1)))
    return shapes + sems


class DpSum:
    def __init__(self, lines, orders, grads, total, scratch):
        self.lines = lines
        self.orders = orders
        self.parts = range(len(orders))
        self.grads = grads
        self.total = total
        self.rows = grads.shape[2]
        self.work, self.final = grads.at[0], scratch.pop(0)
        self.slots = [[scratch.pop(0) for _ in order] for order in orders]
        self.core_sem = scratch.pop(0)
        self.sems = [[scratch.pop(0) for _ in order] for order in orders]
        self.base = []
        for order in orders:
            bases, piece = [0], self.rows
            for axis in order:
                piece //= lines.sizes[axis]
                bases.append(bases[-1] + lines.places[axis] * piece)
            self.base.append(bases)

    def remote(self, source, target, send_sem, recv_sem, device):
        return pltpu.make_async_remote_copy(
            src_ref=source,
            dst_ref=target,
            send_sem=send_sem,
            recv_sem=recv_sem,
            device_id=device,
            device_id_type=pl.DeviceIdType.MESH,
        )

    def core_copy(self):
        return self.remote(
            self.grads.at[1],
            self.final,
            self.core_sem.at[0],
            self.core_sem.at[1],
            self.lines.partner(),
        )

    def core_send(self):
        self.core_copy().start()

    def core_sum(self):
        self.core_copy().wait()
        chunk = chunk_rows(self.rows)
        for part in self.parts:

            def add(index, carry, part=part):
                rows = pl.ds(pl.multiple_of(index * chunk, chunk), chunk)
                self.work[part, rows, :] = self.work[part, rows, :] + self.final[part, rows, :]
                return carry

            lax.fori_loop(0, self.rows // chunk, add, 0)

    def spread_copies(self, part, stage):
        axis = self.orders[part][stage]
        size = self.lines.sizes[axis]
        base = self.base[part][stage]
        piece = self.rows
        for at in self.orders[part][: stage + 1]:
            piece //= self.lines.sizes[at]
        copies = []
        for ahead in range(1, size):
            place, device = self.lines.member(axis, ahead)
            start = pl.multiple_of(base + place * piece, 16)
            copies.append(
                self.remote(
                    self.work.at[part, pl.ds(start, piece)],
                    self.slots[part][stage].at[ahead - 1],
                    self.sems[part][stage].at[0, 0, ahead - 1],
                    self.sems[part][stage].at[0, 1, ahead - 1],
                    device,
                )
            )
        return copies, self.base[part][stage + 1], piece

    def spread_send(self, part, stage):
        for copy in self.spread_copies(part, stage)[0]:
            copy.start()

    def spread_sum(self, part, stage):
        copies, mine, piece = self.spread_copies(part, stage)
        for copy in copies:
            copy.wait()
        slots = self.slots[part][stage]
        target = self.final if stage == 2 else self.work
        chunk = chunk_rows(piece)

        def add(index, carry):
            offset = pl.multiple_of(index * chunk, chunk)
            rows = pl.ds(pl.multiple_of(mine + offset, 16), chunk)
            value = self.work[part, rows, :]
            if len(copies) > 1:
                value = value.astype(f32)
            for slot in range(len(copies)):
                value = value + slots[slot, pl.ds(offset, chunk), :].astype(value.dtype)
            target[part, rows, :] = value.astype(bf16)
            return carry

        lax.fori_loop(0, piece // chunk, add, 0)

    def gather_copies(self, part, stage):
        axis = self.orders[part][stage]
        size = self.lines.sizes[axis]
        piece = self.rows
        for at in self.orders[part][: stage + 1]:
            piece //= self.lines.sizes[at]
        mine = pl.multiple_of(self.base[part][stage + 1], 16)
        rows = pl.ds(mine, piece)
        copies = []
        for ahead in range(1, size):
            _, device = self.lines.member(axis, ahead)
            copies.append(
                self.remote(
                    self.final.at[part, rows],
                    self.final.at[part, rows],
                    self.sems[part][stage].at[1, 0, ahead - 1],
                    self.sems[part][stage].at[1, 1, ahead - 1],
                    device,
                )
            )
        return copies

    def gather_send(self, part, stage):
        for copy in self.gather_copies(part, stage):
            copy.start()

    def gather_wait(self, part, stage):
        for copy in self.gather_copies(part, stage):
            copy.wait()

    def store_copy(self):
        return pltpu.make_async_copy(self.final, self.total, self.core_sem.at[2])

    def event(self, index):
        if index == 0:
            self.core_send()
        elif index == 1:
            self.core_sum()
        for part in self.parts:
            if 2 <= index <= 4:
                self.spread_sum(part, index - 2)
            elif index >= 5:
                self.gather_wait(part, 7 - index)
            if 1 <= index <= 3:
                self.spread_send(part, index - 1)
            elif 4 <= index <= 6:
                self.gather_send(part, 6 - index)
        if index == 7:
            self.store_copy().start()

    def finish(self):
        self.store_copy().wait()


EVENTS = 8


def ln_scratch(count):
    return [
        pltpu.VMEM((2, 4, D), f32),
        pltpu.SemaphoreType.DMA((2,)),
        *[pltpu.VMEM((size, 4, D), f32) for size in chip_grid(count)],
        *[pltpu.SemaphoreType.DMA((2, max(size - 1, 1))) for size in chip_grid(count)],
    ]


class LnSum:
    def __init__(self, lines, value, total, scratch):
        self.lines = lines
        self.value = value
        self.total = total
        self.core, self.core_sem = scratch[:2]
        self.slots = scratch[2:5]
        self.sems = scratch[5:8]

    def stage_copies(self, stage):
        lines = self.lines
        if stage == 0:
            mine = self.core.at[lines.head]
            return [
                pltpu.make_async_remote_copy(
                    src_ref=mine,
                    dst_ref=mine,
                    send_sem=self.core_sem.at[0],
                    recv_sem=self.core_sem.at[1],
                    device_id=lines.partner(),
                    device_id_type=pl.DeviceIdType.MESH,
                )
            ]
        axis = stage - 1
        mine = self.slots[axis].at[lines.places[axis]]
        return [
            pltpu.make_async_remote_copy(
                src_ref=mine,
                dst_ref=mine,
                send_sem=self.sems[axis].at[0, ahead - 1],
                recv_sem=self.sems[axis].at[1, ahead - 1],
                device_id=lines.member(axis, ahead)[1],
                device_id_type=pl.DeviceIdType.MESH,
            )
            for ahead in range(1, lines.sizes[axis])
        ]

    def send(self, stage):
        if stage == 0:
            self.core[self.lines.head] = self.value[...]
        for copy in self.stage_copies(stage):
            copy.start()

    def finish(self, stage):
        for copy in self.stage_copies(stage):
            copy.wait()
        slots = self.core if stage == 0 else self.slots[stage - 1]
        value = slots[0]
        for slot in range(1, slots.shape[0]):
            value = value + slots[slot]
        if stage == 3:
            self.total[...] = value
        else:
            self.slots[stage][self.lines.places[stage]] = value


PIECES = (
    ((2, 1024, HALF), (X_FIRST, Y_FIRST)),
    ((2, 1024, HALF), (X_FIRST, Y_FIRST)),
    ((1, HALF, D), (Y_FIRST,)),
    ((2, 3 * HALF, HALF), (X_FIRST, Y_FIRST)),
)
CHUNKS = FF // 512
CHUNK_STEP = TILES
POST_STEP = CHUNK_STEP + CHUNKS
ATT_STEP = POST_STEP + TILES
SPANS_STEP = 2
ATT_STEPS = ROWS // SPANS_STEP
LAST_STEP = ATT_STEP + ATT_STEPS
STEPS = LAST_STEP + TILES
EVENT_AT = (
    ((6, 0), (6, 1), (7, 1), (8, 0), (12, 0), (15, 0), (17, 0), (19, 0),),
    ((8, 0), (9, 0), (13, 0), (16, 0), (19, 0),),
    ((14, 0), (16, 0), (18, 0),),
    ((20, 0), (22, 0),),
)


def mlp_and_back(
    count,
    table,
    lengths,
    ln,
    x_own_at,
    x_other_at,
    dy_own_at,
    dy_other_at,
    ctx_at,
    qkv_at,
    bars_at,
    probs_at,
    out_own_at,
    out_other_at,
    w_own_at,
    w_other_at,
    up_own,
    up_other,
    down_own,
    down_other,
    y_own_at,
    y_other_at,
    gx_own_at,
    gx_other_at,
    *refs,
):
    summing = whole_slices(count)
    kinds = len(PIECES)
    totals, ln_total = refs[:kinds], refs[kinds]
    (x_own, x_other, dy_own, dy_other, ctx, qkv_two, bars_two, probs_two, out_own, out_other,
     w_own, w_other, up_all, down_all, load_sem, weight_sem, block_sem, store_sem, res, grad_qkv,
     normed_t, gm, mlp, grad_n, acc_one, acc_two, hid, grad_hid, after,
     acc_ln) = refs[kinds + 1 : kinds + 31]
    grads = refs[kinds + 31 : kinds + 31 + len(PIECES)]
    scratch = list(refs[kinds + 31 + len(PIECES) :])
    head = lax.axis_index("head")
    used = lengths[head]
    sums = []
    if summing:
        lines = Lines(count)
        for (_, orders), grad, total in zip(PIECES, grads, totals):
            sums.append(DpSum(lines, orders, grad, total, scratch))
        small = LnSum(lines, acc_ln, ln_total, scratch)

    def run_events(events):
        for index, event in events:
            sums[index].event(event)

    def hook(step, first, end, place=0):
        for at in range(first, end if summing else 0):
            events = [
                (index, event)
                for index, times in enumerate(EVENT_AT)
                for event, time in enumerate(times)
                if time == (at, place)
            ]
            if events:

                @pl.when(step == at)
                def _(events=events):
                    run_events(events)

    mine = pl.ds(head * SEQ, SEQ)
    loads = [
        pltpu.make_async_copy(source, target, load_sem.at[index])
        for index, (source, target) in enumerate(
            (
                (ctx_at, ctx),
                (out_own_at, out_own),
                (out_other_at, out_other),
                (x_own_at.at[mine], x_own),
                (x_other_at.at[mine], x_other),
                (dy_own_at.at[mine], dy_own),
                (dy_other_at.at[mine], dy_other),
                (w_own_at, w_own),
                (w_other_at, w_other),
            )
        )
    ]
    weight_copies = []
    for chunk in range(CHUNKS):
        up_w, down_w = ((up_own, down_own), (up_other, down_other))[chunk % 2]
        cut = pl.ds(chunk // 2 * 512, 512)
        pairs = ((up_w.at[:, cut], up_all.at[chunk]), (down_w.at[cut], down_all.at[chunk]))
        for which, (source, target) in enumerate(pairs):
            sem = weight_sem.at[2 * chunk + which]
            weight_copies.append(pltpu.make_async_copy(source, target, sem))
    block_rows = SPANS_STEP * SPAN
    block_probs = SPANS_STEP * PAIRS

    def block_copies(index):
        block = ATT_STEPS - 1 - index
        slot = lax.rem(index, 2)
        rows = pl.ds(block * block_rows, block_rows)
        many = pl.ds(block * block_probs, block_probs)
        pairs = (
            (qkv_at.at[rows], qkv_two.at[slot]),
            (bars_at.at[rows], bars_two.at[slot]),
            (probs_at.at[many], probs_two.at[slot]),
        )
        return [
            pltpu.make_async_copy(source, target, block_sem.at[slot, which])
            for which, (source, target) in enumerate(pairs)
        ]

    stores = []
    for index, (source, target) in enumerate(
        (
            (ctx.at[:, pl.ds(0, HALF)], y_own_at),
            (ctx.at[:, pl.ds(HALF, HALF)], y_other_at),
            (dy_own, gx_own_at),
            (dy_other, gx_other_at),
        )
    ):
        if summing and index % 2 == 1:
            stores.append(
                pltpu.make_async_remote_copy(
                    src_ref=source,
                    dst_ref=target,
                    send_sem=store_sem.at[index],
                    recv_sem=store_sem.at[4 + index // 2],
                    device_id=lines.partner(),
                    device_id_type=pl.DeviceIdType.MESH,
                )
            )
        else:
            stores.append(pltpu.make_async_copy(source, target, store_sem.at[index]))

    def x_rows(rows):
        return join_columns(head, x_own[rows, :].astype(f32), x_other[rows, :].astype(f32))

    def dy_rows(rows):
        return join_columns(head, dy_own[rows, :].astype(f32), dy_other[rows, :].astype(f32))

    def valid_rows(first):
        ids = lax.broadcasted_iota(jnp.int32, (128, 1), 0) + first
        return (ids < used).astype(f32)

    def before_mlp(tile, carry):
        base = tile * TILE
        tokens = pl.ds(pl.multiple_of(base, TILE), TILE)
        res[tokens, :] = mm(ctx[tokens, :HALF], out_own[...]) + mm(
            ctx[tokens, HALF:], out_other[...]
        )
        mlp[tokens, :] = jnp.zeros((TILE, D), f32)
        grad_n[tokens, :] = jnp.zeros((TILE, D), f32)
        for row in range(0, TILE, 128):
            at = pl.ds(pl.multiple_of(base + row, 128), 128)
            valid = valid_rows(base + row)
            h = x_rows(at) + valid * res[at, :]
            res[at, :] = h
            hat, _ = norm_stats(h)
            n2 = (hat * ln[2:3, :] + ln[3:4, :]).astype(bf16)
            grad_qkv[at, :D] = n2
            normed_t[:, at] = n2.T
            gm[at, :] = (valid * dy_rows(at)).astype(bf16)
        return carry

    def chunk_in(chunk, tile):
        tokens = pl.ds(tile * TILE, TILE)
        hid[tile % 2] = mm(grad_qkv[tokens, :D], up_all[chunk])
        grad_hid[tile % 2] = mm(gm[tokens, :], down_all[chunk], NT)

    def act_rows(tile, row, size):
        return pl.ds(tile % 2 * TILE + row, size), pl.ds((2 + tile % 2) * TILE + row, size)

    def chunk_mid(tile):
        slot = tile % 2
        for row in range(0, TILE, 16):
            rows = pl.ds(row, 16)
            a, da = gelu_parts(hid[slot, rows, :])
            at_act, at_gu = act_rows(tile, row, 16)
            grad_qkv[at_act, D : 2 * D] = a.astype(bf16)
            grad_qkv[at_gu, D : 2 * D] = (grad_hid[slot, rows, :] * da).astype(bf16)

    def chunk_out(chunk, tile):
        tokens = pl.ds(tile * TILE, TILE)
        at_act, at_gu = act_rows(tile, 0, TILE)
        act = grad_qkv[at_act, D : 2 * D]
        gu = grad_qkv[at_gu, D : 2 * D]
        mlp[tokens, :] += mm(act, down_all[chunk])
        grad_n[tokens, :] += mm(gu, up_all[chunk], NT)
        part_down = mm(act, gm[tokens, :], TN)
        part_up = mm(normed_t[:, tokens], gu)
        if tile == 0:
            acc_one[...] = part_down
            acc_two[...] = part_up
        else:
            acc_one[...] += part_down
            acc_two[...] += part_up

    def chunk_tiles(chunk, first):
        chunk_in(chunk, first)
        chunk_in(chunk, first + 1)
        chunk_mid(first)
        chunk_out(chunk, first)
        chunk_mid(first + 1)
        chunk_out(chunk, first + 1)

    def hidden_chunk(chunk, carry):
        step = CHUNK_STEP + chunk
        hook(step, CHUNK_STEP, POST_STEP)
        chunk_tiles(chunk, 0)
        hook(step, CHUNK_STEP, POST_STEP, 1)
        chunk_tiles(chunk, 2)
        side = lax.rem(chunk, 2)

        for half in range(2):

            @pl.when(chunk // 2 == half)
            def _(half=half):
                for part in range(2):
                    lanes = slice(part * HALF, (part + 1) * HALF)
                    grads[half][side, part, :512] = acc_one[:, lanes].astype(bf16)
                    grads[half][side, part, 512:] = acc_two[:, lanes].astype(bf16)

        return carry

    def after_mlp(tile, carry):
        hook(POST_STEP + tile, POST_STEP, ATT_STEP)
        base = tile * TILE
        tokens = pl.ds(pl.multiple_of(base, TILE), TILE)
        for row in range(0, TILE, 128):
            at = pl.ds(pl.multiple_of(base + row, 128), 128)
            valid = valid_rows(base + row)
            h = res[at, :]
            mlp[at, :] = h + valid * mlp[at, :]
            gn = grad_n[at, :]
            hat, rstd = norm_stats(h)
            acc_ln[2:3, :] += jnp.sum(gn * hat, axis=0, keepdims=True)
            acc_ln[3:4, :] += jnp.sum(gn, axis=0, keepdims=True)
            scaled = gn * ln[2:3, :]
            back = rstd * (
                scaled
                - jnp.mean(scaled, axis=1, keepdims=True)
                - hat * jnp.mean(scaled * hat, axis=1, keepdims=True)
            )
            gh = dy_rows(at) + back
            res[at, :] = gh
            gm[at, :] = (valid * gh).astype(bf16)
        ga = gm[tokens, :]
        acc_one[...] += mm(ctx[tokens, :], ga, TN)
        low, high = mlp[tokens, :HALF], mlp[tokens, HALF:]
        ctx[tokens, :HALF] = jnp.where(head == 0, low, high).astype(bf16)
        ctx[tokens, HALF:] = jnp.where(head == 0, high, low).astype(bf16)
        grad_low = mm(ga, out_own[...], NT)
        grad_high = mm(ga, out_other[...], NT)
        gm[tokens, :HALF] = grad_low.astype(bf16)
        gm[tokens, HALF:] = grad_high.astype(bf16)
        return carry

    low_lanes, high_lanes = lane_masks(bf16)
    scale_factor = float(HEAD_DIM) ** (-0.5)

    def span_tokens(block, span):
        return pl.ds(pl.multiple_of(block * block_rows + span * SPAN, SPAN), SPAN)

    def attention_in(block, qkv, bars, span):
        rows = pl.ds(span * SPAN, SPAN)
        held = []
        for pair in range(PAIRS):
            _, _, at_v = pair_columns(pair)
            lanes = pl.ds(pair * 128, 128)
            lanes_v = pl.ds(512 + pair * 128, 128)
            values = jnp.concatenate([qkv[rows, at_v : at_v + 128], bars[rows, lanes_v]], axis=0)
            grad = head_stack(gm[span_tokens(block, span), lanes], low_lanes, high_lanes)
            held.append((grad, mm(values, grad, NT)))
        return held

    def attention_mid(probs, span, held):
        scores = []
        for pair in range(PAIRS):
            prob_f = probs[span * PAIRS + pair].astype(f32)
            weighted = held[pair][1] * prob_f
            delta = jnp.sum(weighted, axis=0, keepdims=True)
            scores.append((weighted - prob_f * delta).astype(bf16))
        return scores

    def attention_out(block, qkv, bars, probs, span, held, scores):
        rows = pl.ds(span * SPAN, SPAN)
        tokens = span_tokens(block, span)
        inverse = table[0, block * SPANS_STEP + span]
        for pair in range(PAIRS):
            at_q, at_k, at_v = pair_columns(pair)
            lanes = pl.ds(pair * 128, 128)
            lanes_v = pl.ds(512 + pair * 128, 128)
            keys = jnp.concatenate([qkv[rows, at_k : at_k + 128], bars[rows, lanes]], axis=0)
            query = head_stack(qkv[rows, at_q : at_q + 128], low_lanes, high_lanes)
            grad_q = unstack_transposed(mm(keys, scores[pair], TN)) * scale_factor
            grad_k = mm(scores[pair], query)
            grad_v = mm(probs[span * PAIRS + pair], held[pair][0])
            grad_qkv[tokens, at_q : at_q + 128] = grad_q.astype(bf16)
            grad_qkv[tokens, at_k : at_k + 128] = (grad_k[:SPAN] + after[:, lanes]).astype(bf16)
            grad_qkv[tokens, at_v : at_v + 128] = (grad_v[:SPAN] + after[:, lanes_v]).astype(bf16)
            after[:, lanes] += grad_k[SPAN:] * inverse
            after[:, lanes_v] += grad_v[SPAN:] * inverse

    def attention_block(index, carry):
        block = ATT_STEPS - 1 - index
        slot = lax.rem(index, 2)
        hook(ATT_STEP + index, ATT_STEP, LAST_STEP)
        for copy in block_copies(index):
            copy.wait()
        qkv, bars, probs = qkv_two.at[slot], bars_two.at[slot], probs_two.at[slot]
        for row in range(0, block_rows, 128):
            rows = pl.ds(pl.multiple_of(block * block_rows + row, 128), 128)
            hat, _ = norm_stats(x_rows(rows))
            normed_t[:, row : row + 128] = (hat * ln[0:1, :] + ln[1:2, :]).astype(bf16).T
        held_one = attention_in(block, qkv, bars, 1)
        held_two = attention_in(block, qkv, bars, 0)
        scores = attention_mid(probs, 1, held_one)
        attention_out(block, qkv, bars, probs, 1, held_one, scores)
        scores = attention_mid(probs, 0, held_two)
        attention_out(block, qkv, bars, probs, 0, held_two, scores)
        tokens = pl.ds(pl.multiple_of(block * block_rows, block_rows), block_rows)
        for side in range(2):
            for part in range(3):
                at = side * 3 * HALF + part * HALF
                rows = slice(part * D, (part + 1) * D)
                lanes = slice(side * HALF, (side + 1) * HALF)
                mlp[rows, lanes] += mm(
                    normed_t[:, :block_rows], grad_qkv[tokens, at : at + HALF]
                )


        @pl.when(index + 2 < ATT_STEPS)
        def _():
            for copy in block_copies(index + 2):
                copy.start()

        return carry

    def first_norm(tile, carry):
        hook(LAST_STEP + tile, LAST_STEP, STEPS)
        base = tile * TILE
        tokens = pl.ds(pl.multiple_of(base, TILE), TILE)
        for side, w in enumerate((w_own, w_other)):
            for part in range(3):
                at = side * 3 * HALF + part * HALF
                back = mm(grad_qkv[tokens, at : at + HALF], w[part], NT)
                if side == 0 and part == 0:
                    grad_n[:TILE, :] = back
                else:
                    grad_n[:TILE, :] += back
        for row in range(0, TILE, 128):
            at = pl.ds(pl.multiple_of(base + row, 128), 128)
            hat, rstd = norm_stats(x_rows(at))
            gn = grad_n[row : row + 128, :]
            acc_ln[0:1, :] += jnp.sum(gn * hat, axis=0, keepdims=True)
            acc_ln[1:2, :] += jnp.sum(gn, axis=0, keepdims=True)
            scaled = gn * ln[0:1, :]
            back = rstd * (
                scaled
                - jnp.mean(scaled, axis=1, keepdims=True)
                - hat * jnp.mean(scaled * hat, axis=1, keepdims=True)
            )
            gx = res[at, :] + back
            low, high = gx[:, :HALF], gx[:, HALF:]
            dy_own[at, :] = jnp.where(head == 0, low, high).astype(bf16)
            dy_other[at, :] = jnp.where(head == 0, high, low).astype(bf16)
        return carry

    for copy in loads + weight_copies + block_copies(0) + block_copies(1):
        copy.start()
    if summing:
        lines.greet()
    after[...] = jnp.zeros_like(after)
    acc_ln[...] = jnp.zeros_like(acc_ln)
    for copy in loads:
        copy.wait()
    lax.fori_loop(0, TILES, before_mlp, 0)
    for copy in weight_copies:
        copy.wait()
    lax.fori_loop(0, CHUNKS, hidden_chunk, 0)
    acc_one[...] = jnp.zeros_like(acc_one)
    lax.fori_loop(0, TILES, after_mlp, 0)
    for copy in stores[:2]:
        copy.start()
    for side in range(2):
        grads[2][side, 0] = acc_one[side * HALF : (side + 1) * HALF, :].astype(bf16)
    mlp[...] = jnp.zeros_like(mlp)
    lax.fori_loop(0, ATT_STEPS, attention_block, 0)
    for side in range(2):
        for part in range(2):
            for kind in range(3):
                rows = slice(kind * HALF, (kind + 1) * HALF)
                source = slice(kind * D + part * HALF, kind * D + (part + 1) * HALF)
                lanes = slice(side * HALF, (side + 1) * HALF)
                grads[3][side, part, rows] = mlp[source, lanes].astype(bf16)
    lax.fori_loop(0, TILES, first_norm, 0)
    for copy in stores[2:]:
        copy.start()
    if summing:
        small.send(0)
        for index in range(EVENTS):
            left = [
                (which, len(times) + index)
                for which, times in enumerate(EVENT_AT)
                if len(times) + index < EVENTS
            ]
            run_events(left[::-1])
            if index <= 3:
                small.finish(index)
            if index < 3:
                small.send(index + 1)
        for entry in sums:
            entry.finish()
    else:
        for total, grad in zip(totals, grads):
            total[...] = grad[...]
        ln_total[...] = acc_ln[...]
    for copy in stores:
        copy.wait()


def rows_spec(width):
    return pl.BlockSpec((TILE, width), lambda i, *_: (i, 0))


def whole_spec(shape):
    rank = len(shape)
    return pl.BlockSpec(shape, lambda i, *_: (0,) * rank, pipeline_mode=pl.Buffered(1))


def shaped(shape, dtype=bf16):
    return jax.ShapeDtypeStruct(shape, dtype)


smem_spec = pl.BlockSpec(memory_space=pltpu.SMEM)
limits = pltpu.CompilerParams(vmem_limit_bytes=60 * 1024 * 1024)


def span_table():
    ids = np.arange(ROWS)
    inverse = 1.0 / np.maximum(ids, 1)
    shift = np.where(ids >= 1, np.log(np.maximum(ids, 1)), masked_score)
    return jnp.asarray(np.stack([inverse, shift]).astype(np.float32))


def causal_bias():
    key = np.arange(SPAN)[:, None]
    query = np.arange(2 * SPAN)[None, :] % SPAN
    return jnp.asarray(np.where(key <= query, 0.0, masked_score).astype(np.float32))


def layer_local(x_own, x_other, dy_own, dy_other, lengths, ln_params, weights):
    qkv_own, qkv_other, out_own, out_other, up_own, up_other, down_own, down_other = weights
    table = span_table()
    qkv, bars, probs, ctx = pl.pallas_call(
        forward_attention,
        grid_spec=pltpu.PrefetchScalarGridSpec(
        num_scalar_prefetch=1,
        grid=(TILES,),
        in_specs=[
            smem_spec,
            pl.BlockSpec((TILE, HALF), lambda i, head: (head[0] * TILES + i, 0)),
            pl.BlockSpec((TILE, HALF), lambda i, head: (head[0] * TILES + i, 0)),
            whole_spec((4, D)),
            whole_spec((3, D, HALF)),
            whole_spec((3, D, HALF)),
            whole_spec((SPAN, 2 * SPAN)),
        ],
        out_specs=[
            rows_spec(3 * D),
            rows_spec(2 * D),
            pl.BlockSpec((SPANS_TILE * PAIRS, 2 * SPAN, 2 * SPAN), lambda i, head: (i, 0, 0)),
            rows_spec(D),
        ],
        scratch_shapes=[pltpu.VMEM((SPAN, 2 * D), f32), pltpu.VMEM((TILE, D), bf16)],
        ),
        out_shape=[
            shaped((SEQ, 3 * D)),
            shaped((SEQ, 2 * D)),
            shaped((ROWS * PAIRS, 2 * SPAN, 2 * SPAN)),
            shaped((SEQ, D)),
        ],
        compiler_params=limits,
        name="forward_attention",
    )(lax.axis_index("head").reshape(1), table, x_own, x_other, ln_params, qkv_own, qkv_other, causal_bias())
    count = lax.axis_size("dp")
    summing = whole_slices(count)
    sum_buffers, extra, total_specs, total_shapes = [], {}, [], []
    anywhere = pl.BlockSpec(memory_space=pl.ANY)
    if summing:
        for shape, orders in PIECES:
            sum_buffers += sum_scratch(shape, orders, count)
            total_specs.append(anywhere)
            total_shapes.append(shaped(shape))
        sum_buffers += ln_scratch(count)
        extra = dict(collective_id=0, has_side_effects=True)
    else:
        for shape, _ in PIECES:
            total_specs.append(pl.BlockSpec(memory_space=pltpu.VMEM))
            total_shapes.append(shaped((2, *shape)))
    block_rows = SPANS_STEP * SPAN
    vmem = pl.BlockSpec(memory_space=pltpu.VMEM)
    y_own, y_other, gx_own, gx_other, *totals = pl.pallas_call(
        functools.partial(mlp_and_back, count),
        in_specs=[smem_spec, smem_spec, vmem] + [anywhere] * 16,
        out_specs=[anywhere] * 4 + total_specs + [vmem],
        out_shape=[shaped((SEQ, HALF))] * 4 + total_shapes + [shaped((4, D), f32)],
        scratch_shapes=[
            pltpu.VMEM((SEQ, HALF), bf16),
            pltpu.VMEM((SEQ, HALF), bf16),
            pltpu.VMEM((SEQ, HALF), bf16),
            pltpu.VMEM((SEQ, HALF), bf16),
            pltpu.VMEM((SEQ, D), bf16),
            pltpu.VMEM((2, block_rows, 3 * D), bf16),
            pltpu.VMEM((2, block_rows, 2 * D), bf16),
            pltpu.VMEM((2, SPANS_STEP * PAIRS, 2 * SPAN, 2 * SPAN), bf16),
            pltpu.VMEM((HALF, D), bf16),
            pltpu.VMEM((HALF, D), bf16),
            pltpu.VMEM((3, D, HALF), bf16),
            pltpu.VMEM((3, D, HALF), bf16),
            pltpu.VMEM((CHUNKS, D, 512), bf16),
            pltpu.VMEM((CHUNKS, 512, D), bf16),
            pltpu.SemaphoreType.DMA((9,)),
            pltpu.SemaphoreType.DMA((2 * CHUNKS,)),
            pltpu.SemaphoreType.DMA((2, 3)),
            pltpu.SemaphoreType.DMA((6,)),
            pltpu.VMEM((SEQ, D), f32),
            pltpu.VMEM((SEQ, 3 * D), bf16),
            pltpu.VMEM((D, SEQ), bf16),
            pltpu.VMEM((SEQ, D), bf16),
            pltpu.VMEM((SEQ, D), f32),
            pltpu.VMEM((SEQ, D), f32),
            pltpu.VMEM((512, D), f32),
            pltpu.VMEM((D, 512), f32),
            pltpu.VMEM((2, TILE, 512), f32),
            pltpu.VMEM((2, TILE, 512), f32),
            pltpu.VMEM((SPAN, 2 * D), f32),
            pltpu.VMEM((4, D), f32),
        ]
        + [pltpu.VMEM((2, *shape), bf16) for shape, _ in PIECES]
        + sum_buffers,
        compiler_params=pltpu.CompilerParams(vmem_limit_bytes=63 * 1024 * 1024, **extra),
        name="mlp_and_back",
    )(
        table,
        lengths,
        ln_params,
        x_own,
        x_other,
        dy_own,
        dy_other,
        ctx,
        qkv,
        bars,
        probs,
        out_own,
        out_other,
        qkv_own,
        qkv_other,
        up_own,
        up_other,
        down_own,
        down_other,
    )
    if not summing:
        *grads, g_ln = totals
        chips = [grad[0].astype(f32) + swap_heads(grad[1]).astype(f32) for grad in grads]
        pieces = [lax.psum(chip.astype(bf16), "dp") for chip in chips]
        totals = (*pieces, lax.psum(g_ln, ("dp", "head")))
        y_other, gx_other = swap_heads(y_other), swap_heads(gx_other)
    return (y_own, y_other), (gx_own, gx_other), totals


RATES = (
    float(D) ** (-0.5),
    4.0 * float(D) ** (-0.5),
    float(D) ** (-0.5),
    float(FF) ** (-0.5),
    0.7,
)


def adam_step(gradient, weight, moment_one, moment_two, step_rate):
    first_new = beta_one * moment_one + (1.0 - beta_one) * gradient
    second_new = beta_two * moment_two + (1.0 - beta_two) * gradient * gradient
    first_hat = first_new * (1.0 / (1.0 - beta_one**STEP))
    second_hat = second_new * (1.0 / (1.0 - beta_two**STEP))
    weight_new = weight - step_rate * (
        first_hat / (jnp.sqrt(second_hat) + epsilon_adam) + decay_rate * weight
    )
    return (weight_new, first_new, second_new)


KINDS = (
    ((3 * D, HALF), 3, D),
    ((HALF, D), 1, HALF),
    ((D, FF // 2), 4, 128),
    ((FF // 2, D), 4, HALF),
)
BLOCK_LIST = [(kind, block) for kind in (3, 2, 1, 0) for block in range(KINDS[kind][1])]
STRIP = 32


def strip_gradient(kind, block, strip, pieces):
    def take(piece, part, start):
        rows = pl.ds(pl.multiple_of(start + strip * STRIP, STRIP), STRIP)
        return pieces[piece][part, rows, :].astype(f32)

    if kind == 1:
        return take(2, 0, 0)
    if kind == 2:
        start = 512 + block * 128
        return jnp.concatenate(
            [take(piece, part, start) for piece in range(2) for part in range(2)], axis=1
        )
    start = (block % 2) * HALF
    return jnp.concatenate([take(block // 2, part, start) for part in range(2)], axis=1)


def finish_step(owners, t_ln, ln, m_ln, v_ln, *refs):
    refs = list(refs)

    def some(count):
        taken, refs[:] = refs[:count], refs[count:]
        return taken

    pieces_at, weights_at, ones_at, twos_at = some(4), some(4), some(4), some(4)
    rows_at = some(4)
    owned_at, new_at, first_at, second_at, copy_at = [some(4) for _ in range(5)]
    y_at, gx_at = some(2)
    ln_owned, ln_new, ln_first, ln_second = some(4)
    pieces, weights, ones, twos, owned, copies = [some(4) for _ in range(6)]
    row_buffer, piece_sem, in_sem, out_sem, row_sem = some(5)
    head, chip = lax.axis_index("head"), lax.axis_index("dp")

    def block_copies(index, arrays, buffers, sems, back):
        kind, block = BLOCK_LIST[index]
        rows = pl.ds(block * KINDS[kind][2], KINDS[kind][2])
        result = []
        for which, (array, buffer) in enumerate(zip(arrays, buffers)):
            outside, inside = array[kind].at[rows], buffer[kind].at[rows]
            pair = (inside, outside) if back else (outside, inside)
            result.append(pltpu.make_async_copy(*pair, sems.at[index, which]))
        return result

    row_reads = [
        pltpu.make_async_copy(rows_at[index], row_buffer.at[index], row_sem.at[0, index])
        for index in range(4)
    ]
    row_writes = [
        pltpu.make_async_copy(
            row_buffer.at[index],
            (y_at, gx_at)[index // 2].at[pl.ds((head if index % 2 == 0 else 1 - head) * SEQ, SEQ)],
            row_sem.at[1, index],
        )
        for index in range(4)
    ]
    piece_copies = [
        pltpu.make_async_copy(pieces_at[index], pieces[index], piece_sem.at[index])
        for index in range(4)
    ]
    count = len(BLOCK_LIST)
    reads = [
        block_copies(index, (weights_at, ones_at, twos_at), (weights, ones, twos), in_sem, False)
        for index in range(count)
    ]
    writes = [
        block_copies(
            index,
            (owned_at, new_at, first_at, second_at, copy_at),
            (owned, weights, ones, twos, copies),
            out_sem,
            True,
        )
        for index in range(count)
    ]
    for copy in piece_copies + [copy for block in reads for copy in block]:
        copy.start()
    for copy in row_reads:
        copy.start()
    gradient = t_ln[...]
    results = adam_step(gradient, ln[...], m_ln[...], v_ln[...], RATES[4])
    ln_owned[...] = jnp.where(owners[4] == chip, gradient, 0.0)
    ln_new[...], ln_first[...], ln_second[...] = results
    for copy in piece_copies:
        copy.wait()
    for index, (kind, block) in enumerate(BLOCK_LIST):
        for copy in reads[index]:
            copy.wait()
        size = KINDS[kind][2]
        mine = owners[kind] == chip

        def update(rows, gradient, kind=kind, mine=mine):
            results = adam_step(
                gradient, weights[kind][rows], ones[kind][rows], twos[kind][rows], RATES[kind]
            )
            owned[kind][rows] = jnp.where(mine, gradient, 0.0)
            weights[kind][rows], ones[kind][rows], twos[kind][rows] = results
            copies[kind][rows] = results[0].astype(bf16)

        def strips(strip, carry, kind=kind, block=block, size=size, update=update):
            start = block * size + strip * STRIP
            if kind == 0:
                source = pl.ds(pl.multiple_of(block * HALF + strip * STRIP, STRIP), STRIP)
                for part in range(2):
                    rows = pl.ds(pl.multiple_of(start + part * HALF, STRIP), STRIP)
                    update(rows, pieces[3][part, source, :].astype(f32))
            else:
                rows = pl.ds(pl.multiple_of(start, STRIP), STRIP)
                update(rows, strip_gradient(kind, block, strip, pieces))
            return carry

        lax.fori_loop(0, (HALF if kind == 0 else size) // STRIP, strips, 0)
        for copy in writes[index]:
            copy.start()
    for read, write in zip(row_reads, row_writes):
        read.wait()
        write.start()
    for copy in row_writes + [copy for block in writes for copy in block]:
        copy.wait()


def update_all(owners, pieces, t_ln, ln_all, weights, ones, twos, rows):
    anywhere = pl.BlockSpec(memory_space=pl.ANY)
    vmem = pl.BlockSpec(memory_space=pltpu.VMEM)
    shapes = [kind[0] for kind in KINDS]
    whole = [shaped(shape, f32) for shape in shapes]
    buffers = [pltpu.VMEM(shape, f32) for shape in shapes]
    results = pl.pallas_call(
        finish_step,
        in_specs=[smem_spec] + [vmem] * 4 + [anywhere] * 20,
        out_specs=[anywhere] * 22 + [vmem] * 4,
        out_shape=whole * 4
        + [shaped(shape) for shape in shapes]
        + [shaped((2 * SEQ, HALF))] * 2
        + [shaped((4, D), f32)] * 4,
        scratch_shapes=[pltpu.VMEM(piece.shape, bf16) for piece in pieces]
        + buffers * 4
        + [pltpu.VMEM(shape, bf16) for shape in shapes]
        + [
            pltpu.VMEM((4, SEQ, HALF), bf16),
            pltpu.SemaphoreType.DMA((4,)),
            pltpu.SemaphoreType.DMA((len(BLOCK_LIST), 3)),
            pltpu.SemaphoreType.DMA((len(BLOCK_LIST), 5)),
            pltpu.SemaphoreType.DMA((2, 4)),
        ],
        compiler_params=limits,
        name="update_all",
    )(owners, t_ln, *ln_all, *pieces, *weights, *ones, *twos, *rows)
    return results[:20], results[20:22], results[22:]


def gather_inputs(tokens, cotangent, w_qkv, w_out, w_up, w_down):
    def both(array):
        return array, swap_heads(array)

    x_own, x_other = both(tokens)
    qkv_own = w_qkv.transpose(1, 0, 2).astype(bf16)
    out_own = w_out.astype(bf16)
    up_own = w_up.astype(bf16)
    down_own = w_down.astype(bf16)
    qkv_other = swap_heads(qkv_own)
    later, _, _ = lax.optimization_barrier((cotangent, x_other, qkv_other))
    dy_own, dy_other = cotangent, swap_heads(later)

    def swap_later(value):
        return swap_heads(lax.optimization_barrier((value, x_other, qkv_other))[0])

    weights = (
        qkv_own,
        qkv_other,
        out_own,
        swap_heads(out_own),
        up_own,
        swap_later(up_own),
        down_own,
        swap_later(down_own),
    )
    return x_own, x_other, dy_own, dy_other, weights


def body(
    tokens,
    cotangent,
    lengths,
    owners,
    w_qkv,
    w_out,
    w_up,
    w_down,
    ln_params,
    m_qkv,
    m_out,
    m_up,
    m_down,
    m_ln,
    v_qkv,
    v_out,
    v_up,
    v_down,
    v_ln,
):
    x_own, x_other, dy_own, dy_other, weights = gather_inputs(
        tokens, cotangent, w_qkv, w_out, w_up, w_down
    )
    y, gx, totals = layer_local(
        x_own, x_other, dy_own, dy_other, lengths, ln_params, weights
    )
    *pieces, t_ln = totals

    def as_rows(array):
        return array.transpose(1, 0, 2).reshape(3 * D, HALF)

    results, (output_rows, grad_input), ln_results = update_all(
        owners,
        pieces,
        t_ln,
        (ln_params, m_ln, v_ln),
        (as_rows(w_qkv), w_out, w_up, w_down),
        (as_rows(m_qkv), m_out, m_up, m_down),
        (as_rows(v_qkv), v_out, v_up, v_down),
        (*y, *gx),
    )
    groups = []
    for slot in range(5):
        group = list(results[slot * 4 : slot * 4 + 4])
        group[0] = group[0].reshape(3, D, HALF).transpose(1, 0, 2)
        if slot < 4:
            group.append(ln_results[slot])
        groups.append(tuple(group))
    owned = tuple(array[None] for array in groups[0])
    return (output_rows, grad_input) + owned + groups[1] + groups[2] + groups[3] + groups[4]


PLACED = (
    (P("dp", "head"),) * 2
    + (P("dp"), P())
    + (P(None, None, "head"), P("head", None), P(None, "head"), P("head", None), P()) * 3
)
RESULTS = (
    (P("dp", "head"),) * 2
    + (
        P("dp", None, None, "head"),
        P("dp", "head", None),
        P("dp", None, "head"),
        P("dp", "head", None),
        P("dp", None, None),
    )
    + (P(None, None, "head"), P("head", None), P(None, "head"), P("head", None), P()) * 3
    + (P(None, None, "head"), P("head", None), P(None, "head"), P("head", None))
)


def solution(mesh):
    return jax.shard_map(
        body, mesh=mesh, in_specs=PLACED, out_specs=RESULTS, check_vma=False
    )
```

```python
import functools

import jax
import jax.numpy as jnp
import numpy as np
from jax import lax
from jax.experimental import pallas as pl
from jax.experimental.pallas import tpu as pltpu
from jax.sharding import PartitionSpec as P

D = 512
HALF = 256
HEAD_DIM = 64
FF = 2048
SPAN = 128
SEQ = 2048
STEP = 5
ROWS = 16
PAIRS = 4
TILE = 512
TILES = SEQ // TILE
SPANS_TILE = TILE // SPAN

epsilon_norm = 1e-05
epsilon_adam = 1e-08
beta_one = 0.5
beta_two = 0.5
decay_rate = 0.1
masked_score = -1e30

bf16 = jnp.bfloat16
f32 = jnp.float32

NN = (((1,), (0,)), ((), ()))
NT = (((1,), (1,)), ((), ()))
TN = (((0,), (0,)), ((), ()))


def mm(left, right, dims=NN):
    return lax.dot_general(left, right, dims, preferred_element_type=f32)


def join_columns(head, own, other):
    low = jnp.where(head == 0, own, other)
    high = jnp.where(head == 0, other, own)
    return jnp.concatenate([low, high], axis=1)


def norm_stats(values):
    mean = jnp.mean(values, axis=1, keepdims=True)
    centered = values - mean
    rstd = lax.rsqrt(jnp.mean(centered * centered, axis=1, keepdims=True) + epsilon_norm)
    return centered * rstd, rstd


def head_stack(pair, low_lanes, high_lanes):
    return jnp.concatenate([pair * low_lanes, pair * high_lanes], axis=0)


def lane_masks(dtype):
    lane = lax.broadcasted_iota(jnp.int32, (1, 2 * HEAD_DIM), 1)
    low = (lane < HEAD_DIM).astype(f32)
    return low.astype(dtype), (1.0 - low).astype(dtype)


def pair_columns(pair):
    base = 3 * HALF * (pair // 2) + 2 * HEAD_DIM * (pair % 2)
    return base, base + HALF, base + 2 * HALF


def unstack_transposed(product):
    joined = jnp.concatenate(
        [product[:HEAD_DIM, :SPAN], product[HEAD_DIM:, SPAN:]], axis=0
    )
    return joined.T


def forward_attention(
    head_at, table, x_own, x_other, ln, w_own, w_other, causal, qkv, bars, probs, ctx, run_sum, normed
):
    head = lax.axis_index("head")
    step = pl.program_id(0)

    @pl.when(step == 0)
    def _():
        run_sum[...] = jnp.zeros_like(run_sum)

    for row in range(0, TILE, 128):
        rows = pl.ds(row, 128)
        x = join_columns(head, x_own[rows, :].astype(f32), x_other[rows, :].astype(f32))
        xhat, _ = norm_stats(x)
        normed[rows, :] = (xhat * ln[0:1, :] + ln[1:2, :]).astype(bf16)
    for side, w in enumerate((w_own, w_other)):
        for part in range(3):
            value = mm(normed[...], w[part])
            if part == 0:
                value = value * float(HEAD_DIM) ** (-0.5)
            base = side * 3 * HALF + part * HALF
            qkv[:, base : base + HALF] = value.astype(bf16)
    low_lanes, high_lanes = lane_masks(bf16)

    def score_span(span):
        rows = pl.ds(span * SPAN, SPAN)
        row_id = step * SPANS_TILE + span
        inverse = table[0, row_id]
        shift = table[1, row_id]
        scores, stacked = [], []
        for pair in range(PAIRS):
            at_q, at_k, at_v = pair_columns(pair)
            lanes = pl.ds(pair * 128, 128)
            lanes_v = pl.ds(512 + pair * 128, 128)
            key = qkv[rows, at_k : at_k + 128]
            value = qkv[rows, at_v : at_v + 128]
            key_bar = (run_sum[:, lanes] * inverse).astype(bf16)
            value_bar = (run_sum[:, lanes_v] * inverse).astype(bf16)
            run_sum[:, lanes] += key.astype(f32)
            run_sum[:, lanes_v] += value.astype(f32)
            bars[rows, lanes] = key_bar
            bars[rows, lanes_v] = value_bar
            query = head_stack(qkv[rows, at_q : at_q + 128], low_lanes, high_lanes)
            scores.append((mm(key, query, NT) + causal[...], mm(key_bar, query, NT) + shift))
            stacked.append(jnp.concatenate([value, value_bar], axis=0))
        return scores, stacked

    def soft_span(span, scores):
        expo = []
        for direct, summary in scores:
            top = jnp.maximum(
                jnp.max(direct, axis=0, keepdims=True), jnp.max(summary, axis=0, keepdims=True)
            )
            expo.append((jnp.exp(direct - top), jnp.exp(summary - top)))
        both = []
        for pair, (direct, summary) in enumerate(expo):
            total = jnp.sum(direct, axis=0, keepdims=True) + jnp.sum(
                summary, axis=0, keepdims=True
            )
            scale = 1.0 / total
            prob = jnp.concatenate(
                [(direct * scale).astype(bf16), (summary * scale).astype(bf16)], axis=0
            )
            probs[span * PAIRS + pair] = prob
            both.append(prob)
        return both

    def context_span(span, stacked, both):
        rows = pl.ds(span * SPAN, SPAN)
        for pair in range(PAIRS):
            lanes = pl.ds(pair * 128, 128)
            ctx[rows, lanes] = unstack_transposed(mm(stacked[pair], both[pair], TN)).astype(bf16)

    ready = score_span(0)
    for span in range(SPANS_TILE):
        scores, stacked = ready
        if span + 1 < SPANS_TILE:
            ready = score_span(span + 1)
        both = soft_span(span, scores)
        context_span(span, stacked, both)


def gelu_parts(u):
    share = lax.erf(u * 0.7071067811865476) * 0.5 + 0.5
    bell = jnp.exp2((u * u) * -0.7213475204444817)
    return u * share, share + u * bell * 0.3989422804014327


def swap_heads(value):
    return lax.ppermute(value, "head", [(0, 1), (1, 0)])


def chip_grid(count):
    side = 1 << ((count.bit_length() - 1) // 3)
    return (count // (side * side), side, side)


class Lines:
    def __init__(self, count):
        self.sizes = chip_grid(count)
        self.strides = (self.sizes[1] * self.sizes[2], self.sizes[2], 1)
        self.chip = lax.axis_index("dp")
        self.head = lax.axis_index("head")
        self.places = [
            lax.rem(self.chip // stride, size) for stride, size in zip(self.strides, self.sizes)
        ]
        self.members = [
            [self.find(axis, ahead) for ahead in range(1, size)]
            for axis, size in enumerate(self.sizes)
        ]

    def partner(self):
        return (self.chip, 1 - self.head)

    def member(self, axis, ahead):
        return self.members[axis][ahead - 1]

    def find(self, axis, ahead):
        size = self.sizes[axis]
        place = 1 - self.places[axis]
        if size > 2:
            place = lax.rem(self.places[axis] + ahead, size)
        chip = self.chip + (place - self.places[axis]) * self.strides[axis]
        return place, (chip, self.head)

    def greet(self):
        barrier = pltpu.get_barrier_semaphore()
        others = [self.partner()]
        for axis in range(3):
            others += [self.member(axis, ahead)[1] for ahead in range(1, self.sizes[axis])]
        for other in others:
            pl.semaphore_signal(
                barrier, inc=1, device_id=other, device_id_type=pl.DeviceIdType.MESH
            )
        pl.semaphore_wait(barrier, len(others))


X_FIRST, Y_FIRST = (2, 1, 0), (1, 2, 0)


def whole_slices(count):
    return all(shape[1] % (16 * count) == 0 for shape, _ in PIECES)


def chunk_rows(rows):
    return next(chunk for chunk in (128, 96, 64, 48, 32, 16) if rows % chunk == 0)


def sum_scratch(shape, orders, count):
    parts, rows, lanes = shape
    sizes = chip_grid(count)
    shapes = [pltpu.VMEM(shape, bf16)]
    sems = [pltpu.SemaphoreType.DMA((3,))]
    for order in orders:
        left = rows
        for axis in order:
            left //= sizes[axis]
            shapes.append(pltpu.VMEM((sizes[axis] - 1, left, lanes), bf16))
            sems.append(pltpu.SemaphoreType.DMA((2, 2, sizes[axis] - 1)))
    return shapes + sems


class DpSum:
    def __init__(self, lines, orders, grads, total, scratch):
        self.lines = lines
        self.orders = orders
        self.parts = range(len(orders))
        self.grads = grads
        self.total = total
        self.rows = grads.shape[2]
        self.work, self.final = grads.at[0], scratch.pop(0)
        self.slots = [[scratch.pop(0) for _ in order] for order in orders]
        self.core_sem = scratch.pop(0)
        self.sems = [[scratch.pop(0) for _ in order] for order in orders]
        self.base = []
        for order in orders:
            bases, piece = [0], self.rows
            for axis in order:
                piece //= lines.sizes[axis]
                bases.append(bases[-1] + lines.places[axis] * piece)
            self.base.append(bases)

    def remote(self, source, target, send_sem, recv_sem, device):
        return pltpu.make_async_remote_copy(
            src_ref=source,
            dst_ref=target,
            send_sem=send_sem,
            recv_sem=recv_sem,
            device_id=device,
            device_id_type=pl.DeviceIdType.MESH,
        )

    def core_copy(self):
        return self.remote(
            self.grads.at[1],
            self.final,
            self.core_sem.at[0],
            self.core_sem.at[1],
            self.lines.partner(),
        )

    def core_send(self):
        self.core_copy().start()

    def core_sum(self):
        self.core_copy().wait()
        chunk = chunk_rows(self.rows)
        for part in self.parts:

            def add(index, carry, part=part):
                rows = pl.ds(pl.multiple_of(index * chunk, chunk), chunk)
                self.work[part, rows, :] = self.work[part, rows, :] + self.final[part, rows, :]
                return carry

            lax.fori_loop(0, self.rows // chunk, add, 0)

    def spread_copies(self, part, stage):
        axis = self.orders[part][stage]
        size = self.lines.sizes[axis]
        base = self.base[part][stage]
        piece = self.rows
        for at in self.orders[part][: stage + 1]:
            piece //= self.lines.sizes[at]
        copies = []
        for ahead in range(1, size):
            place, device = self.lines.member(axis, ahead)
            start = pl.multiple_of(base + place * piece, 16)
            copies.append(
                self.remote(
                    self.work.at[part, pl.ds(start, piece)],
                    self.slots[part][stage].at[ahead - 1],
                    self.sems[part][stage].at[0, 0, ahead - 1],
                    self.sems[part][stage].at[0, 1, ahead - 1],
                    device,
                )
            )
        return copies, self.base[part][stage + 1], piece

    def spread_send(self, part, stage):
        for copy in self.spread_copies(part, stage)[0]:
            copy.start()

    def spread_sum(self, part, stage):
        copies, mine, piece = self.spread_copies(part, stage)
        for copy in copies:
            copy.wait()
        slots = self.slots[part][stage]
        target = self.final if stage == 2 else self.work
        chunk = chunk_rows(piece)

        def add(index, carry):
            offset = pl.multiple_of(index * chunk, chunk)
            rows = pl.ds(pl.multiple_of(mine + offset, 16), chunk)
            value = self.work[part, rows, :]
            if len(copies) > 1:
                value = value.astype(f32)
            for slot in range(len(copies)):
                value = value + slots[slot, pl.ds(offset, chunk), :].astype(value.dtype)
            target[part, rows, :] = value.astype(bf16)
            return carry

        lax.fori_loop(0, piece // chunk, add, 0)

    def gather_copies(self, part, stage):
        axis = self.orders[part][stage]
        size = self.lines.sizes[axis]
        piece = self.rows
        for at in self.orders[part][: stage + 1]:
            piece //= self.lines.sizes[at]
        mine = pl.multiple_of(self.base[part][stage + 1], 16)
        rows = pl.ds(mine, piece)
        copies = []
        for ahead in range(1, size):
            _, device = self.lines.member(axis, ahead)
            copies.append(
                self.remote(
                    self.final.at[part, rows],
                    self.final.at[part, rows],
                    self.sems[part][stage].at[1, 0, ahead - 1],
                    self.sems[part][stage].at[1, 1, ahead - 1],
                    device,
                )
            )
        return copies

    def gather_send(self, part, stage):
        for copy in self.gather_copies(part, stage):
            copy.start()

    def gather_wait(self, part, stage):
        for copy in self.gather_copies(part, stage):
            copy.wait()

    def store_copy(self):
        return pltpu.make_async_copy(self.final, self.total, self.core_sem.at[2])

    def event(self, index):
        if index == 0:
            self.core_send()
        elif index == 1:
            self.core_sum()
        for part in self.parts:
            if 2 <= index <= 4:
                self.spread_sum(part, index - 2)
            elif index >= 5:
                self.gather_wait(part, 7 - index)
            if 1 <= index <= 3:
                self.spread_send(part, index - 1)
            elif 4 <= index <= 6:
                self.gather_send(part, 6 - index)
        if index == 7:
            self.store_copy().start()

    def finish(self):
        self.store_copy().wait()


EVENTS = 8


def ln_scratch(count):
    return [
        pltpu.VMEM((2, 4, D), f32),
        pltpu.SemaphoreType.DMA((2,)),
        *[pltpu.VMEM((size, 4, D), f32) for size in chip_grid(count)],
        *[pltpu.SemaphoreType.DMA((2, max(size - 1, 1))) for size in chip_grid(count)],
    ]


class LnSum:
    def __init__(self, lines, value, total, scratch):
        self.lines = lines
        self.value = value
        self.total = total
        self.core, self.core_sem = scratch[:2]
        self.slots = scratch[2:5]
        self.sems = scratch[5:8]

    def stage_copies(self, stage):
        lines = self.lines
        if stage == 0:
            mine = self.core.at[lines.head]
            return [
                pltpu.make_async_remote_copy(
                    src_ref=mine,
                    dst_ref=mine,
                    send_sem=self.core_sem.at[0],
                    recv_sem=self.core_sem.at[1],
                    device_id=lines.partner(),
                    device_id_type=pl.DeviceIdType.MESH,
                )
            ]
        axis = stage - 1
        mine = self.slots[axis].at[lines.places[axis]]
        return [
            pltpu.make_async_remote_copy(
                src_ref=mine,
                dst_ref=mine,
                send_sem=self.sems[axis].at[0, ahead - 1],
                recv_sem=self.sems[axis].at[1, ahead - 1],
                device_id=lines.member(axis, ahead)[1],
                device_id_type=pl.DeviceIdType.MESH,
            )
            for ahead in range(1, lines.sizes[axis])
        ]

    def send(self, stage):
        if stage == 0:
            self.core[self.lines.head] = self.value[...]
        for copy in self.stage_copies(stage):
            copy.start()

    def finish(self, stage):
        for copy in self.stage_copies(stage):
            copy.wait()
        slots = self.core if stage == 0 else self.slots[stage - 1]
        value = slots[0]
        for slot in range(1, slots.shape[0]):
            value = value + slots[slot]
        if stage == 3:
            self.total[...] = value
        else:
            self.slots[stage][self.lines.places[stage]] = value


PIECES = (
    ((2, 1024, HALF), (X_FIRST, Y_FIRST)),
    ((2, 1024, HALF), (X_FIRST, Y_FIRST)),
    ((1, HALF, D), (Y_FIRST,)),
    ((2, 3 * HALF, HALF), (X_FIRST, Y_FIRST)),
)
CHUNKS = FF // 512
CHUNK_STEP = TILES
POST_STEP = CHUNK_STEP + CHUNKS
ATT_STEP = POST_STEP + TILES
SPANS_STEP = 2
ATT_STEPS = ROWS // SPANS_STEP
LAST_STEP = ATT_STEP + ATT_STEPS
STEPS = LAST_STEP + TILES
EVENT_AT = (
    ((6, 0), (6, 1), (7, 1), (8, 0), (12, 0), (15, 0), (17, 0), (19, 0),),
    ((8, 0), (9, 0), (13, 0), (16, 0), (19, 0),),
    ((14, 0), (16, 0), (18, 0),),
    ((20, 0), (22, 0),),
)


def mlp_and_back(
    count,
    table,
    lengths,
    ln,
    x_own_at,
    x_other_at,
    dy_own_at,
    dy_other_at,
    ctx_at,
    qkv_at,
    bars_at,
    probs_at,
    out_own_at,
    out_other_at,
    w_own_at,
    w_other_at,
    up_own,
    up_other,
    down_own,
    down_other,
    y_own_at,
    y_other_at,
    gx_own_at,
    gx_other_at,
    *refs,
):
    summing = whole_slices(count)
    kinds = len(PIECES)
    totals, ln_total = refs[:kinds], refs[kinds]
    (x_own, x_other, dy_own, dy_other, ctx, qkv_two, bars_two, probs_two, out_own, out_other,
     w_own, w_other, up_all, down_all, load_sem, weight_sem, block_sem, store_sem, res, grad_qkv,
     normed_t, gm, mlp, grad_n, acc_one, acc_two, hid, grad_hid, after,
     acc_ln) = refs[kinds + 1 : kinds + 31]
    grads = refs[kinds + 31 : kinds + 31 + len(PIECES)]
    scratch = list(refs[kinds + 31 + len(PIECES) :])
    head = lax.axis_index("head")
    used = lengths[head]
    sums = []
    if summing:
        lines = Lines(count)
        for (_, orders), grad, total in zip(PIECES, grads, totals):
            sums.append(DpSum(lines, orders, grad, total, scratch))
        small = LnSum(lines, acc_ln, ln_total, scratch)

    def run_events(events):
        for index, event in events:
            sums[index].event(event)

    def hook(step, first, end, place=0):
        for at in range(first, end if summing else 0):
            events = [
                (index, event)
                for index, times in enumerate(EVENT_AT)
                for event, time in enumerate(times)
                if time == (at, place)
            ]
            if events:

                @pl.when(step == at)
                def _(events=events):
                    run_events(events)

    mine = pl.ds(head * SEQ, SEQ)
    loads = [
        pltpu.make_async_copy(source, target, load_sem.at[index])
        for index, (source, target) in enumerate(
            (
                (ctx_at, ctx),
                (out_own_at, out_own),
                (out_other_at, out_other),
                (x_own_at.at[mine], x_own),
                (x_other_at.at[mine], x_other),
                (dy_own_at.at[mine], dy_own),
                (dy_other_at.at[mine], dy_other),
                (w_own_at, w_own),
                (w_other_at, w_other),
            )
        )
    ]
    weight_copies = []
    for chunk in range(CHUNKS):
        up_w, down_w = ((up_own, down_own), (up_other, down_other))[chunk % 2]
        cut = pl.ds(chunk // 2 * 512, 512)
        pairs = ((up_w.at[:, cut], up_all.at[chunk]), (down_w.at[cut], down_all.at[chunk]))
        for which, (source, target) in enumerate(pairs):
            sem = weight_sem.at[2 * chunk + which]
            weight_copies.append(pltpu.make_async_copy(source, target, sem))
    block_rows = SPANS_STEP * SPAN
    block_probs = SPANS_STEP * PAIRS

    def block_copies(index):
        block = ATT_STEPS - 1 - index
        slot = lax.rem(index, 2)
        rows = pl.ds(block * block_rows, block_rows)
        many = pl.ds(block * block_probs, block_probs)
        pairs = (
            (qkv_at.at[rows], qkv_two.at[slot]),
            (bars_at.at[rows], bars_two.at[slot]),
            (probs_at.at[many], probs_two.at[slot]),
        )
        return [
            pltpu.make_async_copy(source, target, block_sem.at[slot, which])
            for which, (source, target) in enumerate(pairs)
        ]

    stores = []
    for index, (source, target) in enumerate(
        (
            (ctx.at[:, pl.ds(0, HALF)], y_own_at),
            (ctx.at[:, pl.ds(HALF, HALF)], y_other_at),
            (dy_own, gx_own_at),
            (dy_other, gx_other_at),
        )
    ):
        if summing and index % 2 == 1:
            stores.append(
                pltpu.make_async_remote_copy(
                    src_ref=source,
                    dst_ref=target,
                    send_sem=store_sem.at[index],
                    recv_sem=store_sem.at[4 + index // 2],
                    device_id=lines.partner(),
                    device_id_type=pl.DeviceIdType.MESH,
                )
            )
        else:
            stores.append(pltpu.make_async_copy(source, target, store_sem.at[index]))

    def x_rows(rows):
        return join_columns(head, x_own[rows, :].astype(f32), x_other[rows, :].astype(f32))

    def dy_rows(rows):
        return join_columns(head, dy_own[rows, :].astype(f32), dy_other[rows, :].astype(f32))

    def valid_rows(first):
        ids = lax.broadcasted_iota(jnp.int32, (128, 1), 0) + first
        return (ids < used).astype(f32)

    def before_mlp(tile, carry):
        base = tile * TILE
        tokens = pl.ds(pl.multiple_of(base, TILE), TILE)
        res[tokens, :] = mm(ctx[tokens, :HALF], out_own[...]) + mm(
            ctx[tokens, HALF:], out_other[...]
        )
        mlp[tokens, :] = jnp.zeros((TILE, D), f32)
        grad_n[tokens, :] = jnp.zeros((TILE, D), f32)
        for row in range(0, TILE, 128):
            at = pl.ds(pl.multiple_of(base + row, 128), 128)
            valid = valid_rows(base + row)
            h = x_rows(at) + valid * res[at, :]
            res[at, :] = h
            hat, _ = norm_stats(h)
            n2 = (hat * ln[2:3, :] + ln[3:4, :]).astype(bf16)
            grad_qkv[at, :D] = n2
            normed_t[:, at] = n2.T
            gm[at, :] = (valid * dy_rows(at)).astype(bf16)
        return carry

    def chunk_in(chunk, tile):
        tokens = pl.ds(tile * TILE, TILE)
        hid[tile % 2] = mm(grad_qkv[tokens, :D], up_all[chunk])
        grad_hid[tile % 2] = mm(gm[tokens, :], down_all[chunk], NT)

    def act_rows(tile, row, size):
        return pl.ds(tile % 2 * TILE + row, size), pl.ds((2 + tile % 2) * TILE + row, size)

    def chunk_mid(tile):
        slot = tile % 2
        for row in range(0, TILE, 16):
            rows = pl.ds(row, 16)
            a, da = gelu_parts(hid[slot, rows, :])
            at_act, at_gu = act_rows(tile, row, 16)
            grad_qkv[at_act, D : 2 * D] = a.astype(bf16)
            grad_qkv[at_gu, D : 2 * D] = (grad_hid[slot, rows, :] * da).astype(bf16)

    def chunk_out(chunk, tile):
        tokens = pl.ds(tile * TILE, TILE)
        at_act, at_gu = act_rows(tile, 0, TILE)
        act = grad_qkv[at_act, D : 2 * D]
        gu = grad_qkv[at_gu, D : 2 * D]
        mlp[tokens, :] += mm(act, down_all[chunk])
        grad_n[tokens, :] += mm(gu, up_all[chunk], NT)
        part_down = mm(act, gm[tokens, :], TN)
        part_up = mm(normed_t[:, tokens], gu)
        if tile == 0:
            acc_one[...] = part_down
            acc_two[...] = part_up
        else:
            acc_one[...] += part_down
            acc_two[...] += part_up

    def chunk_tiles(chunk, first):
        chunk_in(chunk, first)
        chunk_in(chunk, first + 1)
        chunk_mid(first)
        chunk_out(chunk, first)
        chunk_mid(first + 1)
        chunk_out(chunk, first + 1)

    def hidden_chunk(chunk, carry):
        step = CHUNK_STEP + chunk
        hook(step, CHUNK_STEP, POST_STEP)
        chunk_tiles(chunk, 0)
        hook(step, CHUNK_STEP, POST_STEP, 1)
        chunk_tiles(chunk, 2)
        side = lax.rem(chunk, 2)

        for half in range(2):

            @pl.when(chunk // 2 == half)
            def _(half=half):
                for part in range(2):
                    lanes = slice(part * HALF, (part + 1) * HALF)
                    grads[half][side, part, :512] = acc_one[:, lanes].astype(bf16)
                    grads[half][side, part, 512:] = acc_two[:, lanes].astype(bf16)

        return carry

    def after_mlp(tile, carry):
        hook(POST_STEP + tile, POST_STEP, ATT_STEP)
        base = tile * TILE
        tokens = pl.ds(pl.multiple_of(base, TILE), TILE)
        for row in range(0, TILE, 128):
            at = pl.ds(pl.multiple_of(base + row, 128), 128)
            valid = valid_rows(base + row)
            h = res[at, :]
            mlp[at, :] = h + valid * mlp[at, :]
            gn = grad_n[at, :]
            hat, rstd = norm_stats(h)
            acc_ln[2:3, :] += jnp.sum(gn * hat, axis=0, keepdims=True)
            acc_ln[3:4, :] += jnp.sum(gn, axis=0, keepdims=True)
            scaled = gn * ln[2:3, :]
            back = rstd * (
                scaled
                - jnp.mean(scaled, axis=1, keepdims=True)
                - hat * jnp.mean(scaled * hat, axis=1, keepdims=True)
            )
            gh = dy_rows(at) + back
            res[at, :] = gh
            gm[at, :] = (valid * gh).astype(bf16)
        ga = gm[tokens, :]
        acc_one[...] += mm(ctx[tokens, :], ga, TN)
        low, high = mlp[tokens, :HALF], mlp[tokens, HALF:]
        ctx[tokens, :HALF] = jnp.where(head == 0, low, high).astype(bf16)
        ctx[tokens, HALF:] = jnp.where(head == 0, high, low).astype(bf16)
        grad_low = mm(ga, out_own[...], NT)
        grad_high = mm(ga, out_other[...], NT)
        gm[tokens, :HALF] = grad_low.astype(bf16)
        gm[tokens, HALF:] = grad_high.astype(bf16)
        return carry

    low_lanes, high_lanes = lane_masks(bf16)
    scale_factor = float(HEAD_DIM) ** (-0.5)

    def span_tokens(block, span):
        return pl.ds(pl.multiple_of(block * block_rows + span * SPAN, SPAN), SPAN)

    def attention_in(block, qkv, bars, span):
        rows = pl.ds(span * SPAN, SPAN)
        held = []
        for pair in range(PAIRS):
            _, _, at_v = pair_columns(pair)
            lanes = pl.ds(pair * 128, 128)
            lanes_v = pl.ds(512 + pair * 128, 128)
            values = jnp.concatenate([qkv[rows, at_v : at_v + 128], bars[rows, lanes_v]], axis=0)
            grad = head_stack(gm[span_tokens(block, span), lanes], low_lanes, high_lanes)
            held.append((grad, mm(values, grad, NT)))
        return held

    def attention_mid(probs, span, held):
        scores = []
        for pair in range(PAIRS):
            prob_f = probs[span * PAIRS + pair].astype(f32)
            weighted = held[pair][1] * prob_f
            delta = jnp.sum(weighted, axis=0, keepdims=True)
            scores.append((weighted - prob_f * delta).astype(bf16))
        return scores

    def attention_out(block, qkv, bars, probs, span, held, scores):
        rows = pl.ds(span * SPAN, SPAN)
        tokens = span_tokens(block, span)
        inverse = table[0, block * SPANS_STEP + span]
        for pair in range(PAIRS):
            at_q, at_k, at_v = pair_columns(pair)
            lanes = pl.ds(pair * 128, 128)
            lanes_v = pl.ds(512 + pair * 128, 128)
            keys = jnp.concatenate([qkv[rows, at_k : at_k + 128], bars[rows, lanes]], axis=0)
            query = head_stack(qkv[rows, at_q : at_q + 128], low_lanes, high_lanes)
            grad_q = unstack_transposed(mm(keys, scores[pair], TN)) * scale_factor
            grad_k = mm(scores[pair], query)
            grad_v = mm(probs[span * PAIRS + pair], held[pair][0])
            grad_qkv[tokens, at_q : at_q + 128] = grad_q.astype(bf16)
            grad_qkv[tokens, at_k : at_k + 128] = (grad_k[:SPAN] + after[:, lanes]).astype(bf16)
            grad_qkv[tokens, at_v : at_v + 128] = (grad_v[:SPAN] + after[:, lanes_v]).astype(bf16)
            after[:, lanes] += grad_k[SPAN:] * inverse
            after[:, lanes_v] += grad_v[SPAN:] * inverse

    def attention_block(index, carry):
        block = ATT_STEPS - 1 - index
        slot = lax.rem(index, 2)
        hook(ATT_STEP + index, ATT_STEP, LAST_STEP)
        for copy in block_copies(index):
            copy.wait()
        qkv, bars, probs = qkv_two.at[slot], bars_two.at[slot], probs_two.at[slot]
        for row in range(0, block_rows, 128):
            rows = pl.ds(pl.multiple_of(block * block_rows + row, 128), 128)
            hat, _ = norm_stats(x_rows(rows))
            normed_t[:, row : row + 128] = (hat * ln[0:1, :] + ln[1:2, :]).astype(bf16).T
        held_one = attention_in(block, qkv, bars, 1)
        held_two = attention_in(block, qkv, bars, 0)
        scores = attention_mid(probs, 1, held_one)
        attention_out(block, qkv, bars, probs, 1, held_one, scores)
        scores = attention_mid(probs, 0, held_two)
        attention_out(block, qkv, bars, probs, 0, held_two, scores)
        tokens = pl.ds(pl.multiple_of(block * block_rows, block_rows), block_rows)
        for side in range(2):
            for part in range(3):
                at = side * 3 * HALF + part * HALF
                rows = slice(part * D, (part + 1) * D)
                lanes = slice(side * HALF, (side + 1) * HALF)
                mlp[rows, lanes] += mm(
                    normed_t[:, :block_rows], grad_qkv[tokens, at : at + HALF]
                )


        @pl.when(index + 2 < ATT_STEPS)
        def _():
            for copy in block_copies(index + 2):
                copy.start()

        return carry

    def first_norm(tile, carry):
        hook(LAST_STEP + tile, LAST_STEP, STEPS)
        base = tile * TILE
        tokens = pl.ds(pl.multiple_of(base, TILE), TILE)
        for side, w in enumerate((w_own, w_other)):
            for part in range(3):
                at = side * 3 * HALF + part * HALF
                back = mm(grad_qkv[tokens, at : at + HALF], w[part], NT)
                if side == 0 and part == 0:
                    grad_n[:TILE, :] = back
                else:
                    grad_n[:TILE, :] += back
        for row in range(0, TILE, 128):
            at = pl.ds(pl.multiple_of(base + row, 128), 128)
            hat, rstd = norm_stats(x_rows(at))
            gn = grad_n[row : row + 128, :]
            acc_ln[0:1, :] += jnp.sum(gn * hat, axis=0, keepdims=True)
            acc_ln[1:2, :] += jnp.sum(gn, axis=0, keepdims=True)
            scaled = gn * ln[0:1, :]
            back = rstd * (
                scaled
                - jnp.mean(scaled, axis=1, keepdims=True)
                - hat * jnp.mean(scaled * hat, axis=1, keepdims=True)
            )
            gx = res[at, :] + back
            low, high = gx[:, :HALF], gx[:, HALF:]
            dy_own[at, :] = jnp.where(head == 0, low, high).astype(bf16)
            dy_other[at, :] = jnp.where(head == 0, high, low).astype(bf16)
        return carry

    for copy in loads + weight_copies + block_copies(0) + block_copies(1):
        copy.start()
    if summing:
        lines.greet()
    after[...] = jnp.zeros_like(after)
    acc_ln[...] = jnp.zeros_like(acc_ln)
    for copy in loads:
        copy.wait()
    lax.fori_loop(0, TILES, before_mlp, 0)
    for copy in weight_copies:
        copy.wait()
    lax.fori_loop(0, CHUNKS, hidden_chunk, 0)
    acc_one[...] = jnp.zeros_like(acc_one)
    lax.fori_loop(0, TILES, after_mlp, 0)
    for copy in stores[:2]:
        copy.start()
    for side in range(2):
        grads[2][side, 0] = acc_one[side * HALF : (side + 1) * HALF, :].astype(bf16)
    mlp[...] = jnp.zeros_like(mlp)
    lax.fori_loop(0, ATT_STEPS, attention_block, 0)
    for side in range(2):
        for part in range(2):
            for kind in range(3):
                rows = slice(kind * HALF, (kind + 1) * HALF)
                source = slice(kind * D + part * HALF, kind * D + (part + 1) * HALF)
                lanes = slice(side * HALF, (side + 1) * HALF)
                grads[3][side, part, rows] = mlp[source, lanes].astype(bf16)
    lax.fori_loop(0, TILES, first_norm, 0)
    for copy in stores[2:]:
        copy.start()
    if summing:
        small.send(0)
        for index in range(EVENTS):
            left = [
                (which, len(times) + index)
                for which, times in enumerate(EVENT_AT)
                if len(times) + index < EVENTS
            ]
            run_events(left[::-1])
            if index <= 3:
                small.finish(index)
            if index < 3:
                small.send(index + 1)
        for entry in sums:
            entry.finish()
    else:
        for total, grad in zip(totals, grads):
            total[...] = grad[...]
        ln_total[...] = acc_ln[...]
    for copy in stores:
        copy.wait()


def rows_spec(width):
    return pl.BlockSpec((TILE, width), lambda i, *_: (i, 0))


def whole_spec(shape):
    rank = len(shape)
    return pl.BlockSpec(shape, lambda i, *_: (0,) * rank, pipeline_mode=pl.Buffered(1))


def shaped(shape, dtype=bf16):
    return jax.ShapeDtypeStruct(shape, dtype)


smem_spec = pl.BlockSpec(memory_space=pltpu.SMEM)
limits = pltpu.CompilerParams(vmem_limit_bytes=60 * 1024 * 1024)


def span_table():
    ids = np.arange(ROWS)
    inverse = 1.0 / np.maximum(ids, 1)
    shift = np.where(ids >= 1, np.log(np.maximum(ids, 1)), masked_score)
    return jnp.asarray(np.stack([inverse, shift]).astype(np.float32))


def causal_bias():
    key = np.arange(SPAN)[:, None]
    query = np.arange(2 * SPAN)[None, :] % SPAN
    return jnp.asarray(np.where(key <= query, 0.0, masked_score).astype(np.float32))


def layer_local(x_own, x_other, dy_own, dy_other, lengths, ln_params, weights):
    qkv_own, qkv_other, out_own, out_other, up_own, up_other, down_own, down_other = weights
    table = span_table()
    qkv, bars, probs, ctx = pl.pallas_call(
        forward_attention,
        grid_spec=pltpu.PrefetchScalarGridSpec(
        num_scalar_prefetch=1,
        grid=(TILES,),
        in_specs=[
            smem_spec,
            pl.BlockSpec((TILE, HALF), lambda i, head: (head[0] * TILES + i, 0)),
            pl.BlockSpec((TILE, HALF), lambda i, head: (head[0] * TILES + i, 0)),
            whole_spec((4, D)),
            whole_spec((3, D, HALF)),
            whole_spec((3, D, HALF)),
            whole_spec((SPAN, 2 * SPAN)),
        ],
        out_specs=[
            rows_spec(3 * D),
            rows_spec(2 * D),
            pl.BlockSpec((SPANS_TILE * PAIRS, 2 * SPAN, 2 * SPAN), lambda i, head: (i, 0, 0)),
            rows_spec(D),
        ],
        scratch_shapes=[pltpu.VMEM((SPAN, 2 * D), f32), pltpu.VMEM((TILE, D), bf16)],
        ),
        out_shape=[
            shaped((SEQ, 3 * D)),
            shaped((SEQ, 2 * D)),
            shaped((ROWS * PAIRS, 2 * SPAN, 2 * SPAN)),
            shaped((SEQ, D)),
        ],
        compiler_params=limits,
        name="forward_attention",
    )(lax.axis_index("head").reshape(1), table, x_own, x_other, ln_params, qkv_own, qkv_other, causal_bias())
    count = lax.axis_size("dp")
    summing = whole_slices(count)
    sum_buffers, extra, total_specs, total_shapes = [], {}, [], []
    anywhere = pl.BlockSpec(memory_space=pl.ANY)
    if summing:
        for shape, orders in PIECES:
            sum_buffers += sum_scratch(shape, orders, count)
            total_specs.append(anywhere)
            total_shapes.append(shaped(shape))
        sum_buffers += ln_scratch(count)
        extra = dict(collective_id=0, has_side_effects=True)
    else:
        for shape, _ in PIECES:
            total_specs.append(pl.BlockSpec(memory_space=pltpu.VMEM))
            total_shapes.append(shaped((2, *shape)))
    block_rows = SPANS_STEP * SPAN
    vmem = pl.BlockSpec(memory_space=pltpu.VMEM)
    y_own, y_other, gx_own, gx_other, *totals = pl.pallas_call(
        functools.partial(mlp_and_back, count),
        in_specs=[smem_spec, smem_spec, vmem] + [anywhere] * 16,
        out_specs=[anywhere] * 4 + total_specs + [vmem],
        out_shape=[shaped((SEQ, HALF))] * 4 + total_shapes + [shaped((4, D), f32)],
        scratch_shapes=[
            pltpu.VMEM((SEQ, HALF), bf16),
            pltpu.VMEM((SEQ, HALF), bf16),
            pltpu.VMEM((SEQ, HALF), bf16),
            pltpu.VMEM((SEQ, HALF), bf16),
            pltpu.VMEM((SEQ, D), bf16),
            pltpu.VMEM((2, block_rows, 3 * D), bf16),
            pltpu.VMEM((2, block_rows, 2 * D), bf16),
            pltpu.VMEM((2, SPANS_STEP * PAIRS, 2 * SPAN, 2 * SPAN), bf16),
            pltpu.VMEM((HALF, D), bf16),
            pltpu.VMEM((HALF, D), bf16),
            pltpu.VMEM((3, D, HALF), bf16),
            pltpu.VMEM((3, D, HALF), bf16),
            pltpu.VMEM((CHUNKS, D, 512), bf16),
            pltpu.VMEM((CHUNKS, 512, D), bf16),
            pltpu.SemaphoreType.DMA((9,)),
            pltpu.SemaphoreType.DMA((2 * CHUNKS,)),
            pltpu.SemaphoreType.DMA((2, 3)),
            pltpu.SemaphoreType.DMA((6,)),
            pltpu.VMEM((SEQ, D), f32),
            pltpu.VMEM((SEQ, 3 * D), bf16),
            pltpu.VMEM((D, SEQ), bf16),
            pltpu.VMEM((SEQ, D), bf16),
            pltpu.VMEM((SEQ, D), f32),
            pltpu.VMEM((SEQ, D), f32),
            pltpu.VMEM((512, D), f32),
            pltpu.VMEM((D, 512), f32),
            pltpu.VMEM((2, TILE, 512), f32),
            pltpu.VMEM((2, TILE, 512), f32),
            pltpu.VMEM((SPAN, 2 * D), f32),
            pltpu.VMEM((4, D), f32),
        ]
        + [pltpu.VMEM((2, *shape), bf16) for shape, _ in PIECES]
        + sum_buffers,
        compiler_params=pltpu.CompilerParams(vmem_limit_bytes=63 * 1024 * 1024, **extra),
        name="mlp_and_back",
    )(
        table,
        lengths,
        ln_params,
        x_own,
        x_other,
        dy_own,
        dy_other,
        ctx,
        qkv,
        bars,
        probs,
        out_own,
        out_other,
        qkv_own,
        qkv_other,
        up_own,
        up_other,
        down_own,
        down_other,
    )
    if not summing:
        *grads, g_ln = totals
        chips = [grad[0].astype(f32) + swap_heads(grad[1]).astype(f32) for grad in grads]
        pieces = [lax.psum(chip.astype(bf16), "dp") for chip in chips]
        totals = (*pieces, lax.psum(g_ln, ("dp", "head")))
        y_other, gx_other = swap_heads(y_other), swap_heads(gx_other)
    return (y_own, y_other), (gx_own, gx_other), totals


RATES = (
    float(D) ** (-0.5),
    4.0 * float(D) ** (-0.5),
    float(D) ** (-0.5),
    float(FF) ** (-0.5),
    0.7,
)


def adam_step(gradient, weight, moment_one, moment_two, step_rate):
    first_new = beta_one * moment_one + (1.0 - beta_one) * gradient
    second_new = beta_two * moment_two + (1.0 - beta_two) * gradient * gradient
    first_hat = first_new * (1.0 / (1.0 - beta_one**STEP))
    second_hat = second_new * (1.0 / (1.0 - beta_two**STEP))
    weight_new = weight - step_rate * (
        first_hat / (jnp.sqrt(second_hat) + epsilon_adam) + decay_rate * weight
    )
    return (weight_new, first_new, second_new)


KINDS = (
    ((3 * D, HALF), 3, D),
    ((HALF, D), 1, HALF),
    ((D, FF // 2), 4, 128),
    ((FF // 2, D), 4, HALF),
)
BLOCK_LIST = [(kind, block) for kind in (3, 2, 1, 0) for block in range(KINDS[kind][1])]
STRIP = 32


def strip_gradient(kind, block, strip, pieces):
    def take(piece, part, start):
        rows = pl.ds(pl.multiple_of(start + strip * STRIP, STRIP), STRIP)
        return pieces[piece][part, rows, :].astype(f32)

    if kind == 1:
        return take(2, 0, 0)
    if kind == 2:
        start = 512 + block * 128
        return jnp.concatenate(
            [take(piece, part, start) for piece in range(2) for part in range(2)], axis=1
        )
    start = (block % 2) * HALF
    return jnp.concatenate([take(block // 2, part, start) for part in range(2)], axis=1)


def finish_step(owners, t_ln, ln, m_ln, v_ln, *refs):
    refs = list(refs)

    def some(count):
        taken, refs[:] = refs[:count], refs[count:]
        return taken

    pieces_at, weights_at, ones_at, twos_at = some(4), some(4), some(4), some(4)
    rows_at = some(4)
    owned_at, new_at, first_at, second_at, copy_at = [some(4) for _ in range(5)]
    y_at, gx_at = some(2)
    ln_owned, ln_new, ln_first, ln_second = some(4)
    pieces, weights, ones, twos, owned, copies = [some(4) for _ in range(6)]
    row_buffer, piece_sem, in_sem, out_sem, row_sem = some(5)
    head, chip = lax.axis_index("head"), lax.axis_index("dp")

    def block_copies(index, arrays, buffers, sems, back):
        kind, block = BLOCK_LIST[index]
        rows = pl.ds(block * KINDS[kind][2], KINDS[kind][2])
        result = []
        for which, (array, buffer) in enumerate(zip(arrays, buffers)):
            outside, inside = array[kind].at[rows], buffer[kind].at[rows]
            pair = (inside, outside) if back else (outside, inside)
            result.append(pltpu.make_async_copy(*pair, sems.at[index, which]))
        return result

    row_reads = [
        pltpu.make_async_copy(rows_at[index], row_buffer.at[index], row_sem.at[0, index])
        for index in range(4)
    ]
    row_writes = [
        pltpu.make_async_copy(
            row_buffer.at[index],
            (y_at, gx_at)[index // 2].at[pl.ds((head if index % 2 == 0 else 1 - head) * SEQ, SEQ)],
            row_sem.at[1, index],
        )
        for index in range(4)
    ]
    piece_copies = [
        pltpu.make_async_copy(pieces_at[index], pieces[index], piece_sem.at[index])
        for index in range(4)
    ]
    count = len(BLOCK_LIST)
    reads = [
        block_copies(index, (weights_at, ones_at, twos_at), (weights, ones, twos), in_sem, False)
        for index in range(count)
    ]
    writes = [
        block_copies(
            index,
            (owned_at, new_at, first_at, second_at, copy_at),
            (owned, weights, ones, twos, copies),
            out_sem,
            True,
        )
        for index in range(count)
    ]
    for copy in piece_copies + [copy for block in reads for copy in block]:
        copy.start()
    for copy in row_reads:
        copy.start()
    gradient = t_ln[...]
    results = adam_step(gradient, ln[...], m_ln[...], v_ln[...], RATES[4])
    ln_owned[...] = jnp.where(owners[4] == chip, gradient, 0.0)
    ln_new[...], ln_first[...], ln_second[...] = results
    for copy in piece_copies:
        copy.wait()
    for index, (kind, block) in enumerate(BLOCK_LIST):
        for copy in reads[index]:
            copy.wait()
        size = KINDS[kind][2]
        mine = owners[kind] == chip

        def update(rows, gradient, kind=kind, mine=mine):
            results = adam_step(
                gradient, weights[kind][rows], ones[kind][rows], twos[kind][rows], RATES[kind]
            )
            owned[kind][rows] = jnp.where(mine, gradient, 0.0)
            weights[kind][rows], ones[kind][rows], twos[kind][rows] = results
            copies[kind][rows] = results[0].astype(bf16)

        def strips(strip, carry, kind=kind, block=block, size=size, update=update):
            start = block * size + strip * STRIP
            if kind == 0:
                source = pl.ds(pl.multiple_of(block * HALF + strip * STRIP, STRIP), STRIP)
                for part in range(2):
                    rows = pl.ds(pl.multiple_of(start + part * HALF, STRIP), STRIP)
                    update(rows, pieces[3][part, source, :].astype(f32))
            else:
                rows = pl.ds(pl.multiple_of(start, STRIP), STRIP)
                update(rows, strip_gradient(kind, block, strip, pieces))
            return carry

        lax.fori_loop(0, (HALF if kind == 0 else size) // STRIP, strips, 0)
        for copy in writes[index]:
            copy.start()
        if index == count - 3:
            for read, write in zip(row_reads, row_writes):
                read.wait()
                write.start()
    for copy in row_writes + [copy for block in writes for copy in block]:
        copy.wait()


def update_all(owners, pieces, t_ln, ln_all, weights, ones, twos, rows):
    anywhere = pl.BlockSpec(memory_space=pl.ANY)
    vmem = pl.BlockSpec(memory_space=pltpu.VMEM)
    shapes = [kind[0] for kind in KINDS]
    whole = [shaped(shape, f32) for shape in shapes]
    buffers = [pltpu.VMEM(shape, f32) for shape in shapes]
    results = pl.pallas_call(
        finish_step,
        in_specs=[smem_spec] + [vmem] * 4 + [anywhere] * 20,
        out_specs=[anywhere] * 22 + [vmem] * 4,
        out_shape=whole * 4
        + [shaped(shape) for shape in shapes]
        + [shaped((2 * SEQ, HALF))] * 2
        + [shaped((4, D), f32)] * 4,
        scratch_shapes=[pltpu.VMEM(piece.shape, bf16) for piece in pieces]
        + buffers * 4
        + [pltpu.VMEM(shape, bf16) for shape in shapes]
        + [
            pltpu.VMEM((4, SEQ, HALF), bf16),
            pltpu.SemaphoreType.DMA((4,)),
            pltpu.SemaphoreType.DMA((len(BLOCK_LIST), 3)),
            pltpu.SemaphoreType.DMA((len(BLOCK_LIST), 5)),
            pltpu.SemaphoreType.DMA((2, 4)),
        ],
        compiler_params=limits,
        name="update_all",
    )(owners, t_ln, *ln_all, *pieces, *weights, *ones, *twos, *rows)
    return results[:20], results[20:22], results[22:]


def gather_inputs(tokens, cotangent, w_qkv, w_out, w_up, w_down):
    def both(array):
        return array, swap_heads(array)

    x_own, x_other = both(tokens)
    qkv_own = w_qkv.transpose(1, 0, 2).astype(bf16)
    out_own = w_out.astype(bf16)
    up_own = w_up.astype(bf16)
    down_own = w_down.astype(bf16)
    qkv_other = swap_heads(qkv_own)
    later, _, _ = lax.optimization_barrier((cotangent, x_other, qkv_other))
    dy_own, dy_other = cotangent, swap_heads(later)

    def swap_later(value):
        return swap_heads(lax.optimization_barrier((value, x_other, qkv_other))[0])

    weights = (
        qkv_own,
        qkv_other,
        out_own,
        swap_heads(out_own),
        up_own,
        swap_later(up_own),
        down_own,
        swap_later(down_own),
    )
    return x_own, x_other, dy_own, dy_other, weights


def body(
    tokens,
    cotangent,
    lengths,
    owners,
    w_qkv,
    w_out,
    w_up,
    w_down,
    ln_params,
    m_qkv,
    m_out,
    m_up,
    m_down,
    m_ln,
    v_qkv,
    v_out,
    v_up,
    v_down,
    v_ln,
):
    x_own, x_other, dy_own, dy_other, weights = gather_inputs(
        tokens, cotangent, w_qkv, w_out, w_up, w_down
    )
    y, gx, totals = layer_local(
        x_own, x_other, dy_own, dy_other, lengths, ln_params, weights
    )
    *pieces, t_ln = totals

    def as_rows(array):
        return array.transpose(1, 0, 2).reshape(3 * D, HALF)

    results, (output_rows, grad_input), ln_results = update_all(
        owners,
        pieces,
        t_ln,
        (ln_params, m_ln, v_ln),
        (as_rows(w_qkv), w_out, w_up, w_down),
        (as_rows(m_qkv), m_out, m_up, m_down),
        (as_rows(v_qkv), v_out, v_up, v_down),
        (*y, *gx),
    )
    groups = []
    for slot in range(5):
        group = list(results[slot * 4 : slot * 4 + 4])
        group[0] = group[0].reshape(3, D, HALF).transpose(1, 0, 2)
        if slot < 4:
            group.append(ln_results[slot])
        groups.append(tuple(group))
    owned = tuple(array[None] for array in groups[0])
    return (output_rows, grad_input) + owned + groups[1] + groups[2] + groups[3] + groups[4]


PLACED = (
    (P("dp", "head"),) * 2
    + (P("dp"), P())
    + (P(None, None, "head"), P("head", None), P(None, "head"), P("head", None), P()) * 3
)
RESULTS = (
    (P("dp", "head"),) * 2
    + (
        P("dp", None, None, "head"),
        P("dp", "head", None),
        P("dp", None, "head"),
        P("dp", "head", None),
        P("dp", None, None),
    )
    + (P(None, None, "head"), P("head", None), P(None, "head"), P("head", None), P()) * 3
    + (P(None, None, "head"), P("head", None), P(None, "head"), P("head", None))
)


def solution(mesh):
    return jax.shard_map(
        body, mesh=mesh, in_specs=PLACED, out_specs=RESULTS, check_vma=False
    )
```
